32 devices in a mesh: tp: 4 (over x, core), ep: 8 (over z, y).
Axes of the slice: x: 2, y: 2, z: 4, core: 2. Of those that a mesh axis runs over, the one named last changes fastest.
Arguments:
- tokens: bfloat16 [8192, 1024], P('ep'), may hold values from -6 to 6
- segments: int32 [8, 1024], P('ep'), may hold values from 0 to 7, never falling along the last dimension, each value on 1 to 512 neighbouring positions
- routes: int32 [8192], P('ep'), may hold values from 0 to 7, as said below
- capacity: int32 [8], replicated, may hold values from 96 to 192, as said below
- ln1_gain: float32 [1024], replicated, may hold values from 0.25 to 1.75
- ln1_bias: float32 [1024], replicated, may hold values from -1.2 to 1.2
- qkv_weight: bfloat16 [3, 1024, 1024], P(None, None, 'tp'), may hold values from -0.1875 to 0.1875
- out_weight: bfloat16 [1024, 1024], P('tp'), may hold values from -0.75 to 0.75
- ln2_gain: float32 [1024], replicated, may hold values from 0.25 to 1.75
- ln2_bias: float32 [1024], replicated, may hold values from -1.2 to 1.2
- mix_weight: bfloat16 [1024, 2], replicated, may hold values from -0.1875 to 0.1875
- up_weight: bfloat16 [1024, 4096], P(None, 'tp'), may hold values from -0.1875 to 0.1875
- down_weight: bfloat16 [4096, 1024], P('tp'), may hold values from -0.1875 to 0.1875
- expert_up: bfloat16 [8, 1024, 4096], P('ep', None, 'tp'), may hold values from -0.1875 to 0.1875
- expert_down: bfloat16 [8, 4096, 1024], P('ep', 'tp'), may hold values from -0.1875 to 0.1875
- cotangent: bfloat16 [8192, 1024], P('ep'), may hold values from -6 to 6
Outputs:
- output: bfloat16 [8192, 1024], P('ep')
- grad_tokens: bfloat16 [8192, 1024], P('ep')
- grad_ln1_gain: float32 [1024], replicated
- grad_ln1_bias: float32 [1024], replicated
- grad_qkv: float32 [3, 1024, 1024], P(None, None, 'tp')
- grad_out: float32 [1024, 1024], P('tp')
- grad_ln2_gain: float32 [1024], replicated
- grad_ln2_bias: float32 [1024], replicated
- grad_mix: float32 [1024, 2], replicated
- grad_up: float32 [1024, 4096], P(None, 'tp')
- grad_down: float32 [4096, 1024], P('tp')
- grad_expert_up: float32 [8, 1024, 4096], P('ep', None, 'tp')
- grad_expert_down: float32 [8, 4096, 1024], P('ep', 'tp')
The draws below stay inside these ranges and needn't reach their ends.
Inputs may be any that keep to these rules, and one draw needn't show every extreme that they name: `routes`: in the tokens of each index of ep, one expert is named 192 times or more, and its capacity is 192. One expert's capacity is 192.
All inputs are finite; a program needn't handle non-finite values.
Results may differ from the reference program's by a relative error of at most 0.033.
Values may be sent and summed in bfloat16 or wider, within the bound.
A program may use at most 192 MiB of HBM per device.

```python
import math
import jax
import jax.numpy as jnp
import numpy as np
from jax import lax

MODEL_WIDTH = 1024
HEADS = 16
FF = 4096
HD = 64
LEN = 1024
SEQ_DEV = 1
TOK_DEV = 1024
SEQS = 8
TOKENS = 8192
EXPERT_COUNT = 8
CAP = 192
N_TP = 4
N_EP = 8


def favoured_expert(key):
    return jax.random.randint(key, (), 0, EXPERT_COUNT)


def block_order(subkey):
    return jax.random.permutation(subkey, TOK_DEV)


def draw_routes(key, part):
    favoured = favoured_expert(key)
    key = jax.random.fold_in(key, 3)
    first_key, second_key, third_key, fourth_key = jax.random.split(key, 4)
    left_pick = jax.random.randint(first_key, (TOKENS,), 0, EXPERT_COUNT)
    right_pick = jax.random.randint(second_key, (TOKENS,), 0, EXPERT_COUNT)
    relabel = jax.random.permutation(third_key, EXPERT_COUNT)
    skewed = relabel[jnp.minimum(left_pick, right_pick)]
    orders = jax.vmap(block_order)(jax.random.split(fourth_key, TOKENS // TOK_DEV))
    chosen = orders.reshape(TOKENS) < CAP
    return jnp.where(chosen, favoured, skewed).astype(jnp.int32)


def draw_capacity(key, part):
    favoured = favoured_expert(key)
    key = jax.random.fold_in(key, 5)
    drawn = jax.random.randint(key, (EXPERT_COUNT,), (CAP + 1) // 2, CAP + 1)
    return jnp.where(jnp.arange(EXPERT_COUNT) == favoured, CAP, drawn).astype(jnp.int32)


def block_scale(stream_key, shape, cuts, least, largest):
    gain = 1.0
    for axis_at, blocks in cuts:
        draws = jax.random.uniform(jax.random.fold_in(jax.random.fold_in(stream_key, 6), axis_at), (blocks,), jnp.float32, least / len(cuts), largest / len(cuts))
        gain = gain * jnp.repeat(jnp.exp(draws), shape[axis_at] // blocks).reshape((-1,) + (1,) * (len(shape) - 1 - axis_at))
    return gain


def split_up(count, total, limit, skew):
    portions = [(1 << 20) // math.isqrt(rank ** skew) + 1 for rank in range(2, count + 1)]
    spare, given = total - limit - (count - 1), [1] * (count - 1)
    while spare > 0:
        free = [i for i in range(count - 1) if given[i] < limit]
        whole, remaining = sum([portions[i] for i in free]), spare
        for i in free:
            addition = min(limit - given[i], max(1, remaining * portions[i] // whole), spare)
            given[i] = given[i] + addition
            spare = spare - addition
    return np.array([limit] + given)


def uneven_parts(own_key, amount, total, limit, slope):
    if amount == 2:
        one = jax.random.randint(own_key, (), max(1, total - limit), min(limit, total - 1) + 1)
        return jnp.stack([one, total - one])
    tallies = jnp.asarray(split_up(amount, total, limit, slope), jnp.int32)
    pairs = (amount - 1) // 2
    source_of, receiver = tallies[1:1 + 2 * pairs:2], tallies[2:2 + 2 * pairs:2]
    slack = jnp.minimum(source_of - 1, limit - receiver)
    passed = jax.random.randint(jax.random.fold_in(own_key, 1), (pairs,), 0, 1 << 20) % (slack + 1)
    tallies = tallies.at[1:1 + 2 * pairs:2].set(source_of - passed).at[2:2 + 2 * pairs:2].set(receiver + passed)
    return tallies[jax.random.permutation(jax.random.fold_in(own_key, 2), amount)]


def noise(rng, shape, deviation, most, cuts=(), held_as=jnp.bfloat16):
    values = jax.random.normal(rng, shape, jnp.float32) * deviation
    if len(cuts) > 0:
        values = block_scale(rng, shape, cuts, -0.22, 0.18) * values
    return jnp.clip(values, min=-most, max=most).astype(held_as)


def setup_inputs(seed: int = 0) -> dict:
    arg_keys = jax.random.split(jax.random.key(seed), 17)
    return {
        "tokens": noise(arg_keys[0], (TOKENS, MODEL_WIDTH), 1.0, 6.0, ((0, 8),)),
        "segments": jax.vmap(lambda own: jnp.searchsorted(jnp.cumsum(uneven_parts(own, 8, LEN, LEN // 2, 0)), jnp.arange(LEN), side="right"))(jax.random.split(arg_keys[1], SEQS)).reshape((SEQS, LEN)).astype(jnp.int32),
        "routes": draw_routes(jax.random.fold_in(arg_keys[16], 71), 0),
        "capacity": draw_capacity(jax.random.fold_in(arg_keys[16], 71), 0),
        "ln1_gain": jnp.clip(1.0 + 0.15 * jax.random.normal(arg_keys[4], (MODEL_WIDTH,), jnp.float32), 0.25, 1.75),
        "ln1_bias": noise(arg_keys[5], (MODEL_WIDTH,), 0.3, 1.2, (), jnp.float32),
        "qkv_weight": noise(arg_keys[6], (3, MODEL_WIDTH, MODEL_WIDTH), MODEL_WIDTH ** -0.5, 0.1875, ((2, 4),)),
        "out_weight": noise(arg_keys[7], (MODEL_WIDTH, MODEL_WIDTH), (MODEL_WIDTH // 16) ** -0.5, 0.75, ((0, 4),)),
        "ln2_gain": jnp.clip(1.0 + 0.15 * jax.random.normal(arg_keys[8], (MODEL_WIDTH,), jnp.float32), 0.25, 1.75),
        "ln2_bias": noise(arg_keys[9], (MODEL_WIDTH,), 0.3, 1.2, (), jnp.float32),
        "mix_weight": noise(arg_keys[10], (MODEL_WIDTH, 2), MODEL_WIDTH ** -0.5, 0.1875),
        "up_weight": noise(arg_keys[11], (MODEL_WIDTH, FF), MODEL_WIDTH ** -0.5, 0.1875, ((1, 4),)),
        "down_weight": noise(arg_keys[12], (FF, MODEL_WIDTH), (FF // 4) ** -0.5, 0.1875, ((0, 4),)),
        "expert_up": noise(arg_keys[13], (EXPERT_COUNT, MODEL_WIDTH, FF), MODEL_WIDTH ** -0.5, 0.1875, ((0, 8), (2, 4))),
        "expert_down": noise(arg_keys[14], (EXPERT_COUNT, FF, MODEL_WIDTH), (FF // 4) ** -0.5, 0.1875, ((0, 8), (1, 4))),
        "cotangent": noise(arg_keys[15], (TOKENS, MODEL_WIDTH), 1.0, 6.0, ((0, 8),)),
    }


@jax.custom_vjp
def low(v):
    return lax.optimization_barrier(v.astype(jnp.bfloat16)).astype(jnp.float32)

@jax.custom_vjp
def reduced_backward(v):
    return v

def low_keep(v):
    return (low(v), None)

def low_pass(kept, grad):
    return (grad,)

def back_keep(v):
    return (v, None)

def back_low(kept, grad):
    return (low(grad),)
low.defvjp(low_keep, low_pass)
reduced_backward.defvjp(back_keep, back_low)
epsilon = 1e-05
highest_precision = lax.Precision.HIGHEST
masked_value = -1e+30

def layer_norm(values, gain_row, bias_row):
    centred = values - lax.optimization_barrier(jnp.mean(values, axis=-1, keepdims=True))
    variance = lax.optimization_barrier(jnp.mean(centred * centred, axis=-1, keepdims=True))
    return centred * lax.rsqrt(variance + epsilon) * gain_row + bias_row

def attend_block(query_rows, key_rows, value_rows, seg_query, seg_keys, first_row):
    scale = 1.0 / math.sqrt(HD)
    scores = reduced_backward(jnp.einsum('qhd,khd->hqk', query_rows, key_rows, precision=highest_precision) * scale)
    query_pos = first_row + jnp.arange(query_rows.shape[0], dtype=jnp.int32)
    key_pos = jnp.arange(key_rows.shape[0], dtype=jnp.int32)
    allowed = (seg_query[:, None] == seg_keys[None, :]) & (key_pos[None, :] <= query_pos[:, None])
    chances = jax.nn.softmax(jnp.where(allowed[None], scores, masked_value), axis=-1)
    return jnp.einsum('hqk,khd->qhd', low(chances), value_rows, precision=highest_precision)

def attend_sequence(operands):
    query_rows, key_rows, value_rows, seg_row = operands
    block_len = min(512, LEN)
    block_count = LEN // block_len
    starts = jnp.arange(block_count, dtype=jnp.int32) * block_len

    def one_block(pieces):
        return attend_block(pieces[0], key_rows, value_rows, pieces[1], seg_row, pieces[2])
    result = lax.map(jax.checkpoint(one_block), (query_rows.reshape(block_count, block_len, HEADS, HD), seg_row.reshape(block_count, block_len), starts))
    return result.reshape(LEN, HEADS * HD)

def dispatch_table(route_rows, capacity):
    onehot = (route_rows[:, None] == jnp.arange(EXPERT_COUNT, dtype=jnp.int32)[None, :]).astype(jnp.int32)
    before = jnp.cumsum(onehot, axis=0) - onehot
    slot_rank = lax.optimization_barrier(jnp.sum(before * onehot, axis=1))
    cap_limit = lax.optimization_barrier(jnp.sum(capacity[None, :] * onehot, axis=1))
    target = jnp.where(slot_rank < cap_limit, route_rows * CAP + slot_rank, -1)
    return (target[:, None] == jnp.arange(EXPERT_COUNT * CAP, dtype=jnp.int32)[None, :]).astype(jnp.float32)

def reference(tokens, segments, routes, capacity, ln1_gain, ln1_bias, qkv_weight, out_weight, ln2_gain, ln2_bias, mix_weight, up_weight, down_weight, expert_up, expert_down, cotangent):
    group_devs = math.gcd(N_EP, max(1, 4096 // TOK_DEV))
    block_total = N_EP // group_devs
    block_rows = group_devs * TOK_DEV
    block_seqs = group_devs * SEQ_DEV
    head_share = MODEL_WIDTH // N_TP
    normalized_share = FF // N_TP

    def block_forward(parameters, operands):
        first_gain, first_bias, query_key_value_weight, output_weight, second_gain, second_bias, mixing_weight, dense_up_weight, dense_down_weight, expert_up_weight, expert_down_weight = parameters
        input_rows, seg_rows, route_rows = operands
        first_low = low(layer_norm(input_rows, first_gain, first_bias))
        projected = [reduced_backward(low(jnp.dot(first_low, query_key_value_weight[j], precision=highest_precision))) for j in range(3)]
        shaped = [item.reshape(block_seqs, LEN, HEADS, HD) for item in projected]
        heads_out = lax.map(attend_sequence, (shaped[0], shaped[1], shaped[2], seg_rows)).reshape(block_rows, MODEL_WIDTH)
        heads_out = reduced_backward(low(heads_out))
        parts = jnp.einsum('ngk,gkd->gnd', heads_out.reshape(block_rows, N_TP, head_share), output_weight.reshape(N_TP, head_share, MODEL_WIDTH), precision=highest_precision)
        hidden = input_rows + lax.optimization_barrier(jnp.sum(low(reduced_backward(parts)), axis=0))
        second_low = low(layer_norm(hidden, second_gain, second_bias))
        mixing = jax.nn.softmax(jnp.dot(second_low, mixing_weight, precision=highest_precision), axis=-1)
        pre_dense = reduced_backward(jnp.dot(second_low, dense_up_weight, precision=highest_precision))
        act_dense = low(jax.nn.gelu(pre_dense))
        dense_parts = reduced_backward(jnp.einsum('ngf,gfd->gnd', act_dense.reshape(block_rows, N_TP, normalized_share), dense_down_weight.reshape(N_TP, normalized_share, MODEL_WIDTH), precision=highest_precision))
        dense = lax.optimization_barrier(jnp.sum(dense_parts, axis=0))
        tables = jax.vmap(dispatch_table, in_axes=(0, None))(route_rows.reshape(group_devs, TOK_DEV), capacity)
        outgoing = jnp.einsum('stj,std->sjd', tables, second_low.reshape(group_devs, TOK_DEV, MODEL_WIDTH), precision=highest_precision)
        expert_rows = outgoing.reshape(group_devs, EXPERT_COUNT, CAP, MODEL_WIDTH).transpose(1, 0, 2, 3).reshape(EXPERT_COUNT, group_devs * CAP, MODEL_WIDTH)
        expert_rows = reduced_backward(expert_rows)
        replicas = reduced_backward(jnp.broadcast_to(expert_rows[None], (N_TP,) + expert_rows.shape))
        expert_preactivation = reduced_backward(jnp.einsum('hzkv,zvhc->hzkc', replicas, expert_up_weight.reshape(EXPERT_COUNT, MODEL_WIDTH, N_TP, normalized_share), precision=highest_precision))
        expert_act = low(jax.nn.gelu(expert_preactivation))
        expert_res = low(reduced_backward(jnp.einsum('gerf,egfd->gerd', expert_act, expert_down_weight.reshape(EXPERT_COUNT, N_TP, normalized_share, MODEL_WIDTH), precision=highest_precision)))
        expert_sum = reduced_backward(low(lax.optimization_barrier(jnp.sum(expert_res, axis=0))))
        laid_back = expert_sum.reshape(EXPERT_COUNT, group_devs, CAP, MODEL_WIDTH).transpose(1, 0, 2, 3).reshape(group_devs, EXPERT_COUNT * CAP, MODEL_WIDTH)
        returned = jnp.einsum('stj,sjd->std', tables, laid_back, precision=highest_precision).reshape(block_rows, MODEL_WIDTH)
        return hidden + mixing[:, 0:1] * dense + mixing[:, 1:2] * returned
    checked = jax.checkpoint(block_forward)

    def forward_pass(input_values, first_gain, first_bias, query_key_value_weight, output_weight, second_gain, second_bias, mixing_weight, dense_up_weight, dense_down_weight, expert_up_weight, expert_down_weight):
        parameters = (first_gain, first_bias, query_key_value_weight, output_weight, second_gain, second_bias, mixing_weight, dense_up_weight, dense_down_weight, expert_up_weight, expert_down_weight)

        def run_block(operands):
            return checked(parameters, operands)
        operands = (input_values.reshape(block_total, block_rows, MODEL_WIDTH), segments.reshape(block_total, block_seqs, LEN), routes.reshape(block_total, block_rows))
        return lax.map(run_block, operands).reshape(N_EP * TOK_DEV, MODEL_WIDTH)
    output, pullback = jax.vjp(forward_pass, tokens.astype(jnp.float32), ln1_gain.astype(jnp.float32), ln1_bias.astype(jnp.float32), qkv_weight.astype(jnp.float32), out_weight.astype(jnp.float32), ln2_gain.astype(jnp.float32), ln2_bias.astype(jnp.float32), mix_weight.astype(jnp.float32), up_weight.astype(jnp.float32), down_weight.astype(jnp.float32), expert_up.astype(jnp.float32), expert_down.astype(jnp.float32))
    grads = pullback(cotangent.astype(jnp.float32))
    return (output.astype(jnp.bfloat16), grads[0].astype(jnp.bfloat16), grads[1], grads[2], grads[3], grads[4], grads[5], grads[6], grads[7], grads[8], grads[9], grads[10], grads[11])
```

```python
import functools
import math

import jax
import jax.numpy as jnp
from jax import lax
from jax.experimental import pallas as pl
from jax.experimental.pallas import tpu as pltpu
from jax.sharding import PartitionSpec as P

HD = 64
epsilon = 1e-05
masked_value = -1e30
F32 = jnp.float32
BF16 = jnp.bfloat16
VMEM_LIMIT = 60 * 2**20
MESH = pl.DeviceIdType.MESH


def mm(a, b):
    return lax.dot_general(a, b, (((1,), (0,)), ((), ())), preferred_element_type=F32)


def mm_t(a, b):
    return lax.dot_general(a, b, (((1,), (1,)), ((), ())), preferred_element_type=F32)


def t_mm(a, b):
    return lax.dot_general(a, b, (((0,), (0,)), ((), ())), preferred_element_type=F32)


def norm_rows(x):
    centred = x - jnp.mean(x, axis=-1, keepdims=True)
    spread = lax.rsqrt(jnp.mean(centred * centred, axis=-1, keepdims=True) + epsilon)
    return centred * spread, spread


def place():
    t = lax.axis_index("tp")
    return t, lax.div(t, 2), lax.rem(t, 2), lax.axis_index("ep")


def remote(src, dst, send, recv, t, e):
    return pltpu.make_async_remote_copy(
        src_ref=src, dst_ref=dst, send_sem=send, recv_sem=recv, device_id=(t, e), device_id_type=MESH
    )


def greet(partners, loop_partner, loop_count):
    bar = pltpu.get_barrier_semaphore()
    for t, e in partners:
        pl.semaphore_signal(bar, inc=1, device_id=(t, e), device_id_type=MESH)

    def one(i, carry):
        t, e = loop_partner(i)
        pl.semaphore_signal(bar, inc=1, device_id=(t, e), device_id_type=MESH)
        return carry

    if loop_count:
        lax.fori_loop(0, loop_count, one, 0)
    pl.semaphore_wait(bar, len(partners) + loop_count)


def onehot_rows(tgt, first, count):
    rows = lax.broadcasted_iota(jnp.int32, (count, tgt.shape[1]), 0) + first
    return (rows == tgt).astype(F32).astype(BF16)


def forward_kernel(
    n_tp, n_ep, tok, cot, segr, segc, rts, cap, g1, b1, g2, b2, wqkv, wout, mixw,
    qkv_o, ht_o, lse_o, n2_o, attn_o, mix_o, crow_o, tgt_o,
    n1, vt, snd, part, cbuf, xbuf, bias,
    as_, ar_, fs_, fr_, cs_, cr_, xs_, xr_, gs_, gr_, lsem,
):
    t, x, c, e = place()
    nx = n_tp // 2
    rows_all, width = tok.shape
    half = width // 2
    experts, slots = snd.shape[0], snd.shape[1]
    wl = wout.shape[0]
    heads = wl // HD
    blk = rows_all // 4
    mate = 2 * x + 1 - c
    x_peers = [2 * lax.rem(x + d, nx) + c for d in range(1, nx)]
    greet([(mate, e)] + [(p, e) for p in x_peers], lambda i: (t, lax.rem(e + 1 + i, n_ep)), n_ep - 1)

    hot = lax.broadcasted_iota(jnp.int32, (experts, rows_all), 0) == rts[...]
    hot_f = hot.astype(F32)
    hot_b = hot_f.astype(BF16)
    counts = jnp.zeros((experts, rows_all), F32)
    for k in range(4):
        earlier = (
            lax.broadcasted_iota(jnp.int32, (blk, rows_all), 0) + k * blk
            < lax.broadcasted_iota(jnp.int32, (blk, rows_all), 1)
        )
        counts = counts + mm(hot_b[:, k * blk : (k + 1) * blk], earlier.astype(F32).astype(BF16))
    rank = jnp.sum(counts * hot_f, axis=0, keepdims=True).astype(jnp.int32)
    limit = jnp.sum(jnp.where(hot, cap[...], 0), axis=0, keepdims=True)
    tgt = jnp.where(rank < limit, rts[...] * slots + rank, -1)
    tgt_o[...] = tgt

    my_half = pl.ds(pl.multiple_of(c * half, half), half)

    def rows_for(dest):
        hot_rows = onehot_rows(tgt_o[...], dest * slots, slots)
        return mm(hot_rows, cot[:, my_half]).astype(BF16)

    def a2a_copy(dest, src):
        return remote(snd.at[dest], crow_o.at[c, src], as_.at[dest], ar_.at[src], t, dest)

    def send_rows(i, carry):
        dest = lax.rem(e + 1 + i, n_ep)
        snd[dest] = rows_for(dest)
        a2a_copy(dest, e).start()
        return carry

    lax.fori_loop(0, n_ep - 1, send_rows, 0)
    snd[e] = rows_for(e)
    own = pltpu.make_async_copy(snd.at[e], crow_o.at[c, e], lsem)
    own.start()
    remote(snd.at[e], crow_o.at[c, e], fs_.at[e], fr_.at[e], mate, e).start()

    for i in range(4):
        rs = pl.ds(i * blk, blk)
        unit, _ = norm_rows(tok[rs, :].astype(F32))
        normed = (unit * g1[...] + b1[...]).astype(BF16)
        n1[rs, :] = normed
        for j in range(3):
            qkv_o[j, rs, :] = mm(normed, wqkv[j]).astype(BF16)
        vt[:, rs] = qkv_o[2, rs, :].astype(F32).T.astype(BF16)

    def chunk(i):
        return pl.ds(i * blk, blk)

    other_half = pl.ds(pl.multiple_of((1 - c) * half, half), half)

    def core_copy(i):
        return remote(part.at[chunk(i), other_half], cbuf.at[chunk(i)], cs_.at[i], cr_.at[i], mate, e)

    def x_copy(i, d):
        return remote(
            xbuf.at[x, chunk(i)], xbuf.at[x, chunk(i)], xs_.at[i, d - 1], xr_.at[i, d - 1], x_peers[d - 1], e
        )

    def x_arrival(i, d):
        src = lax.rem(x + nx - d, nx)
        return remote(
            xbuf.at[src, chunk(i)], xbuf.at[src, chunk(i)], xs_.at[i, d - 1], xr_.at[i, d - 1], x_peers[d - 1], e
        )

    def share_copy(i):
        return remote(
            attn_o.at[chunk(i), my_half], attn_o.at[chunk(i), my_half], gs_.at[i], gr_.at[i], mate, e
        )

    def share_arrival(i):
        return remote(
            attn_o.at[chunk(i), other_half], attn_o.at[chunk(i), other_half], gs_.at[i], gr_.at[i], mate, e
        )

    def attend(i):
        keys = (i + 1) * blk
        ks = pl.ds(0, keys)
        allowed = (segc[ks, :] == segr[:, chunk(i)]) & (
            lax.broadcasted_iota(jnp.int32, (keys, blk), 0)
            <= lax.broadcasted_iota(jnp.int32, (keys, blk), 1) + i * blk
        )
        bias[ks, :] = jnp.where(allowed, 0.0, masked_value)
        head_of = lax.div(lax.broadcasted_iota(jnp.int32, (blk, wl), 1), HD)

        def one_head(h, carry):
            q_h = jnp.where(head_of == h, qkv_o[0, chunk(i), :].astype(F32) * 0.125, 0.0).astype(BF16)
            scores = mm_t(qkv_o[1, ks, :], q_h) + bias[ks, :]
            top = jnp.max(scores, axis=0, keepdims=True)
            weights = jnp.exp(scores - top)
            mass = jnp.sum(weights, axis=0, keepdims=True)
            lse_o[pl.ds(h, 1), chunk(i)] = top + jnp.log(mass)
            probs = (weights * (1.0 / mass)).astype(BF16)
            hs = pl.ds(pl.multiple_of(h * HD, HD), HD)
            ht_o[hs, chunk(i)] = mm(vt[hs, ks], probs).astype(BF16)
            return carry

        lax.fori_loop(0, heads, one_head, 0)
        part[chunk(i), :] = t_mm(ht_o[:, chunk(i)], wout[...]).astype(BF16)
        core_copy(i).start()

    def sum_cores(i):
        core_copy(i).wait_recv()
        both = part[chunk(i), my_half].astype(F32) + cbuf[chunk(i), :].astype(F32)
        xbuf[x, chunk(i), :] = both.astype(BF16)
        for d in range(1, nx):
            x_copy(i, d).start()

    def sum_chips(i):
        for d in range(1, nx):
            x_arrival(i, d).wait_recv()
        total = xbuf[0, chunk(i), :].astype(F32)
        for j in range(1, nx):
            total = total + xbuf[j, chunk(i), :].astype(F32)
        attn_o[chunk(i), my_half] = total.astype(BF16)
        share_copy(i).start()

    def finish(i):
        share_arrival(i).wait_recv()
        hidden = tok[chunk(i), :].astype(F32) + attn_o[chunk(i), :].astype(F32)
        unit, _ = norm_rows(hidden)
        normed = (unit * g2[...] + b2[...]).astype(BF16)
        n2_o[chunk(i), :] = normed
        logits = mm(normed, mixw[...])
        lane = lax.broadcasted_iota(jnp.int32, logits.shape, 1)
        logits = jnp.where(lane < 2, logits, masked_value)
        mix = jnp.exp(logits - jnp.max(logits, axis=1, keepdims=True))
        mix_o[chunk(i), :] = mix / jnp.sum(mix, axis=1, keepdims=True)

    attend(0)
    attend(1)
    sum_cores(0)
    attend(2)
    sum_cores(1)
    attend(3)
    sum_cores(2)
    sum_cores(3)

    def forward_rows(i, carry):
        src = lax.rem(e + n_ep - 1 - i, n_ep)
        a2a_copy(e, src).wait_recv()
        remote(crow_o.at[c, src], crow_o.at[c, src], fs_.at[src], fr_.at[src], mate, e).start()
        return carry

    def forward_done(src, carry):
        remote(crow_o.at[1 - c, src], crow_o.at[1 - c, src], fs_.at[src], fr_.at[src], mate, e).wait()
        return carry

    for i in range(4):
        sum_chips(i)
        if i >= 1:
            finish(i - 1)
    finish(3)
    lax.fori_loop(0, n_ep - 1, forward_rows, 0)
    lax.fori_loop(0, n_ep, forward_done, 0)
    own.wait()

    def sent(i, carry):
        a2a_copy(lax.rem(e + 1 + i, n_ep), e).wait_send()
        return carry

    lax.fori_loop(0, n_ep - 1, sent, 0)
    for i in range(4):
        core_copy(i).wait_send()
        for d in range(1, nx):
            x_copy(i, d).wait_send()
        share_copy(i).wait_send()


def forward(tokens, cotangent, segments, routes, capacity, g1, b1, g2, b2, wqkv, wout, mix_weight):
    n_tp, n_ep = lax.axis_size("tp"), lax.axis_size("ep")
    rows, width = tokens.shape
    wl = wout.shape[0]
    experts = capacity.shape[0]
    slots = 3 * rows // (2 * experts)
    nx = n_tp // 2
    half = width // 2
    vm = pl.BlockSpec(memory_space=pltpu.VMEM)
    dma = pltpu.SemaphoreType.DMA
    shape = jax.ShapeDtypeStruct
    mixw = jnp.pad(mix_weight, ((0, 0), (0, 126)))
    return pl.pallas_call(
        functools.partial(forward_kernel, n_tp, n_ep),
        out_shape=(
            shape((3, rows, wl), BF16),
            shape((wl, rows), BF16),
            shape((wl // HD, rows), F32),
            shape((rows, width), BF16),
            shape((rows, width), BF16),
            shape((rows, 128), F32),
            shape((2, experts, slots, half), BF16),
            shape((1, rows), jnp.int32),
        ),
        in_specs=[vm] * 13,
        out_specs=(vm,) * 6 + (pl.BlockSpec(memory_space=pl.ANY), vm),
        scratch_shapes=[
            pltpu.VMEM((rows, width), BF16),
            pltpu.VMEM((wl, rows), BF16),
            pltpu.VMEM((experts, slots, half), BF16),
            pltpu.VMEM((rows, width), BF16),
            pltpu.VMEM((rows, half), BF16),
            pltpu.VMEM((nx, rows, half), BF16),
            pltpu.VMEM((rows, rows // 4), F32),
            dma((experts,)), dma((experts,)), dma((experts,)), dma((experts,)),
            dma((4,)), dma((4,)), dma((4, max(nx - 1, 1))), dma((4, max(nx - 1, 1))), dma((4,)), dma((4,)),
            dma,
        ],
        compiler_params=pltpu.CompilerParams(
            collective_id=0, has_side_effects=True, vmem_limit_bytes=VMEM_LIMIT
        ),
        cost_estimate=pl.CostEstimate(flops=8 * 10**9, bytes_accessed=30 * 10**6, transcendentals=0),
        name="attention_forward",
    )(
        tokens, cotangent, segments, segments.reshape(rows, 1), routes.reshape(1, rows),
        capacity.reshape(experts, 1), g1.reshape(1, width), b1.reshape(1, width), g2.reshape(1, width),
        b2.reshape(1, width), wqkv, wout, mixw,
    )

block_limit = 512


def layer_norm(values, gain_row, bias_row):
    centred = values - jnp.mean(values, axis=-1, keepdims=True)
    spread = lax.rsqrt(jnp.mean(centred * centred, axis=-1, keepdims=True) + epsilon)
    unit_rows = centred * spread
    return (unit_rows * gain_row + bias_row, unit_rows, spread)


def norm_back(upstream, unit_rows, spread, gain_row):
    scaled = upstream * gain_row
    inner = (
        scaled
        - jnp.mean(scaled, axis=-1, keepdims=True)
        - unit_rows * jnp.mean(scaled * unit_rows, axis=-1, keepdims=True)
    )
    return (spread * inner, jnp.sum(upstream * unit_rows, axis=0), jnp.sum(upstream, axis=0))


def block_scores(query_rows, key_rows, seg_row, first_row):
    scale = 1.0 / math.sqrt(HD)
    scores = (
        jnp.einsum("qhd,khd->hqk", query_rows, key_rows, preferred_element_type=jnp.float32) * scale
    )
    query_pos = first_row + jnp.arange(query_rows.shape[0], dtype=jnp.int32)
    key_pos = jnp.arange(key_rows.shape[0], dtype=jnp.int32)
    seg_query = seg_row[first_row : first_row + query_rows.shape[0]]
    allowed = (seg_query[:, None] == seg_row[None, :]) & (key_pos[None, :] <= query_pos[:, None])
    return jnp.where(allowed[None], scores, masked_value)


def dispatch_table(routes, capacity, experts, slots):
    onehot = (routes[:, None] == jnp.arange(experts, dtype=jnp.int32)[None, :]).astype(jnp.int32)
    before = jnp.cumsum(onehot, axis=0) - onehot
    slot_rank = jnp.sum(before * onehot, axis=1)
    cap_limit = jnp.sum(capacity[None, :] * onehot, axis=1)
    target = jnp.where(slot_rank < cap_limit, routes * slots + slot_rank, -1)
    return (target[:, None] == jnp.arange(experts * slots, dtype=jnp.int32)[None, :]).astype(
        jnp.bfloat16
    )


def contract_rows(left, right):
    return lax.dot_general(
        left, right, (((0,), (0,)), ((), ())), preferred_element_type=jnp.float32
    )


def contract_cols(left, right):
    return lax.dot_general(
        left, right, (((1,), (1,)), ((), ())), preferred_element_type=jnp.float32
    )


def fanout(piece):
    return lax.all_gather(piece, "tp", axis=2, tiled=True)


def share_sum(terms):
    return lax.psum_scatter(
        terms.astype(jnp.bfloat16), "tp", scatter_dimension=2, tiled=True
    ).astype(jnp.float32)


def share_back(rows):
    return lax.all_to_all(rows, "ep", split_axis=0, concat_axis=0, tiled=True)


def local(
    tokens,
    segments,
    routes,
    capacity,
    ln1_gain,
    ln1_bias,
    qkv_weight,
    out_weight,
    ln2_gain,
    ln2_bias,
    mix_weight,
    up_weight,
    down_weight,
    expert_up,
    expert_down,
    cotangent,
):
    tok_rows, width = tokens.shape
    seq_count, seq_len = segments.shape
    local_width = out_weight.shape[0]
    local_heads = local_width // HD
    experts = capacity.shape[0]
    slots = 3 * tok_rows // (2 * experts)
    block_len = min(block_limit, seq_len)
    scale = 1.0 / math.sqrt(HD)
    col_share = width // lax.axis_size("tp")
    col_start = lax.axis_index("tp") * col_share
    (projected, heads_t, lse, second_low, attn_sum, mix_wide, cot_rows, targets) = forward(
        tokens, cotangent, segments, routes, capacity, ln1_gain, ln1_bias, ln2_gain, ln2_bias,
        qkv_weight, out_weight, mix_weight,
    )
    input_values = tokens.astype(jnp.float32)
    first_norm, first_unit, first_spread = layer_norm(input_values, ln1_gain, ln1_bias)
    first_low = first_norm.astype(jnp.bfloat16)
    split_heads = projected.reshape(3, seq_count, seq_len, local_heads, HD)
    kept_sums = [lse[:, i : i + block_len, None] for i in range(0, seq_len, block_len)]
    heads_out = heads_t.T
    hidden = input_values + attn_sum.astype(jnp.float32)
    _, second_unit, second_spread = layer_norm(hidden, ln2_gain, ln2_bias)
    mixing = mix_wide[:, :2]
    pre_dense = jnp.dot(second_low, up_weight, preferred_element_type=jnp.float32)
    act_dense = jax.nn.gelu(pre_dense).astype(jnp.bfloat16)
    dense_part = jnp.dot(act_dense, down_weight, preferred_element_type=jnp.float32)
    grad_out = cotangent.astype(jnp.float32)
    onehot_table = (
        targets.reshape(-1, 1) == jnp.arange(experts * slots, dtype=jnp.int32)[None, :]
    ).astype(jnp.bfloat16)
    outgoing = (
        contract_rows(onehot_table, second_low).astype(jnp.bfloat16).reshape(experts, slots, width)
    )
    own_cols = lax.dynamic_slice_in_dim(outgoing, col_start, col_share, 2)
    received = fanout(lax.all_to_all(own_cols, "ep", split_axis=0, concat_axis=0, tiled=True))
    row_block = received.reshape(-1, width)
    pre_rows = jnp.dot(row_block, expert_up[0], preferred_element_type=jnp.float32)
    act_rows = jax.nn.gelu(pre_rows).astype(jnp.bfloat16)
    part_rows = jnp.dot(act_rows, expert_down[0], preferred_element_type=jnp.float32).astype(
        jnp.bfloat16
    )
    lead = received.shape[:2]
    part_rows, pre_rows, full_rows = (
        part_rows.reshape(lead + (width,)),
        pre_rows.reshape(lead + (pre_rows.shape[-1],)),
        received,
    )
    expert_share = share_sum(part_rows.astype(jnp.float32)).astype(jnp.bfloat16)
    returned = share_back(expert_share)
    expert_cols = jnp.dot(
        onehot_table,
        returned.reshape(experts * slots, col_share),
        preferred_element_type=jnp.float32,
    )
    dense_cols = share_sum(dense_part[None])[0]
    hidden_cols = lax.dynamic_slice_in_dim(hidden, col_start, col_share, 1)
    cot_cols = lax.dynamic_slice_in_dim(grad_out, col_start, col_share, 1)
    out_cols = hidden_cols + mixing[:, 0:1] * dense_cols + mixing[:, 1:2] * expert_cols
    mix_part = jnp.stack(
        [jnp.sum(cot_cols * dense_cols, axis=1), jnp.sum(cot_cols * expert_cols, axis=1)], axis=1
    )
    gathered_out, gathered_mix = (
        lax.all_gather(out_cols.astype(jnp.bfloat16), "tp", axis=1, tiled=True).astype(
            out_cols.dtype
        ),
        lax.all_gather(mix_part.astype(jnp.bfloat16), "tp", axis=1, tiled=True).astype(
            mix_part.dtype
        ),
    )
    grad_mixing = jnp.sum(gathered_mix.reshape(tok_rows, -1, 2), axis=1)
    grad_dense = (mixing[:, 0:1] * grad_out).astype(jnp.bfloat16)
    grad_down = contract_rows(act_dense, grad_dense)
    grad_act = contract_cols(grad_dense, down_weight)
    _, dense_gelu_back = jax.vjp(jax.nn.gelu, pre_dense)
    grad_pre = dense_gelu_back(grad_act)[0].astype(jnp.bfloat16)
    grad_up = contract_rows(second_low, grad_pre)
    grad_second = contract_cols(grad_pre, up_weight)
    cot_all = jnp.concatenate([cot_rows[0], cot_rows[1]], axis=-1).reshape(-1, width)
    mix_rows = jax.nn.softmax(
        jnp.dot(row_block, mix_weight, preferred_element_type=jnp.float32), axis=-1
    )
    grad_in = (mix_rows[:, 1:2] * cot_all.astype(jnp.float32)).astype(jnp.bfloat16).reshape(received.shape)
    rows_input = full_rows.reshape(-1, width)
    rows_grad = grad_in.reshape(-1, width)
    rows_pre = pre_rows.reshape(rows_input.shape[0], -1)
    rows_act, expert_gelu_back = jax.vjp(jax.nn.gelu, rows_pre)
    grad_expert_down = contract_rows(rows_act.astype(jnp.bfloat16), rows_grad)
    grad_rows_act = contract_cols(rows_grad, expert_down[0])
    grad_rows_pre = expert_gelu_back(grad_rows_act)[0].astype(jnp.bfloat16)
    grad_expert_up = contract_rows(rows_input, grad_rows_pre)
    grad_rows_in = (
        contract_cols(grad_rows_pre, expert_up[0]).astype(jnp.bfloat16).reshape(grad_in.shape)
    )
    grad_share = share_sum(grad_rows_in.astype(jnp.float32)).astype(jnp.bfloat16)
    grad_back = share_back(grad_share)
    expert_grad_cols = jnp.dot(
        onehot_table,
        grad_back.reshape(experts * slots, col_share),
        preferred_element_type=jnp.float32,
    )
    dense_grad_cols = share_sum(grad_second[None])[0]
    grad_second = lax.all_gather(
        (dense_grad_cols + expert_grad_cols).astype(jnp.bfloat16), "tp", axis=1, tiled=True
    ).astype(jnp.float32)
    grad_logits = mixing * (grad_mixing - jnp.sum(mixing * grad_mixing, axis=1, keepdims=True))
    mix_float = mix_weight.astype(jnp.float32)
    grad_second = grad_second + lax.dot_general(
        grad_logits, mix_float, (((1,), (1,)), ((), ())), precision=lax.Precision.HIGHEST
    )
    grad_mix_weight = lax.dot_general(
        second_low.astype(jnp.float32),
        grad_logits,
        (((0,), (0,)), ((), ())),
        precision=lax.Precision.HIGHEST,
    )
    grad_norm_two, grad_gain_two, grad_bias_two = norm_back(
        grad_second, second_unit, second_spread, ln2_gain
    )
    grad_hidden = grad_out + grad_norm_two
    grad_attn = grad_hidden.astype(jnp.bfloat16)
    grad_out_weight = contract_rows(heads_out, grad_attn)
    grad_heads = contract_cols(grad_attn, out_weight).astype(jnp.bfloat16)
    grad_split = grad_heads.reshape(seq_count, seq_len, local_heads, HD)
    query_grads = []
    position = 0
    sequence = 0
    key_rows = split_heads[1, sequence]
    value_rows = split_heads[2, sequence]
    key_total = jnp.zeros((seq_len, local_heads, HD), jnp.float32)
    value_total = jnp.zeros((seq_len, local_heads, HD), jnp.float32)
    for first_row in range(0, seq_len, block_len):
        query_rows = split_heads[0, sequence, first_row : first_row + block_len]
        scores = block_scores(query_rows, key_rows, segments[sequence], first_row)
        chances = jnp.exp(scores - kept_sums[position])
        position = position + 1
        upstream = grad_split[sequence, first_row : first_row + block_len]
        grad_chances = jnp.einsum(
            "qhd,khd->hqk", upstream, value_rows, preferred_element_type=jnp.float32
        )
        grad_scores = (
            chances * (grad_chances - jnp.sum(chances * grad_chances, axis=-1, keepdims=True))
        ).astype(jnp.bfloat16)
        value_total = value_total + jnp.einsum(
            "hqk,qhd->khd",
            chances.astype(jnp.bfloat16),
            upstream,
            preferred_element_type=jnp.float32,
        )
        query_grads.append(
            jnp.einsum("hqk,khd->qhd", grad_scores, key_rows, preferred_element_type=jnp.float32)
            * scale
        )
        key_total = (
            key_total
            + jnp.einsum(
                "hqk,qhd->khd", grad_scores, query_rows, preferred_element_type=jnp.float32
            )
            * scale
        )
    key_grads = [key_total]
    value_grads = [value_total]
    grad_query = jnp.concatenate(query_grads, axis=0).reshape(tok_rows, local_width)
    grad_key = jnp.stack(key_grads).reshape(tok_rows, local_width)
    grad_value = jnp.stack(value_grads).reshape(tok_rows, local_width)
    grad_projected = jnp.stack([grad_query, grad_key, grad_value]).astype(jnp.bfloat16)
    grad_qkv_weight = jnp.einsum(
        "td,jtk->jdk", first_low, grad_projected, preferred_element_type=jnp.float32
    )
    grad_first = jnp.einsum(
        "jtk,jdk->td", grad_projected, qkv_weight, preferred_element_type=jnp.float32
    )
    grad_first = lax.psum(grad_first.astype(jnp.bfloat16), "tp").astype(jnp.float32)
    grad_norm_one, grad_gain_one, grad_bias_one = norm_back(
        grad_first, first_unit, first_spread, ln1_gain
    )
    grad_tokens = (grad_hidden + grad_norm_one).astype(jnp.bfloat16)
    summed = (
        lax.psum(grad_qkv_weight.astype(jnp.bfloat16), "ep").astype(jnp.float32),
        lax.psum(grad_out_weight.astype(jnp.bfloat16), "ep").astype(jnp.float32),
        lax.psum(grad_up.astype(jnp.bfloat16), "ep").astype(jnp.float32),
        lax.psum(grad_down.astype(jnp.bfloat16), "ep").astype(jnp.float32),
        lax.psum(grad_mix_weight.astype(jnp.bfloat16), "ep").astype(jnp.float32),
        lax.psum(grad_gain_one.astype(jnp.bfloat16), "ep").astype(jnp.float32),
        lax.psum(grad_bias_one.astype(jnp.bfloat16), "ep").astype(jnp.float32),
        lax.psum(grad_gain_two.astype(jnp.bfloat16), "ep").astype(jnp.float32),
        lax.psum(grad_bias_two.astype(jnp.bfloat16), "ep").astype(jnp.float32),
    )
    return (
        gathered_out.astype(jnp.bfloat16),
        grad_tokens,
        summed[5],
        summed[6],
        summed[0],
        summed[1],
        summed[7],
        summed[8],
        summed[4],
        summed[2],
        summed[3],
        grad_expert_up[None],
        grad_expert_down[None],
    )


def solution(mesh):
    return jax.shard_map(
        local,
        mesh=mesh,
        in_specs=(
            P("ep", None),
            P("ep", None),
            P("ep"),
            P(),
            P(),
            P(),
            P(None, None, "tp"),
            P("tp", None),
            P(),
            P(),
            P(),
            P(None, "tp"),
            P("tp", None),
            P("ep", None, "tp"),
            P("ep", "tp", None),
            P("ep", None),
        ),
        out_specs=(
            P("ep", None),
            P("ep", None),
            P(),
            P(),
            P(None, None, "tp"),
            P("tp", None),
            P(),
            P(),
            P(),
            P(None, "tp"),
            P("tp", None),
            P("ep", None, "tp"),
            P("ep", "tp", None),
        ),
        check_vma=False,
    )
```

```python
import functools
import math

import jax
import jax.numpy as jnp
from jax import lax
from jax.experimental import pallas as pl
from jax.experimental.pallas import tpu as pltpu
from jax.sharding import PartitionSpec as P

HD = 64
epsilon = 1e-05
masked_value = -1e30
F32 = jnp.float32
BF16 = jnp.bfloat16
VMEM_LIMIT = 60 * 2**20
MESH = pl.DeviceIdType.MESH


def mm(a, b):
    return lax.dot_general(a, b, (((1,), (0,)), ((), ())), preferred_element_type=F32)


def mm_t(a, b):
    return lax.dot_general(a, b, (((1,), (1,)), ((), ())), preferred_element_type=F32)


def t_mm(a, b):
    return lax.dot_general(a, b, (((0,), (0,)), ((), ())), preferred_element_type=F32)


def norm_rows(x):
    centred = x - jnp.mean(x, axis=-1, keepdims=True)
    spread = lax.rsqrt(jnp.mean(centred * centred, axis=-1, keepdims=True) + epsilon)
    return centred * spread, spread


def place():
    t = lax.axis_index("tp")
    return t, lax.div(t, 2), lax.rem(t, 2), lax.axis_index("ep")


def remote(src, dst, send, recv, t, e):
    return pltpu.make_async_remote_copy(
        src_ref=src, dst_ref=dst, send_sem=send, recv_sem=recv, device_id=(t, e), device_id_type=MESH
    )


def greet(partners, loop_partner, loop_count):
    bar = pltpu.get_barrier_semaphore()
    for t, e in partners:
        pl.semaphore_signal(bar, inc=1, device_id=(t, e), device_id_type=MESH)

    def one(i, carry):
        t, e = loop_partner(i)
        pl.semaphore_signal(bar, inc=1, device_id=(t, e), device_id_type=MESH)
        return carry

    if loop_count:
        lax.fori_loop(0, loop_count, one, 0)
    pl.semaphore_wait(bar, len(partners) + loop_count)


def onehot_rows(tgt, first, count):
    rows = lax.broadcasted_iota(jnp.int32, (count, tgt.shape[1]), 0) + first
    return (rows == tgt).astype(F32).astype(BF16)


def forward_kernel(
    n_tp, n_ep, tok, cot, segr, segc, rts, cap, g1, b1, g2, b2, wqkv, wout, mixw,
    qkv_o, ht_o, lse_o, n2_o, attn_o, mix_o, crow_o, tgt_o, tgtc_o,
    n1, vt, snd, part, cbuf, xbuf, bias,
    as_, ar_, fs_, fr_, cs_, cr_, xs_, xr_, gs_, gr_, lsem,
):
    t, x, c, e = place()
    nx = n_tp // 2
    rows_all, width = tok.shape
    half = width // 2
    experts, slots = snd.shape[0], snd.shape[1]
    wl = wout.shape[0]
    heads = wl // HD
    blk = rows_all // 4
    mate = 2 * x + 1 - c
    x_peers = [2 * lax.rem(x + d, nx) + c for d in range(1, nx)]
    greet([(mate, e)] + [(p, e) for p in x_peers], lambda i: (t, lax.rem(e + 1 + i, n_ep)), n_ep - 1)

    hot = lax.broadcasted_iota(jnp.int32, (experts, rows_all), 0) == rts[...]
    hot_f = hot.astype(F32)
    hot_b = hot_f.astype(BF16)
    counts = jnp.zeros((experts, rows_all), F32)
    for k in range(4):
        earlier = (
            lax.broadcasted_iota(jnp.int32, (blk, rows_all), 0) + k * blk
            < lax.broadcasted_iota(jnp.int32, (blk, rows_all), 1)
        )
        counts = counts + mm(hot_b[:, k * blk : (k + 1) * blk], earlier.astype(F32).astype(BF16))
    rank = jnp.sum(counts * hot_f, axis=0, keepdims=True).astype(jnp.int32)
    limit = jnp.sum(jnp.where(hot, cap[...], 0), axis=0, keepdims=True)
    tgt = jnp.where(rank < limit, rts[...] * slots + rank, -1)
    tgt_o[...] = tgt
    tgtc_o[...] = jnp.broadcast_to(tgt.astype(F32), (8, rows_all)).T.astype(jnp.int32)

    my_half = pl.ds(pl.multiple_of(c * half, half), half)

    def rows_for(dest):
        hot_rows = onehot_rows(tgt_o[...], dest * slots, slots)
        return mm(hot_rows, cot[:, my_half]).astype(BF16)

    def a2a_copy(dest, src):
        return remote(snd.at[dest], crow_o.at[c, src], as_.at[dest], ar_.at[src], t, dest)

    def send_rows(i, carry):
        dest = lax.rem(e + 1 + i, n_ep)
        snd[dest] = rows_for(dest)
        a2a_copy(dest, e).start()
        return carry

    lax.fori_loop(0, n_ep - 1, send_rows, 0)
    snd[e] = rows_for(e)
    own = pltpu.make_async_copy(snd.at[e], crow_o.at[c, e], lsem)
    own.start()
    remote(snd.at[e], crow_o.at[c, e], fs_.at[e], fr_.at[e], mate, e).start()

    for i in range(4):
        rs = pl.ds(i * blk, blk)
        unit, _ = norm_rows(tok[rs, :].astype(F32))
        normed = (unit * g1[...] + b1[...]).astype(BF16)
        n1[rs, :] = normed
        for j in range(3):
            qkv_o[j, rs, :] = mm(normed, wqkv[j]).astype(BF16)
        vt[:, rs] = qkv_o[2, rs, :].astype(F32).T.astype(BF16)

    def chunk(i):
        return pl.ds(i * blk, blk)

    other_half = pl.ds(pl.multiple_of((1 - c) * half, half), half)

    def core_copy(i):
        return remote(part.at[chunk(i), other_half], cbuf.at[chunk(i)], cs_.at[i], cr_.at[i], mate, e)

    def x_copy(i, d):
        return remote(
            xbuf.at[x, chunk(i)], xbuf.at[x, chunk(i)], xs_.at[i, d - 1], xr_.at[i, d - 1], x_peers[d - 1], e
        )

    def x_arrival(i, d):
        src = lax.rem(x + nx - d, nx)
        return remote(
            xbuf.at[src, chunk(i)], xbuf.at[src, chunk(i)], xs_.at[i, d - 1], xr_.at[i, d - 1], x_peers[d - 1], e
        )

    def share_copy(i):
        return remote(
            attn_o.at[chunk(i), my_half], attn_o.at[chunk(i), my_half], gs_.at[i], gr_.at[i], mate, e
        )

    def share_arrival(i):
        return remote(
            attn_o.at[chunk(i), other_half], attn_o.at[chunk(i), other_half], gs_.at[i], gr_.at[i], mate, e
        )

    def attend(i):
        keys = (i + 1) * blk
        ks = pl.ds(0, keys)
        allowed = (segc[ks, :] == segr[:, chunk(i)]) & (
            lax.broadcasted_iota(jnp.int32, (keys, blk), 0)
            <= lax.broadcasted_iota(jnp.int32, (keys, blk), 1) + i * blk
        )
        bias[ks, :] = jnp.where(allowed, 0.0, masked_value)
        head_of = lax.div(lax.broadcasted_iota(jnp.int32, (blk, wl), 1), HD)

        def one_head(h, carry):
            q_h = jnp.where(head_of == h, qkv_o[0, chunk(i), :].astype(F32) * 0.125, 0.0).astype(BF16)
            scores = mm_t(qkv_o[1, ks, :], q_h) + bias[ks, :]
            top = jnp.max(scores, axis=0, keepdims=True)
            weights = jnp.exp(scores - top)
            mass = jnp.sum(weights, axis=0, keepdims=True)
            lse_o[pl.ds(h, 1), chunk(i)] = top + jnp.log(mass)
            probs = (weights * (1.0 / mass)).astype(BF16)
            hs = pl.ds(pl.multiple_of(h * HD, HD), HD)
            ht_o[hs, chunk(i)] = mm(vt[hs, ks], probs).astype(BF16)
            return carry

        lax.fori_loop(0, heads, one_head, 0)
        part[chunk(i), :] = t_mm(ht_o[:, chunk(i)], wout[...]).astype(BF16)
        core_copy(i).start()

    def sum_cores(i):
        core_copy(i).wait_recv()
        both = part[chunk(i), my_half].astype(F32) + cbuf[chunk(i), :].astype(F32)
        xbuf[x, chunk(i), :] = both.astype(BF16)
        for d in range(1, nx):
            x_copy(i, d).start()

    def sum_chips(i):
        for d in range(1, nx):
            x_arrival(i, d).wait_recv()
        total = xbuf[0, chunk(i), :].astype(F32)
        for j in range(1, nx):
            total = total + xbuf[j, chunk(i), :].astype(F32)
        attn_o[chunk(i), my_half] = total.astype(BF16)
        share_copy(i).start()

    def finish(i):
        share_arrival(i).wait_recv()
        hidden = tok[chunk(i), :].astype(F32) + attn_o[chunk(i), :].astype(F32)
        unit, _ = norm_rows(hidden)
        normed = (unit * g2[...] + b2[...]).astype(BF16)
        n2_o[chunk(i), :] = normed
        logits = mm(normed, mixw[...])
        lane = lax.broadcasted_iota(jnp.int32, logits.shape, 1)
        logits = jnp.where(lane < 2, logits, masked_value)
        mix = jnp.exp(logits - jnp.max(logits, axis=1, keepdims=True))
        mix_o[chunk(i), :] = mix / jnp.sum(mix, axis=1, keepdims=True)

    attend(0)
    attend(1)
    sum_cores(0)
    attend(2)
    sum_cores(1)
    attend(3)
    sum_cores(2)
    sum_cores(3)

    def forward_rows(i, carry):
        src = lax.rem(e + n_ep - 1 - i, n_ep)
        a2a_copy(e, src).wait_recv()
        remote(crow_o.at[c, src], crow_o.at[c, src], fs_.at[src], fr_.at[src], mate, e).start()
        return carry

    def forward_done(src, carry):
        remote(crow_o.at[1 - c, src], crow_o.at[1 - c, src], fs_.at[src], fr_.at[src], mate, e).wait()
        return carry

    for i in range(4):
        sum_chips(i)
        if i >= 1:
            finish(i - 1)
    finish(3)
    lax.fori_loop(0, n_ep - 1, forward_rows, 0)
    lax.fori_loop(0, n_ep, forward_done, 0)
    own.wait()

    def sent(i, carry):
        a2a_copy(lax.rem(e + 1 + i, n_ep), e).wait_send()
        return carry

    lax.fori_loop(0, n_ep - 1, sent, 0)
    for i in range(4):
        core_copy(i).wait_send()
        for d in range(1, nx):
            x_copy(i, d).wait_send()
        share_copy(i).wait_send()


def forward(tokens, cotangent, segments, routes, capacity, g1, b1, g2, b2, wqkv, wout, mix_weight):
    n_tp, n_ep = lax.axis_size("tp"), lax.axis_size("ep")
    rows, width = tokens.shape
    wl = wout.shape[0]
    experts = capacity.shape[0]
    slots = 3 * rows // (2 * experts)
    nx = n_tp // 2
    half = width // 2
    vm = pl.BlockSpec(memory_space=pltpu.VMEM)
    dma = pltpu.SemaphoreType.DMA
    shape = jax.ShapeDtypeStruct
    mixw = jnp.pad(mix_weight, ((0, 0), (0, 126)))
    return pl.pallas_call(
        functools.partial(forward_kernel, n_tp, n_ep),
        out_shape=(
            shape((3, rows, wl), BF16),
            shape((wl, rows), BF16),
            shape((wl // HD, rows), F32),
            shape((rows, width), BF16),
            shape((rows, width), BF16),
            shape((rows, 128), F32),
            shape((2, experts, slots, half), BF16),
            shape((1, rows), jnp.int32),
            shape((rows, 8), jnp.int32),
        ),
        in_specs=[vm] * 13,
        out_specs=(vm,) * 6 + (pl.BlockSpec(memory_space=pl.ANY), vm, vm),
        scratch_shapes=[
            pltpu.VMEM((rows, width), BF16),
            pltpu.VMEM((wl, rows), BF16),
            pltpu.VMEM((experts, slots, half), BF16),
            pltpu.VMEM((rows, width), BF16),
            pltpu.VMEM((rows, half), BF16),
            pltpu.VMEM((nx, rows, half), BF16),
            pltpu.VMEM((rows, rows // 4), F32),
            dma((experts,)), dma((experts,)), dma((experts,)), dma((experts,)),
            dma((4,)), dma((4,)), dma((4, max(nx - 1, 1))), dma((4, max(nx - 1, 1))), dma((4,)), dma((4,)),
            dma,
        ],
        compiler_params=pltpu.CompilerParams(
            collective_id=0, has_side_effects=True, vmem_limit_bytes=VMEM_LIMIT
        ),
        cost_estimate=pl.CostEstimate(flops=8 * 10**9, bytes_accessed=30 * 10**6, transcendentals=0),
        name="attention_forward",
    )(
        tokens, cotangent, segments, segments.reshape(rows, 1), routes.reshape(1, rows),
        capacity.reshape(experts, 1), g1.reshape(1, width), b1.reshape(1, width), g2.reshape(1, width),
        b2.reshape(1, width), wqkv, wout, mixw,
    )


def gelu_pair(v):
    c0 = math.sqrt(2.0 / math.pi)
    sq = v * v
    th = jnp.tanh(c0 * v * (1.0 + 0.044715 * sq))
    half_up = 0.5 + 0.5 * th
    slope = half_up + (0.5 * c0) * v * (1.0 - th * th) * (1.0 + (3.0 * 0.044715) * sq)
    return v * half_up, slope


class TpReduce:
    def __init__(self, nx, bufs, sems, span):
        self.part, self.cbuf, self.xrcv = bufs
        self.cs, self.cr, self.xs, self.xr = sems
        self.nx, self.span = nx, span
        self.t, self.x, self.c, self.e = place()
        self.mate = 2 * self.x + 1 - self.c

    def core(self, i):
        return remote(
            self.part.at[1 - self.c, :, self.span(i)], self.cbuf.at[:, self.span(i)],
            self.cs.at[i], self.cr.at[i], self.mate, self.e,
        )

    def chip(self, i, d):
        there = lax.rem(self.x + d, self.nx)
        return remote(
            self.cbuf.at[there, self.span(i)], self.xrcv.at[self.x, self.span(i)],
            self.xs.at[i, d - 1], self.xr.at[i, d - 1], 2 * there + self.c, self.e,
        )

    def arrival(self, i, d):
        src = lax.rem(self.x + self.nx - d, self.nx)
        return remote(
            self.cbuf.at[src, self.span(i)], self.xrcv.at[src, self.span(i)],
            self.xs.at[i, d - 1], self.xr.at[i, d - 1], 2 * src + self.c, self.e,
        ), src

    def start(self, i):
        self.core(i).start()

    def sum_cores(self, i):
        self.core(i).wait_recv()
        s = self.span(i)
        for j in range(self.nx):
            self.cbuf[j, s, :] = (
                self.part[self.c, j, s, :].astype(F32) + self.cbuf[j, s, :].astype(F32)
            ).astype(BF16)
        for d in range(1, self.nx):
            self.chip(i, d).start()

    def total(self, i):
        s = self.span(i)
        total = self.cbuf[self.x, s, :].astype(F32)
        for d in range(1, self.nx):
            copy, src = self.arrival(i, d)
            copy.wait_recv()
            total = total + self.xrcv[src, s, :].astype(F32)
        return total

    def sent(self, i):
        self.core(i).wait_send()
        for d in range(1, self.nx):
            self.chip(i, d).wait_send()


def dense_kernel(
    n_tp, n_ep, n2, tgt, cot, mix, up, down, wdiff,
    rows_o, gup_o, gdown_o, y_o, gshare_o, gmix_o,
    snd, act, gpre, gden, part, cbuf, xrcv,
    as_, ar_, xs_, xr_, ms_, mr_, lsem, rcs, rcr, rxs, rxr,
):
    t, x, c, e = place()
    nx = n_tp // 2
    rows_all, width = n2.shape
    slots, share = snd.shape[1], snd.shape[2]
    units = up.shape[1]
    blk = rows_all // 4
    mate = 2 * x + 1 - c
    x_peers = [2 * lax.rem(x + d, nx) + c for d in range(1, nx)]
    greet([(mate, e)] + [(p, e) for p in x_peers], lambda i: (t, lax.rem(e + 1 + i, n_ep)), n_ep - 1)
    my_cols = pl.ds(pl.multiple_of(t * share, share), share)

    def rows_for(dest):
        return mm(onehot_rows(tgt[...], dest * slots, slots), n2[:, my_cols]).astype(BF16)

    def a2a_copy(dest, src):
        return remote(snd.at[dest], rows_o.at[t, src], as_.at[dest], ar_.at[src], t, dest)

    def send_rows(i, carry):
        dest = lax.rem(e + 1 + i, n_ep)
        snd[dest] = rows_for(dest)
        a2a_copy(dest, e).start()
        return carry

    def x_copy(here, src, d):
        return remote(here, rows_o.at[t, src], xs_.at[src, d - 1], xr_.at[src, d - 1], x_peers[d - 1], e)

    def mate_copy(here, xi, src):
        return remote(here, rows_o.at[2 * xi + c, src], ms_.at[xi, src], mr_.at[xi, src], mate, e)

    def spread(here, src):
        for d in range(1, nx):
            x_copy(here, src, d).start()
        mate_copy(here, x, src).start()

    lax.fori_loop(0, n_ep - 1, send_rows, 0)
    snd[e] = rows_for(e)
    own = pltpu.make_async_copy(snd.at[e], rows_o.at[t, e], lsem)
    own.start()
    spread(snd.at[e], e)

    def source(k):
        return lax.rem(e + n_ep - k, n_ep)

    def spread_block(k, carry):
        src = source(k)
        a2a_copy(e, src).wait_recv()
        spread(rows_o.at[t, src], src)
        return carry

    def pass_block(k, carry):
        src = source(k)
        for d in range(1, nx):
            xi = lax.rem(x + nx - d, nx)
            got = rows_o.at[2 * xi + c, src]
            remote(got, got, xs_.at[src, d - 1], xr_.at[src, d - 1], mate, e).wait_recv()
            mate_copy(got, xi, src).start()
        return carry

    def end_block(src, carry):
        for xi in range(nx):
            got = rows_o.at[2 * xi + 1 - c, src]
            remote(got, got, ms_.at[xi, src], mr_.at[xi, src], mate, e).wait()
        for d in range(1, nx):
            x_copy(rows_o.at[t, src], src, d).wait_send()
        return carry

    def chunk(i):
        return pl.ds(i * blk, blk)

    reduce = TpReduce(nx, (part, cbuf, xrcv), (rcs, rcr, rxs, rxr), chunk)
    fblk = min(256, units)
    steps = units // fblk

    def dense(i, tally):
        rs = chunk(i)
        mix0, mix1 = mix[rs, 0:1], mix[rs, 1:2]
        gden[rs, :] = (mix0 * cot[rs, :].astype(F32)).astype(BF16)

        def one(f, carry):
            fs = pl.ds(pl.multiple_of(f * fblk, fblk), fblk)
            value, slope = gelu_pair(mm(n2[rs, :], up[:, fs]))
            act[rs, fs] = value.astype(BF16)
            gpre[rs, fs] = (mm_t(gden[rs, :], down[fs, :]) * slope).astype(BF16)
            return carry

        lax.fori_loop(0, steps, one, 0)
        col0 = jnp.zeros((blk, 1), F32)
        for g in range(n_tp):
            gs = pl.ds(g * share, share)
            dense_part = mm(act[rs, :], down[:, gs])
            col0 = col0 + jnp.sum(dense_part * cot[rs, gs].astype(F32), axis=1, keepdims=True)
            y_o[g % 2, g // 2, rs, :] = (mix0 * dense_part).astype(BF16)
        logit = mix0 * mix1 * col0
        for g in range(n_tp):
            gs = pl.ds(g * share, share)
            back = mm_t(gpre[rs, :], up[gs, :]) + logit * wdiff[:, gs]
            part[g % 2, g // 2, rs, :] = back.astype(BF16)
        reduce.start(i)
        return tally + jnp.sum(logit * n2[rs, :].astype(F32), axis=0, keepdims=True)

    ends = [1 + (n_ep - 1) * k // 4 for k in range(5)]
    tally = dense(0, jnp.zeros((1, width), F32))
    lax.fori_loop(ends[0], ends[1], spread_block, 0)
    tally = dense(1, tally)
    reduce.sum_cores(0)
    pass_block(0, 0)
    lax.fori_loop(ends[1], ends[2], spread_block, 0)
    lax.fori_loop(ends[0], ends[1], pass_block, 0)
    tally = dense(2, tally)
    reduce.sum_cores(1)
    lax.fori_loop(ends[2], ends[3], spread_block, 0)
    lax.fori_loop(ends[1], ends[2], pass_block, 0)
    tally = dense(3, tally)
    reduce.sum_cores(2)
    lax.fori_loop(ends[3], ends[4], spread_block, 0)
    lax.fori_loop(ends[2], ends[3], pass_block, 0)
    reduce.sum_cores(3)
    gmix_o[...] = jnp.broadcast_to(tally, gmix_o.shape)
    for k in range(steps):
        fs = pl.ds(k * fblk, fblk)
        gdown_o[fs, :] = t_mm(act[:, fs], gden[...]).astype(BF16)
    for k in range(4):
        ws = pl.ds(k * (width // 4), width // 4)
        gup_o[ws, :] = t_mm(n2[:, ws], gpre[...]).astype(BF16)
    lax.fori_loop(ends[3], ends[4], pass_block, 0)
    for i in range(4):
        gshare_o[chunk(i), :] = reduce.total(i)
    lax.fori_loop(0, n_ep, end_block, 0)
    own.wait()

    def sent(i, carry):
        a2a_copy(lax.rem(e + 1 + i, n_ep), e).wait_send()
        return carry

    lax.fori_loop(0, n_ep - 1, sent, 0)
    for i in range(4):
        reduce.sent(i)


def dense_block(n2, targets, cotangent, mix, up, down, wdiff, experts):
    n_tp, n_ep = lax.axis_size("tp"), lax.axis_size("ep")
    rows, width = n2.shape
    slots = 3 * rows // (2 * experts)
    units = up.shape[1]
    nx, share = n_tp // 2, width // n_tp
    dx = max(nx - 1, 1)
    vm = pl.BlockSpec(memory_space=pltpu.VMEM)
    dma = pltpu.SemaphoreType.DMA
    shape = jax.ShapeDtypeStruct
    return pl.pallas_call(
        functools.partial(dense_kernel, n_tp, n_ep),
        out_shape=(
            shape((n_tp, experts, slots, share), BF16),
            shape((width, units), BF16),
            shape((units, width), BF16),
            shape((2, nx, rows, share), BF16),
            shape((rows, share), F32),
            shape((8, width), F32),
        ),
        in_specs=[vm] * 7,
        out_specs=(pl.BlockSpec(memory_space=pl.ANY),) + (vm,) * 5,
        scratch_shapes=[
            pltpu.VMEM((experts, slots, share), BF16),
            pltpu.VMEM((rows, units), BF16),
            pltpu.VMEM((rows, units), BF16),
            pltpu.VMEM((rows, width), BF16),
            pltpu.VMEM((2, nx, rows, share), BF16),
            pltpu.VMEM((nx, rows, share), BF16),
            pltpu.VMEM((nx, rows, share), BF16),
            dma((experts,)), dma((experts,)), dma((experts, dx)), dma((experts, dx)),
            dma((nx, experts)), dma((nx, experts)), dma,
            dma((4,)), dma((4,)), dma((4, dx)), dma((4, dx)),
        ],
        compiler_params=pltpu.CompilerParams(
            collective_id=1, has_side_effects=True, vmem_limit_bytes=VMEM_LIMIT
        ),
        cost_estimate=pl.CostEstimate(flops=16 * 10**9, bytes_accessed=30 * 10**6, transcendentals=0),
        name="dense_and_dispatch",
    )(n2, targets, cotangent, mix, up, down, wdiff)


def expert_kernel(
    n_tp, n_ep, rows, crow, eup, edown, mixw, wdiff, gshare, tgtc,
    geup_o, gedown_o, yr_o, gsec_o, gmix_o,
    act, gpre, grow, part, cbuf, xrcv, rsnd, ret,
    rcs, rcr, rxs, rxr, as_, ar_, lsem, gxs, gxr, gms, gmr,
):
    t, x, c, e = place()
    nx = n_tp // 2
    experts, slots, share = rows.shape[1:]
    total_rows = experts * slots
    half = crow.shape[3]
    width = 2 * half
    units = eup.shape[1]
    nb = experts // 4
    size = nb * slots
    tok_rows = tgtc.shape[0]
    blk = tok_rows // 4
    mate = 2 * x + 1 - c
    x_peers = [2 * lax.rem(x + d, nx) + c for d in range(1, nx)]
    greet([(mate, e)] + [(p, e) for p in x_peers], lambda i: (t, lax.rem(e + 1 + i, n_ep)), n_ep - 1)

    def piece(i):
        return lax.rem(lax.div(e, nb) + 1 + i, 4)

    def span(i):
        return pl.ds(pl.multiple_of(piece(i) * size, size), size)

    reduce = TpReduce(nx, (part, cbuf, xrcv), (rcs, rcr, rxs, rxr), span)
    fblk = min(256, units)
    steps = units // fblk
    gmix_o[...] = jnp.zeros_like(gmix_o)

    def a2a_copy(dest, src):
        return remote(
            rsnd.at[pl.ds(pl.multiple_of(dest * slots, slots), slots)],
            ret.at[pl.ds(pl.multiple_of(src * slots, slots), slots)],
            as_.at[dest], ar_.at[src], t, dest,
        )

    def work(i):
        bs = pl.ds(piece(i) * nb, nb)
        rs = span(i)

        def share_rows(g):
            return rows[g, bs].reshape(size, share)

        logits = jnp.zeros((size, 128), F32)
        for g in range(n_tp):
            logits = logits + mm(share_rows(g), mixw[pl.ds(g * share, share), :])
        lane = lax.broadcasted_iota(jnp.int32, logits.shape, 1)
        logits = jnp.where(lane < 2, logits, masked_value)
        mix = jnp.exp(logits - jnp.max(logits, axis=1, keepdims=True))
        mix = mix / jnp.sum(mix, axis=1, keepdims=True)
        mix0, mix1 = mix[:, 0:1], mix[:, 1:2]
        for h in range(2):
            grow[rs, pl.ds(h * half, half)] = (mix1 * crow[h, bs].reshape(size, half).astype(F32)).astype(BF16)

        def one(f, carry):
            fs = pl.ds(pl.multiple_of(f * fblk, fblk), fblk)
            pre = mm(share_rows(0), eup[pl.ds(0, share), fs])
            for g in range(1, n_tp):
                pre = pre + mm(share_rows(g), eup[pl.ds(g * share, share), fs])
            value, slope = gelu_pair(pre)
            act[rs, fs] = value.astype(BF16)
            gpre[rs, fs] = (mm_t(grow[rs, :], edown[fs, :]) * slope).astype(BF16)
            return carry

        lax.fori_loop(0, steps, one, 0)
        col1 = jnp.zeros((size, 1), F32)
        per_half = n_tp // 2
        for g in range(n_tp):
            gs = pl.ds(g * share, share)
            eout = mm(act[rs, :], edown[:, gs])
            cots = crow[g // per_half, bs, :, pl.ds((g % per_half) * share, share)].reshape(size, share)
            col1 = col1 + jnp.sum(eout * cots.astype(F32), axis=1, keepdims=True)
            yr_o[g % 2, g // 2, rs, :] = (mix1 * eout).astype(BF16)
        logit = -(mix0 * mix1 * col1)
        for g in range(n_tp):
            gs = pl.ds(g * share, share)
            back = mm_t(gpre[rs, :], eup[gs, :]) + logit * wdiff[:, gs]
            part[g % 2, g // 2, rs, :] = back.astype(BF16)
            tally = jnp.sum(logit * share_rows(g).astype(F32), axis=0, keepdims=True)
            gmix_o[:, gs] = gmix_o[:, gs] + jnp.broadcast_to(tally, (8, share))
        reduce.start(i)

    def send_back(i):
        rs = span(i)
        rsnd[rs, :] = reduce.total(i).astype(BF16)

        def one(k, carry):
            dest = piece(i) * nb + k

            @pl.when(dest != e)
            def _():
                a2a_copy(dest, e).start()

            @pl.when(dest == e)
            def _():
                mine = pl.ds(pl.multiple_of(e * slots, slots), slots)
                pltpu.make_async_copy(rsnd.at[mine], ret.at[mine], lsem).start()

            return carry

        lax.fori_loop(0, nb, one, 0)

    def step(i, carry):
        work(i)

        @pl.when(i >= 1)
        def _():
            reduce.sum_cores(i - 1)

        @pl.when(i >= 2)
        def _():
            send_back(i - 2)

        return carry

    lax.fori_loop(0, 4, step, 0)
    reduce.sum_cores(3)

    def down_grad(k):
        fs = pl.ds(k * fblk, fblk)
        gedown_o[fs, :] = t_mm(act[:, fs], grow[...])

    def up_grad(g):
        geup_o[pl.ds(g * share, share), :] = t_mm(rows[g].reshape(total_rows, share), gpre[...])

    for k in range(steps):
        down_grad(k)
        if k == steps // 2:
            send_back(2)
    send_back(3)
    for g in range(n_tp):
        up_grad(g)

    def arrived(k, carry):
        src = lax.rem(e + n_ep - k, n_ep)
        a2a_copy(e, src).wait_recv()
        return carry

    lax.fori_loop(1, n_ep, arrived, 0)
    mine = pl.ds(pl.multiple_of(e * slots, slots), slots)
    pltpu.make_async_copy(rsnd.at[mine], ret.at[mine], lsem).wait()

    gather = TpGather(nx, gsec_o, share, blk, (gxs, gxr, gms, gmr))
    for i in range(4):
        cs = pl.ds(i * blk, blk)
        hot = (lax.broadcasted_iota(jnp.int32, (blk, total_rows), 1) == tgtc[cs, 0:1]).astype(F32).astype(BF16)
        gather.put(i, (gshare[cs, :] + mm(hot, ret[...])).astype(BF16))
    for i in range(4):
        gather.pass_on(i)
    for i in range(4):
        gather.finish(i)

    def sent(k, carry):
        a2a_copy(lax.rem(e + k, n_ep), e).wait_send()
        return carry

    lax.fori_loop(1, n_ep, sent, 0)
    for i in range(4):
        reduce.sent(i)


class TpGather:
    def __init__(self, nx, full, share, blk, sems):
        self.full, self.share, self.blk, self.nx = full, share, blk, nx
        self.xs, self.xr, self.ms, self.mr = sems
        self.t, self.x, self.c, self.e = place()
        self.mate = 2 * self.x + 1 - self.c

    def cut(self, i, g):
        return self.full.at[
            pl.ds(i * self.blk, self.blk), pl.ds(pl.multiple_of(g * self.share, self.share), self.share)
        ]

    def across(self, i, d):
        there = 2 * lax.rem(self.x + d, self.nx) + self.c
        mine = self.cut(i, self.t)
        return remote(mine, mine, self.xs.at[i, d - 1], self.xr.at[i, d - 1], there, self.e)

    def beside(self, i, xi, c):
        got = self.cut(i, 2 * xi + c)
        return remote(got, got, self.ms.at[i, xi], self.mr.at[i, xi], self.mate, self.e)

    def put(self, i, value):
        cols = pl.ds(pl.multiple_of(self.t * self.share, self.share), self.share)
        self.full[pl.ds(i * self.blk, self.blk), cols] = value
        for d in range(1, self.nx):
            self.across(i, d).start()
        self.beside(i, self.x, self.c).start()

    def pass_on(self, i):
        for d in range(1, self.nx):
            xi = lax.rem(self.x + self.nx - d, self.nx)
            got = self.cut(i, 2 * xi + self.c)
            remote(got, got, self.xs.at[i, d - 1], self.xr.at[i, d - 1], self.mate, self.e).wait_recv()
            self.beside(i, xi, self.c).start()

    def finish(self, i):
        for xi in range(self.nx):
            self.beside(i, xi, 1 - self.c).wait_recv()
            self.beside(i, xi, self.c).wait_send()
        for d in range(1, self.nx):
            self.across(i, d).wait_send()


def expert_block(rows, cot_rows, eup, edown, mix_weight, wdiff, gshare, targets_col):
    n_tp, n_ep = lax.axis_size("tp"), lax.axis_size("ep")
    _, experts, slots, share = rows.shape
    tok_rows = targets_col.shape[0]
    width, units = eup.shape
    nx = n_tp // 2
    dx = max(nx - 1, 1)
    total = experts * slots
    vm = pl.BlockSpec(memory_space=pltpu.VMEM)
    dma = pltpu.SemaphoreType.DMA
    shape = jax.ShapeDtypeStruct
    mixw = jnp.pad(mix_weight, ((0, 0), (0, 126)))
    return pl.pallas_call(
        functools.partial(expert_kernel, n_tp, n_ep),
        out_shape=(
            shape((width, units), F32),
            shape((units, width), F32),
            shape((2, nx, total, share), BF16),
            shape((tok_rows, width), BF16),
            shape((8, width), F32),
        ),
        in_specs=[vm] * 8,
        out_specs=(vm,) * 5,
        scratch_shapes=[
            pltpu.VMEM((total, units), BF16),
            pltpu.VMEM((total, units), BF16),
            pltpu.VMEM((total, width), BF16),
            pltpu.VMEM((2, nx, total, share), BF16),
            pltpu.VMEM((nx, total, share), BF16),
            pltpu.VMEM((nx, total, share), BF16),
            pltpu.VMEM((total, share), BF16),
            pltpu.VMEM((total, share), BF16),
            dma((4,)), dma((4,)), dma((4, dx)), dma((4, dx)),
            dma((experts,)), dma((experts,)), dma,
            dma((4, dx)), dma((4, dx)), dma((4, nx)), dma((4, nx)),
        ],
        compiler_params=pltpu.CompilerParams(
            collective_id=2, has_side_effects=True, vmem_limit_bytes=VMEM_LIMIT
        ),
        cost_estimate=pl.CostEstimate(flops=24 * 10**9, bytes_accessed=50 * 10**6, transcendentals=0),
        name="experts",
    )(rows, cot_rows, eup, edown, mixw, wdiff, gshare, targets_col)


class TpSum:
    def __init__(self, nx, full, bufs, sems, blk):
        self.full, self.blk, self.nx = full, blk, nx
        self.part, self.cbuf, self.xbuf = bufs
        self.cs, self.cr, self.xs, self.xr, self.gs, self.gr = sems
        self.t, self.x, self.c, self.e = place()
        self.mate = 2 * self.x + 1 - self.c
        half = self.cbuf.shape[1]
        self.mine = pl.ds(pl.multiple_of(self.c * half, half), half)
        self.other = pl.ds(pl.multiple_of((1 - self.c) * half, half), half)

    def span(self, i):
        return pl.ds(i * self.blk, self.blk)

    def core(self, i):
        return remote(
            self.part.at[self.span(i), self.other], self.cbuf.at[self.span(i)], self.cs.at[i], self.cr.at[i],
            self.mate, self.e,
        )

    def chip(self, i, d):
        there = 2 * lax.rem(self.x + d, self.nx) + self.c
        mine = self.xbuf.at[self.x, self.span(i)]
        return remote(mine, mine, self.xs.at[i, d - 1], self.xr.at[i, d - 1], there, self.e)

    def start(self, i):
        self.core(i).start()

    def sum_cores(self, i):
        self.core(i).wait_recv()
        both = self.part[self.span(i), self.mine].astype(F32) + self.cbuf[self.span(i), :].astype(F32)
        self.xbuf[self.x, self.span(i), :] = both.astype(BF16)
        for d in range(1, self.nx):
            self.chip(i, d).start()

    def share(self, i, cols):
        got = self.full.at[self.span(i), cols]
        return remote(got, got, self.gs.at[i], self.gr.at[i], self.mate, self.e)

    def sum_chips(self, i):
        for d in range(1, self.nx):
            src = lax.rem(self.x + self.nx - d, self.nx)
            got = self.xbuf.at[src, self.span(i)]
            remote(got, got, self.xs.at[i, d - 1], self.xr.at[i, d - 1], self.mate, self.e).wait_recv()
        total = self.xbuf[0, self.span(i), :].astype(F32)
        for j in range(1, self.nx):
            total = total + self.xbuf[j, self.span(i), :].astype(F32)
        self.full[self.span(i), self.mine] = total.astype(BF16)
        self.share(i, self.mine).start()

    def wait(self, i):
        self.share(i, self.other).wait_recv()
        self.share(i, self.mine).wait_send()

    def sent(self, i):
        self.core(i).wait_send()
        for d in range(1, self.nx):
            self.chip(i, d).wait_send()


class EpSum:
    def __init__(self, data, land, full, first, rows, order, sems, base):
        self.data, self.land, self.full = data, land, full
        self.first, self.rows, self.order, self.base = first, rows, order, base
        self.ss, self.rs = sems
        self.t, self.x, self.c, self.e = place()
        self.low = [0]
        for s, b in enumerate(order):
            self.low.append(self.low[-1] + self.bit(b) * (rows >> (s + 1)))

    def bit(self, b):
        return lax.rem(lax.div(self.e, 2**b), 2)

    def cut(self, low, size):
        return pl.ds(pl.multiple_of(self.first + low, 16), size)

    def partner(self, b):
        return self.e + (1 - 2 * self.bit(b)) * 2**b

    def halves(self, s):
        size = self.rows >> (s + 1)
        bit = self.bit(self.order[s])
        return self.cut(self.low[s] + bit * size, size), self.cut(self.low[s] + (1 - bit) * size, size), size

    def out(self, s):
        _, give, size = self.halves(s)
        landing = self.first + self.rows - (self.rows >> s)
        return remote(
            self.data.at[give], self.land.at[pl.ds(landing, size)], self.ss.at[self.base, s],
            self.rs.at[self.base, s], self.t, self.partner(self.order[s]),
        )

    def back(self, s, arriving):
        keep, give, _ = self.halves(s)
        k = len(self.order) + s
        part = self.full.at[give if arriving else keep]
        return remote(
            part, part, self.ss.at[self.base, k], self.rs.at[self.base, k], self.t, self.partner(self.order[s])
        )

    def start(self, s):
        self.out(s).start()

    def add(self, s):
        self.out(s).wait_recv()
        keep, _, size = self.halves(s)
        landing = self.first + self.rows - (self.rows >> s)
        into = self.full if s == len(self.order) - 1 else self.data
        into[keep, :] = (
            self.data[keep, :].astype(F32) + self.land[pl.ds(landing, size), :].astype(F32)
        ).astype(BF16)

    def give_back(self, s):
        self.back(s, False).start()

    def take_back(self, s):
        self.back(s, True).wait_recv()

    def sent(self):
        for s in range(len(self.order)):
            self.out(s).wait_send()
            self.back(s, False).wait_send()


def backward_kernel(
    n_tp, n_ep, tok, cot, attn, gsec, qkv, ht, lse, wqkv, wout, g1, b1, g2, segr, segc, y, yr, tgtc, gmix,
    out_o, gtok_o, wsum_o, small_o,
    gh, ga, gheads, kt, dqt, pcat, dcat, gcat, qcat, dk, dv, gj, bias,
    part, cbuf, xbuf, wdat, wland, ycbuf, yxrcv, rcbuf, rxrcv, rsnd, ret, small, sland, mland,
    tcs, tcr, txs, txr, tgs, tgr, wss, wrs, ycs, ycr, yxs, yxr, rcs, rcr, rxs, rxr, as_, ar_, lsem,
    oxs, oxr, oms, omr, ss_, sr_, mgs, mgr,
):
    t, x, c, e = place()
    nx = n_tp // 2
    rows_all, width = tok.shape
    wl = wout.shape[0]
    heads = wl // HD
    blk = rows_all // 4
    total_rows, share = yr.shape[2], yr.shape[3]
    experts = ar_.shape[0]
    slots = total_rows // experts
    nb = experts // 4
    size = nb * slots
    greet(
        [(lax.rem(t + d, n_tp), e) for d in range(1, n_tp)], lambda i: (t, lax.rem(e + 1 + i, n_ep)), n_ep - 1
    )

    def chunk(i):
        return pl.ds(i * blk, blk)

    def piece(i):
        return lax.rem(lax.div(e, nb) + 1 + i, 4)

    def span(i):
        return pl.ds(pl.multiple_of(piece(i) * size, size), size)

    back_rows = TpReduce(nx, (yr, rcbuf, rxrcv), (rcs, rcr, rxs, rxr), span)
    back_dense = TpReduce(nx, (y, ycbuf, yxrcv), (ycs, ycr, yxs, yxr), chunk)
    tp_sum = TpSum(nx, gtok_o, (part, cbuf, xbuf), (tcs, tcr, txs, txr, tgs, tgr), blk)
    gather = TpGather(nx, out_o, share, blk, (oxs, oxr, oms, omr))
    bits = n_ep.bit_length() - 1
    cuts = wss.shape[0]
    wrows = 4 * wl // cuts
    natural = list(range(bits))
    swapped = [natural[1], natural[0]] + natural[2:]
    sums = [
        EpSum(wdat, wland, wsum_o, k * wrows, wrows, swapped if k == 3 else natural, (wss, wrs), k) for k in range(cuts)
    ]

    def a2a_copy(dest, src):
        return remote(
            rsnd.at[pl.ds(pl.multiple_of(dest * slots, slots), slots)],
            ret.at[pl.ds(pl.multiple_of(src * slots, slots), slots)],
            as_.at[dest], ar_.at[src], t, dest,
        )

    def send_back(i):
        rsnd[span(i), :] = back_rows.total(i).astype(BF16)

        def one(k, carry):
            dest = piece(i) * nb + k

            @pl.when(dest != e)
            def _():
                a2a_copy(dest, e).start()

            @pl.when(dest == e)
            def _():
                mine = pl.ds(pl.multiple_of(e * slots, slots), slots)
                pltpu.make_async_copy(rsnd.at[mine], ret.at[mine], lsem).start()

            return carry

        lax.fori_loop(0, nb, one, 0)

    def mix_copy(d):
        return remote(gmix, mland.at[t], mgs.at[d - 1], mgr.at[d - 1], lax.rem(t + d, n_tp), e)

    mland[t] = gmix[...]
    for d in range(1, n_tp):
        mix_copy(d).start()
    for i in range(4):
        back_rows.start(i)
    for i in range(4):
        back_dense.start(i)

    sum_gain = jnp.zeros((1, width), F32)
    sum_bias = jnp.zeros((1, width), F32)
    for i in range(4):
        rs = chunk(i)
        unit, spread = norm_rows(tok[rs, :].astype(F32) + attn[rs, :].astype(F32))
        up = gsec[rs, :].astype(F32)
        sum_gain = sum_gain + jnp.sum(up * unit, axis=0, keepdims=True)
        sum_bias = sum_bias + jnp.sum(up, axis=0, keepdims=True)
        gv = up * g2[...]
        inner = gv - jnp.mean(gv, axis=-1, keepdims=True) - unit * jnp.mean(gv * unit, axis=-1, keepdims=True)
        grad = cot[rs, :].astype(F32) + spread * inner
        gh[rs, :] = grad
        ga[rs, :] = grad.astype(BF16)
        gheads[rs, :] = mm_t(ga[rs, :], wout[...]).astype(BF16)
        back_rows.sum_cores(i)
    small[...] = jnp.zeros_like(small)
    small[2:3, :] = sum_gain
    small[3:4, :] = sum_bias
    wdat[pl.ds(3 * wl, wl), :] = mm(ht[...], ga[...]).astype(BF16)
    if cuts == 4:
        sums[3].start(0)
    for i in range(4):
        rs = chunk(i)
        unit, _ = norm_rows(tok[rs, :].astype(F32))
        ga[rs, :] = (unit * g1[...] + b1[...]).astype(BF16)
        kt[:, rs] = qkv[1, rs, :].astype(F32).T.astype(BF16)

    group = pcat.shape[1] // blk
    head_of = lax.div(lax.broadcasted_iota(jnp.int32, (blk, wl), 1), HD)

    def attend(i):
        keys = (i + 1) * blk
        ks = pl.ds(0, keys)
        allowed = (segc[ks, :] == segr[:, chunk(i)]) & (
            lax.broadcasted_iota(jnp.int32, (keys, blk), 0)
            <= lax.broadcasted_iota(jnp.int32, (keys, blk), 1) + i * blk
        )
        bias[ks, :] = jnp.where(allowed, 0.0, masked_value)

        def one_head(first, k, carry):
            h = first + k
            q_h = jnp.where(head_of == h, qkv[0, chunk(i), :].astype(F32) * 0.125, 0.0).astype(BF16)
            g_h = jnp.where(head_of == h, gheads[chunk(i), :].astype(F32), 0.0).astype(BF16)
            hb = pl.ds(pl.multiple_of(k * blk, blk), blk)
            gcat[hb, :] = g_h
            qcat[hb, :] = q_h
            probs = jnp.exp(mm_t(qkv[1, ks, :], q_h) + bias[ks, :] - lse[pl.ds(h, 1), chunk(i)])
            pcat[ks, hb] = probs.astype(BF16)
            grad = mm_t(qkv[2, ks, :], g_h)
            mean = jnp.sum(probs * grad, axis=0, keepdims=True)
            scores = (probs * (grad - mean)).astype(BF16)
            dcat[ks, hb] = scores
            hs = pl.ds(pl.multiple_of(h * HD, HD), HD)
            dqt[hs, :] = mm(kt[hs, ks], scores)
            return carry

        for first in range(0, heads, group):
            lax.fori_loop(0, group, functools.partial(one_head, first), 0)
            dv_new, dk_new = mm(pcat[ks, :], gcat[...]), mm(dcat[ks, :], qcat[...])
            if i == 3 and first == 0:
                dv[ks, :] = dv_new
                dk[ks, :] = dk_new
            else:
                dv[ks, :] = dv[ks, :] + dv_new
                dk[ks, :] = dk[ks, :] + dk_new
        gj[0, chunk(i), :] = (dqt[...].T * 0.125).astype(BF16)
        gj[1, chunk(i), :] = dk[chunk(i), :].astype(BF16)
        gj[2, chunk(i), :] = dv[chunk(i), :].astype(BF16)
        grad_in = mm_t(gj[0, chunk(i), :], wqkv[0])
        for j in range(1, 3):
            grad_in = grad_in + mm_t(gj[j, chunk(i), :], wqkv[j])
        part[chunk(i), :] = grad_in.astype(BF16)
        tp_sum.start(i)

    attend(3)
    send_back(0)
    attend(2)
    tp_sum.sum_cores(3)
    send_back(1)
    attend(1)
    tp_sum.sum_cores(2)
    send_back(2)
    attend(0)
    tp_sum.sum_cores(1)
    for j in range(3):
        wdat[pl.ds(j * wl, wl), :] = t_mm(gj[j], ga[...]).astype(BF16)
        if cuts == 4:
            sums[j].start(0)
    if cuts != 4:
        for one_sum in sums:
            one_sum.start(0)
    tp_sum.sum_cores(0)
    send_back(3)
    for i in range(4):
        back_dense.sum_cores(i)

    tally = [jnp.zeros((1, width), F32), jnp.zeros((1, width), F32)]

    def finish(i):
        rs = chunk(i)
        tp_sum.wait(i)
        unit, spread = norm_rows(tok[rs, :].astype(F32))
        up = gtok_o[rs, :].astype(F32)
        tally[0] = tally[0] + jnp.sum(up * unit, axis=0, keepdims=True)
        tally[1] = tally[1] + jnp.sum(up, axis=0, keepdims=True)
        gv = up * g1[...]
        inner = gv - jnp.mean(gv, axis=-1, keepdims=True) - unit * jnp.mean(gv * unit, axis=-1, keepdims=True)
        gtok_o[rs, :] = (gh[rs, :] + spread * inner).astype(BF16)

    order = [3] * (cuts == 4) + list(range(min(cuts, 3)))

    def reduce_step(s):
        for k in order:
            sums[k].add(s)
            if s + 1 < bits:
                sums[k].start(s + 1)
            else:
                sums[k].give_back(s)

    tp_sum.sum_chips(3)
    tp_sum.sum_chips(2)
    finish(3)
    reduce_step(0)
    tp_sum.sum_chips(1)
    finish(2)
    for s in range(1, bits - 1):
        reduce_step(s)
    tp_sum.sum_chips(0)
    finish(1)
    if bits > 1:
        reduce_step(bits - 1)
    finish(0)
    small[0:1, :] = tally[0]
    small[1:2, :] = tally[1]
    mix_total = jnp.zeros((1, width), F32)
    for d in range(1, n_tp):
        got = mland.at[lax.rem(t + n_tp - d, n_tp)]
        remote(got, got, mgs.at[d - 1], mgr.at[d - 1], lax.rem(t + d, n_tp), e).wait_recv()
    for j in range(n_tp):
        mix_total = mix_total + mland[j, 0:1, :]
    small[4:5, :] = mix_total
    sland[e] = small[...]

    def small_copy(dest, src):
        return remote(small, sland.at[src], ss_.at[dest], sr_.at[src], t, dest)

    def send_small(k, carry):
        small_copy(lax.rem(e + k, n_ep), e).start()
        return carry

    lax.fori_loop(1, n_ep, send_small, 0)

    def arrived(k, carry):
        a2a_copy(e, lax.rem(e + n_ep - k, n_ep)).wait_recv()
        return carry

    lax.fori_loop(1, n_ep, arrived, 0)
    mine = pl.ds(pl.multiple_of(e * slots, slots), slots)
    pltpu.make_async_copy(rsnd.at[mine], ret.at[mine], lsem).wait()
    my_cols = pl.ds(pl.multiple_of(t * share, share), share)
    for i in range(4):
        rs = chunk(i)
        hot = (lax.broadcasted_iota(jnp.int32, (blk, total_rows), 1) == tgtc[rs, 0:1]).astype(F32).astype(BF16)
        hidden = tok[rs, my_cols].astype(F32) + attn[rs, my_cols].astype(F32)
        gather.put(i, (hidden + back_dense.total(i) + mm(hot, ret[...])).astype(BF16))

    for s in range(bits - 1, -1, -1):
        for k in order:
            sums[k].take_back(s)
            if s > 0:
                sums[k].give_back(s - 1)
        if s == bits - 1:
            for i in range(4):
                gather.pass_on(i)
    for i in range(4):
        gather.finish(i)

    def small_arrived(k, carry):
        small_copy(e, lax.rem(e + n_ep - k, n_ep)).wait_recv()
        return carry

    lax.fori_loop(1, n_ep, small_arrived, 0)
    small_o[...] = lax.fori_loop(0, n_ep, lambda k, total: total + sland[k], jnp.zeros_like(small_o))

    def sent(k, carry):
        dest = lax.rem(e + k, n_ep)
        a2a_copy(dest, e).wait_send()
        small_copy(dest, e).wait_send()
        return carry

    lax.fori_loop(1, n_ep, sent, 0)
    for d in range(1, n_tp):
        mix_copy(d).wait_send()
    for i in range(4):
        back_rows.sent(i)
        back_dense.sent(i)
        tp_sum.sent(i)
    for one_sum in sums:
        one_sum.sent()


def backward(tokens, cotangent, attn, gsec, qkv, ht, lse, wqkv, wout, g1, b1, g2, segments, y, yr, targets_col, gmix, experts):
    n_tp, n_ep = lax.axis_size("tp"), lax.axis_size("ep")
    rows, width = tokens.shape
    wl = wout.shape[0]
    total, share = yr.shape[2:]
    nx = n_tp // 2
    dx = max(nx - 1, 1)
    blk = rows // 4
    group = min(2, wl // HD)
    half = width // 2
    bits = n_ep.bit_length() - 1
    cuts = max(q for q in (4, 1) if 4 * wl // q >= 16 * n_ep or q == 1)
    vm = pl.BlockSpec(memory_space=pltpu.VMEM)
    dma = pltpu.SemaphoreType.DMA
    shape = jax.ShapeDtypeStruct
    return pl.pallas_call(
        functools.partial(backward_kernel, n_tp, n_ep),
        out_shape=(
            shape((rows, width), BF16),
            shape((rows, width), BF16),
            shape((4 * wl, width), BF16),
            shape((8, width), F32),
        ),
        in_specs=[vm] * 18,
        out_specs=(vm,) * 4,
        scratch_shapes=[
            pltpu.VMEM((rows, width), F32),
            pltpu.VMEM((rows, width), BF16),
            pltpu.VMEM((rows, wl), BF16),
            pltpu.VMEM((wl, rows), BF16),
            pltpu.VMEM((wl, blk), F32),
            pltpu.VMEM((rows, group * blk), BF16),
            pltpu.VMEM((rows, group * blk), BF16),
            pltpu.VMEM((group * blk, wl), BF16),
            pltpu.VMEM((group * blk, wl), BF16),
            pltpu.VMEM((rows, wl), F32),
            pltpu.VMEM((rows, wl), F32),
            pltpu.VMEM((3, rows, wl), BF16),
            pltpu.VMEM((rows, blk), F32),
            pltpu.VMEM((rows, width), BF16),
            pltpu.VMEM((rows, half), BF16),
            pltpu.VMEM((nx, rows, half), BF16),
            pltpu.VMEM((4 * wl, width), BF16),
            pltpu.VMEM((4 * wl, width), BF16),
            pltpu.VMEM((nx, rows, share), BF16),
            pltpu.VMEM((nx, rows, share), BF16),
            pltpu.VMEM((nx, total, share), BF16),
            pltpu.VMEM((nx, total, share), BF16),
            pltpu.VMEM((total, share), BF16),
            pltpu.VMEM((total, share), BF16),
            pltpu.VMEM((8, width), F32),
            pltpu.VMEM((n_ep, 8, width), F32),
            pltpu.VMEM((n_tp, 8, width), F32),
            dma((4,)), dma((4,)), dma((4, dx)), dma((4, dx)), dma((4,)), dma((4,)),
            dma((cuts, 2 * bits)), dma((cuts, 2 * bits)),
            dma((4,)), dma((4,)), dma((4, dx)), dma((4, dx)),
            dma((4,)), dma((4,)), dma((4, dx)), dma((4, dx)),
            dma((n_ep,)), dma((n_ep,)), dma,
            dma((4, dx)), dma((4, dx)), dma((4, nx)), dma((4, nx)),
            dma((n_ep,)), dma((n_ep,)), dma((n_tp,)), dma((n_tp,)),
        ],
        compiler_params=pltpu.CompilerParams(
            collective_id=3, has_side_effects=True, vmem_limit_bytes=VMEM_LIMIT + 3 * 2**20
        ),
        cost_estimate=pl.CostEstimate(flops=16 * 10**9, bytes_accessed=50 * 10**6, transcendentals=0),
        name="attention_backward",
    )(
        tokens, cotangent, attn, gsec, qkv, ht, lse, wqkv, wout, g1.reshape(1, width), b1.reshape(1, width),
        g2.reshape(1, width), segments, segments.reshape(rows, 1), y, yr, targets_col, gmix,
    )


def local(
    tokens, segments, routes, capacity, ln1_gain, ln1_bias, qkv_weight, out_weight, ln2_gain, ln2_bias,
    mix_weight, up_weight, down_weight, expert_up, expert_down, cotangent,
):
    width = tokens.shape[1]
    wl = out_weight.shape[0]
    experts = capacity.shape[0]
    qkv, heads_t, lse, normed2, attn_sum, mix, cot_rows, targets, targets_col = forward(
        tokens, cotangent, segments, routes, capacity, ln1_gain, ln1_bias, ln2_gain, ln2_bias,
        qkv_weight, out_weight, mix_weight,
    )
    mix_float = mix_weight.astype(F32)
    wdiff = (mix_float[:, 0] - mix_float[:, 1]).reshape(1, width)
    rows_in, grad_up, grad_down, y_part, gshare, gmix_dense = dense_block(
        normed2, targets, cotangent, mix, up_weight, down_weight, wdiff, experts
    )
    grad_up, grad_down = lax.psum((grad_up, grad_down), "ep")
    grad_expert_up, grad_expert_down, y_rows, gsec, gmix_rows = expert_block(
        rows_in, cot_rows, expert_up[0], expert_down[0], mix_weight, wdiff, gshare, targets_col
    )
    output, grad_tokens, wsum, small = backward(
        tokens, cotangent, attn_sum, gsec, qkv, heads_t, lse, qkv_weight, out_weight, ln1_gain, ln1_bias,
        ln2_gain, segments, y_part, y_rows, targets_col, gmix_dense + gmix_rows, experts,
    )
    grad_qkv = wsum[: 3 * wl].reshape(3, wl, width).transpose(0, 2, 1).astype(F32)
    return (
        output,
        grad_tokens,
        small[0],
        small[1],
        grad_qkv,
        wsum[3 * wl :].astype(F32),
        small[2],
        small[3],
        jnp.stack([small[4], -small[4]], axis=1),
        grad_up.astype(F32),
        grad_down.astype(F32),
        grad_expert_up[None],
        grad_expert_down[None],
    )


def solution(mesh):
    return jax.shard_map(
        local,
        mesh=mesh,
        in_specs=(
            P("ep", None),
            P("ep", None),
            P("ep"),
            P(),
            P(),
            P(),
            P(None, None, "tp"),
            P("tp", None),
            P(),
            P(),
            P(),
            P(None, "tp"),
            P("tp", None),
            P("ep", None, "tp"),
            P("ep", "tp", None),
            P("ep", None),
        ),
        out_specs=(
            P("ep", None),
            P("ep", None),
            P(),
            P(),
            P(None, None, "tp"),
            P("tp", None),
            P(),
            P(),
            P(),
            P(None, "tp"),
            P("tp", None),
            P("ep", None, "tp"),
            P("ep", "tp", None),
        ),
        check_vma=False,
    )
```

```python
import functools
import math

import jax
import jax.numpy as jnp
from jax import lax
from jax.experimental import pallas as pl
from jax.experimental.pallas import tpu as pltpu
from jax.sharding import PartitionSpec as P

HD = 64
epsilon = 1e-05
masked_value = -1e30
F32 = jnp.float32
BF16 = jnp.bfloat16
VMEM_LIMIT = 60 * 2**20
MESH = pl.DeviceIdType.MESH


def mm(a, b):
    return lax.dot_general(a, b, (((1,), (0,)), ((), ())), preferred_element_type=F32)


def mm_t(a, b):
    return lax.dot_general(a, b, (((1,), (1,)), ((), ())), preferred_element_type=F32)


def t_mm(a, b):
    return lax.dot_general(a, b, (((0,), (0,)), ((), ())), preferred_element_type=F32)


def norm_rows(x):
    centred = x - jnp.mean(x, axis=-1, keepdims=True)
    spread = lax.rsqrt(jnp.mean(centred * centred, axis=-1, keepdims=True) + epsilon)
    return centred * spread, spread


def place():
    t = lax.axis_index("tp")
    return t, lax.div(t, 2), lax.rem(t, 2), lax.axis_index("ep")


def remote(src, dst, send, recv, t, e):
    return pltpu.make_async_remote_copy(
        src_ref=src, dst_ref=dst, send_sem=send, recv_sem=recv, device_id=(t, e), device_id_type=MESH
    )


def greet(partners, loop_partner, loop_count):
    bar = pltpu.get_barrier_semaphore()
    for t, e in partners:
        pl.semaphore_signal(bar, inc=1, device_id=(t, e), device_id_type=MESH)

    def one(i, carry):
        t, e = loop_partner(i)
        pl.semaphore_signal(bar, inc=1, device_id=(t, e), device_id_type=MESH)
        return carry

    if loop_count:
        lax.fori_loop(0, loop_count, one, 0)
    pl.semaphore_wait(bar, len(partners) + loop_count)


def onehot_rows(tgt, first, count):
    rows = lax.broadcasted_iota(jnp.int32, (count, tgt.shape[1]), 0) + first
    return (rows == tgt).astype(F32).astype(BF16)


def forward_kernel(
    n_tp, n_ep, tok, cot, segr, segc, rts, cap, g1, b1, g2, b2, wqkv, wout, mixw,
    qkv_o, ht_o, lse_o, n2_o, attn_o, mix_o, crow_o, tgt_o, tgtc_o,
    vt, snd, part, cbuf, xbuf, bias,
    as_, ar_, fs_, fr_, cs_, cr_, xs_, xr_, gs_, gr_, lsem,
):
    t, x, c, e = place()
    nx = n_tp // 2
    rows_all, width = tok.shape
    half = width // 2
    experts, slots = snd.shape[0], snd.shape[1]
    wl = wout.shape[0]
    heads = wl // HD
    blk = rows_all // 4
    mate = 2 * x + 1 - c
    x_peers = [2 * lax.rem(x + d, nx) + c for d in range(1, nx)]
    greet([(mate, e)] + [(p, e) for p in x_peers], lambda i: (t, lax.rem(e + 1 + i, n_ep)), n_ep - 1)

    hot = lax.broadcasted_iota(jnp.int32, (experts, rows_all), 0) == rts[...]
    hot_f = hot.astype(F32)
    hot_b = hot_f.astype(BF16)
    counts = jnp.zeros((experts, rows_all), F32)
    for k in range(4):
        earlier = (
            lax.broadcasted_iota(jnp.int32, (blk, rows_all), 0) + k * blk
            < lax.broadcasted_iota(jnp.int32, (blk, rows_all), 1)
        )
        counts = counts + mm(hot_b[:, k * blk : (k + 1) * blk], earlier.astype(F32).astype(BF16))
    rank = jnp.sum(counts * hot_f, axis=0, keepdims=True).astype(jnp.int32)
    limit = jnp.sum(jnp.where(hot, cap[...], 0), axis=0, keepdims=True)
    tgt = jnp.where(rank < limit, rts[...] * slots + rank, -1)
    tgt_o[...] = tgt
    tgtc_o[...] = jnp.broadcast_to(tgt.astype(F32), (8, rows_all)).T.astype(jnp.int32)

    my_half = pl.ds(pl.multiple_of(c * half, half), half)

    def rows_for(dest):
        hot_rows = onehot_rows(tgt_o[...], dest * slots, slots)
        return mm(hot_rows, cot[:, my_half]).astype(BF16)

    def a2a_copy(dest, src):
        return remote(snd.at[dest], crow_o.at[c, src], as_.at[dest], ar_.at[src], t, dest)

    def send_rows(i, carry):
        dest = lax.rem(e + 1 + i, n_ep)
        snd[dest] = rows_for(dest)
        a2a_copy(dest, e).start()
        return carry

    lax.fori_loop(0, n_ep - 1, send_rows, 0)
    snd[e] = rows_for(e)
    own = pltpu.make_async_copy(snd.at[e], crow_o.at[c, e], lsem)
    own.start()
    remote(snd.at[e], crow_o.at[c, e], fs_.at[e], fr_.at[e], mate, e).start()

    def project(i):
        rs = pl.ds(i * blk, blk)
        unit, _ = norm_rows(tok[rs, :].astype(F32))
        normed = (unit * g1[...] + b1[...]).astype(BF16)
        for j in range(3):
            qkv_o[j, rs, :] = mm(normed, wqkv[j]).astype(BF16)
        vt[:, rs] = qkv_o[2, rs, :].astype(F32).T.astype(BF16)

    def chunk(i):
        return pl.ds(i * blk, blk)

    other_half = pl.ds(pl.multiple_of((1 - c) * half, half), half)

    def core_copy(i):
        return remote(part.at[chunk(i), other_half], cbuf.at[chunk(i)], cs_.at[i], cr_.at[i], mate, e)

    def x_copy(i, d):
        return remote(
            xbuf.at[x, chunk(i)], xbuf.at[x, chunk(i)], xs_.at[i, d - 1], xr_.at[i, d - 1], x_peers[d - 1], e
        )

    def x_arrival(i, d):
        src = lax.rem(x + nx - d, nx)
        return remote(
            xbuf.at[src, chunk(i)], xbuf.at[src, chunk(i)], xs_.at[i, d - 1], xr_.at[i, d - 1], x_peers[d - 1], e
        )

    def share_copy(i):
        return remote(
            attn_o.at[chunk(i), my_half], attn_o.at[chunk(i), my_half], gs_.at[i], gr_.at[i], mate, e
        )

    def share_arrival(i):
        return remote(
            attn_o.at[chunk(i), other_half], attn_o.at[chunk(i), other_half], gs_.at[i], gr_.at[i], mate, e
        )

    def attend(i):
        keys = (i + 1) * blk
        ks = pl.ds(0, keys)
        allowed = (segc[ks, :] == segr[:, chunk(i)]) & (
            lax.broadcasted_iota(jnp.int32, (keys, blk), 0)
            <= lax.broadcasted_iota(jnp.int32, (keys, blk), 1) + i * blk
        )
        bias[ks, :] = jnp.where(allowed, 0.0, masked_value)
        head_of = lax.div(lax.broadcasted_iota(jnp.int32, (blk, wl), 1), HD)

        def one_head(h, carry):
            q_h = jnp.where(head_of == h, qkv_o[0, chunk(i), :].astype(F32) * 0.125, 0.0).astype(BF16)
            scores = mm_t(qkv_o[1, ks, :], q_h) + bias[ks, :]
            top = jnp.max(scores, axis=0, keepdims=True)
            weights = jnp.exp(scores - top)
            mass = jnp.sum(weights, axis=0, keepdims=True)
            lse_o[pl.ds(h, 1), chunk(i)] = top + jnp.log(mass)
            probs = (weights * (1.0 / mass)).astype(BF16)
            hs = pl.ds(pl.multiple_of(h * HD, HD), HD)
            ht_o[hs, chunk(i)] = mm(vt[hs, ks], probs).astype(BF16)
            return carry

        lax.fori_loop(0, heads, one_head, 0)
        part[chunk(i), :] = t_mm(ht_o[:, chunk(i)], wout[...]).astype(BF16)
        core_copy(i).start()

    def sum_cores(i):
        core_copy(i).wait_recv()
        both = part[chunk(i), my_half].astype(F32) + cbuf[chunk(i), :].astype(F32)
        xbuf[x, chunk(i), :] = both.astype(BF16)
        for d in range(1, nx):
            x_copy(i, d).start()

    def sum_chips(i):
        for d in range(1, nx):
            x_arrival(i, d).wait_recv()
        total = xbuf[0, chunk(i), :].astype(F32)
        for j in range(1, nx):
            total = total + xbuf[j, chunk(i), :].astype(F32)
        attn_o[chunk(i), my_half] = total.astype(BF16)
        share_copy(i).start()

    def finish(i):
        share_arrival(i).wait_recv()
        hidden = tok[chunk(i), :].astype(F32) + attn_o[chunk(i), :].astype(F32)
        unit, _ = norm_rows(hidden)
        normed = (unit * g2[...] + b2[...]).astype(BF16)
        n2_o[chunk(i), :] = normed
        logits = mm(normed, mixw[...])
        lane = lax.broadcasted_iota(jnp.int32, logits.shape, 1)
        logits = jnp.where(lane < 2, logits, masked_value)
        mix = jnp.exp(logits - jnp.max(logits, axis=1, keepdims=True))
        mix_o[chunk(i), :] = mix / jnp.sum(mix, axis=1, keepdims=True)

    for i in range(4):
        project(i)
        if i >= 1:
            sum_cores(i - 1)
        attend(i)
        if i >= 2:
            sum_chips(i - 2)
    sum_cores(3)

    def forward_rows(i, carry):
        src = lax.rem(e + n_ep - 1 - i, n_ep)
        a2a_copy(e, src).wait_recv()
        remote(crow_o.at[c, src], crow_o.at[c, src], fs_.at[src], fr_.at[src], mate, e).start()
        return carry

    def forward_done(src, carry):
        remote(crow_o.at[1 - c, src], crow_o.at[1 - c, src], fs_.at[src], fr_.at[src], mate, e).wait()
        return carry

    finish(0)
    sum_chips(2)
    finish(1)
    sum_chips(3)
    finish(2)
    finish(3)
    lax.fori_loop(0, n_ep - 1, forward_rows, 0)
    lax.fori_loop(0, n_ep, forward_done, 0)
    own.wait()

    def sent(i, carry):
        a2a_copy(lax.rem(e + 1 + i, n_ep), e).wait_send()
        return carry

    lax.fori_loop(0, n_ep - 1, sent, 0)
    for i in range(4):
        core_copy(i).wait_send()
        for d in range(1, nx):
            x_copy(i, d).wait_send()
        share_copy(i).wait_send()


def forward(tokens, cotangent, segments, routes, capacity, g1, b1, g2, b2, wqkv, wout, mix_weight):
    n_tp, n_ep = lax.axis_size("tp"), lax.axis_size("ep")
    rows, width = tokens.shape
    wl = wout.shape[0]
    experts = capacity.shape[0]
    slots = 3 * rows // (2 * experts)
    nx = n_tp // 2
    half = width // 2
    vm = pl.BlockSpec(memory_space=pltpu.VMEM)
    dma = pltpu.SemaphoreType.DMA
    shape = jax.ShapeDtypeStruct
    mixw = jnp.pad(mix_weight, ((0, 0), (0, 126)))
    return pl.pallas_call(
        functools.partial(forward_kernel, n_tp, n_ep),
        out_shape=(
            shape((3, rows, wl), BF16),
            shape((wl, rows), BF16),
            shape((wl // HD, rows), F32),
            shape((rows, width), BF16),
            shape((rows, width), BF16),
            shape((rows, 128), F32),
            shape((2, experts, slots, half), BF16),
            shape((1, rows), jnp.int32),
            shape((rows, 8), jnp.int32),
        ),
        in_specs=[vm] * 13,
        out_specs=(vm,) * 6 + (pl.BlockSpec(memory_space=pl.ANY), vm, vm),
        scratch_shapes=[
            pltpu.VMEM((wl, rows), BF16),
            pltpu.VMEM((experts, slots, half), BF16),
            pltpu.VMEM((rows, width), BF16),
            pltpu.VMEM((rows, half), BF16),
            pltpu.VMEM((nx, rows, half), BF16),
            pltpu.VMEM((rows, rows // 4), F32),
            dma((experts,)), dma((experts,)), dma((experts,)), dma((experts,)),
            dma((4,)), dma((4,)), dma((4, max(nx - 1, 1))), dma((4, max(nx - 1, 1))), dma((4,)), dma((4,)),
            dma,
        ],
        compiler_params=pltpu.CompilerParams(
            collective_id=0, has_side_effects=True, vmem_limit_bytes=VMEM_LIMIT
        ),
        cost_estimate=pl.CostEstimate(flops=8 * 10**9, bytes_accessed=30 * 10**6, transcendentals=0),
        name="attention_forward",
    )(
        tokens, cotangent, segments, segments.reshape(rows, 1), routes.reshape(1, rows),
        capacity.reshape(experts, 1), g1.reshape(1, width), b1.reshape(1, width), g2.reshape(1, width),
        b2.reshape(1, width), wqkv, wout, mixw,
    )


def gelu_pair(v):
    c0 = math.sqrt(2.0 / math.pi)
    sq = v * v
    th = jnp.tanh(c0 * v * (1.0 + 0.044715 * sq))
    half_up = 0.5 + 0.5 * th
    slope = half_up + (0.5 * c0) * v * (1.0 - th * th) * (1.0 + (3.0 * 0.044715) * sq)
    return v * half_up, slope


class TpReduce:
    def __init__(self, nx, bufs, sems, span):
        self.part, self.cbuf, self.xrcv = bufs
        self.cs, self.cr, self.xs, self.xr = sems
        self.nx, self.span = nx, span
        self.t, self.x, self.c, self.e = place()
        self.mate = 2 * self.x + 1 - self.c

    def core(self, i):
        return remote(
            self.part.at[1 - self.c, :, self.span(i)], self.cbuf.at[:, self.span(i)],
            self.cs.at[i], self.cr.at[i], self.mate, self.e,
        )

    def chip(self, i, d):
        there = lax.rem(self.x + d, self.nx)
        return remote(
            self.cbuf.at[there, self.span(i)], self.xrcv.at[self.x, self.span(i)],
            self.xs.at[i, d - 1], self.xr.at[i, d - 1], 2 * there + self.c, self.e,
        )

    def arrival(self, i, d):
        src = lax.rem(self.x + self.nx - d, self.nx)
        return remote(
            self.cbuf.at[src, self.span(i)], self.xrcv.at[src, self.span(i)],
            self.xs.at[i, d - 1], self.xr.at[i, d - 1], 2 * src + self.c, self.e,
        ), src

    def start(self, i):
        self.core(i).start()

    def sum_cores(self, i):
        self.core(i).wait_recv()
        s = self.span(i)
        for j in range(self.nx):
            self.cbuf[j, s, :] = (
                self.part[self.c, j, s, :].astype(F32) + self.cbuf[j, s, :].astype(F32)
            ).astype(BF16)
        for d in range(1, self.nx):
            self.chip(i, d).start()

    def total(self, i):
        s = self.span(i)
        total = self.cbuf[self.x, s, :].astype(F32)
        for d in range(1, self.nx):
            copy, src = self.arrival(i, d)
            copy.wait_recv()
            total = total + self.xrcv[src, s, :].astype(F32)
        return total

    def sent(self, i):
        self.core(i).wait_send()
        for d in range(1, self.nx):
            self.chip(i, d).wait_send()


def dense_kernel(
    n_tp, n_ep, n2, tgt, cot, mix, up, down, wdiff,
    rows_o, gup_o, gdown_o, y_o, gshare_o, gmix_o,
    snd, act, gpre, gden, part, cbuf, xrcv,
    as_, ar_, xs_, xr_, ms_, mr_, lsem, rcs, rcr, rxs, rxr,
):
    t, x, c, e = place()
    nx = n_tp // 2
    rows_all, width = n2.shape
    slots, share = snd.shape[1], snd.shape[2]
    units = up.shape[1]
    blk = rows_all // 4
    mate = 2 * x + 1 - c
    x_peers = [2 * lax.rem(x + d, nx) + c for d in range(1, nx)]
    greet([(mate, e)] + [(p, e) for p in x_peers], lambda i: (t, lax.rem(e + 1 + i, n_ep)), n_ep - 1)
    my_cols = pl.ds(pl.multiple_of(t * share, share), share)

    def rows_for(dest):
        return mm(onehot_rows(tgt[...], dest * slots, slots), n2[:, my_cols]).astype(BF16)

    def a2a_copy(dest, src):
        return remote(snd.at[dest], rows_o.at[t, src], as_.at[dest], ar_.at[src], t, dest)

    def send_rows(i, carry):
        dest = lax.rem(e + 1 + i, n_ep)
        snd[dest] = rows_for(dest)
        a2a_copy(dest, e).start()
        return carry

    def x_copy(here, src, d):
        return remote(here, rows_o.at[t, src], xs_.at[src, d - 1], xr_.at[src, d - 1], x_peers[d - 1], e)

    def mate_copy(here, xi, src):
        return remote(here, rows_o.at[2 * xi + c, src], ms_.at[xi, src], mr_.at[xi, src], mate, e)

    def spread(here, src):
        for d in range(1, nx):
            x_copy(here, src, d).start()
        mate_copy(here, x, src).start()

    lax.fori_loop(0, n_ep - 1, send_rows, 0)
    snd[e] = rows_for(e)
    own = pltpu.make_async_copy(snd.at[e], rows_o.at[t, e], lsem)
    own.start()
    spread(snd.at[e], e)

    def source(k):
        return lax.rem(e + n_ep - k, n_ep)

    def spread_block(k, carry):
        src = source(k)
        a2a_copy(e, src).wait_recv()
        spread(rows_o.at[t, src], src)
        return carry

    def pass_block(k, carry):
        src = source(k)
        for d in range(1, nx):
            xi = lax.rem(x + nx - d, nx)
            got = rows_o.at[2 * xi + c, src]
            remote(got, got, xs_.at[src, d - 1], xr_.at[src, d - 1], mate, e).wait_recv()
            mate_copy(got, xi, src).start()
        return carry

    def end_block(src, carry):
        for xi in range(nx):
            got = rows_o.at[2 * xi + 1 - c, src]
            remote(got, got, ms_.at[xi, src], mr_.at[xi, src], mate, e).wait()
        for d in range(1, nx):
            x_copy(rows_o.at[t, src], src, d).wait_send()
        return carry

    def chunk(i):
        return pl.ds(i * blk, blk)

    reduce = TpReduce(nx, (part, cbuf, xrcv), (rcs, rcr, rxs, rxr), chunk)
    fblk = min(256, units)
    steps = units // fblk

    def dense(i, tally):
        rs = chunk(i)
        mix0, mix1 = mix[rs, 0:1], mix[rs, 1:2]
        gden[rs, :] = (mix0 * cot[rs, :].astype(F32)).astype(BF16)

        def one(f, carry):
            fs = pl.ds(pl.multiple_of(f * fblk, fblk), fblk)
            value, slope = gelu_pair(mm(n2[rs, :], up[:, fs]))
            act[rs, fs] = value.astype(BF16)
            gpre[rs, fs] = (mm_t(gden[rs, :], down[fs, :]) * slope).astype(BF16)
            return carry

        lax.fori_loop(0, steps, one, 0)
        col0 = jnp.zeros((blk, 1), F32)
        for g in range(n_tp):
            gs = pl.ds(g * share, share)
            dense_part = mm(act[rs, :], down[:, gs])
            col0 = col0 + jnp.sum(dense_part * cot[rs, gs].astype(F32), axis=1, keepdims=True)
            y_o[g % 2, g // 2, rs, :] = (mix0 * dense_part).astype(BF16)
        logit = mix0 * mix1 * col0
        for g in range(n_tp):
            gs = pl.ds(g * share, share)
            back = mm_t(gpre[rs, :], up[gs, :]) + logit * wdiff[:, gs]
            part[g % 2, g // 2, rs, :] = back.astype(BF16)
        reduce.start(i)
        return tally + jnp.sum(logit * n2[rs, :].astype(F32), axis=0, keepdims=True)

    ends = [1 + (n_ep - 1) * k // 4 for k in range(5)]
    tally = dense(0, jnp.zeros((1, width), F32))
    lax.fori_loop(ends[0], ends[1], spread_block, 0)
    tally = dense(1, tally)
    reduce.sum_cores(0)
    pass_block(0, 0)
    lax.fori_loop(ends[1], ends[2], spread_block, 0)
    lax.fori_loop(ends[0], ends[1], pass_block, 0)
    tally = dense(2, tally)
    reduce.sum_cores(1)
    lax.fori_loop(ends[2], ends[3], spread_block, 0)
    lax.fori_loop(ends[1], ends[2], pass_block, 0)
    tally = dense(3, tally)
    reduce.sum_cores(2)
    lax.fori_loop(ends[3], ends[4], spread_block, 0)
    lax.fori_loop(ends[2], ends[3], pass_block, 0)
    reduce.sum_cores(3)
    gmix_o[...] = jnp.broadcast_to(tally, gmix_o.shape)
    for k in range(steps):
        fs = pl.ds(k * fblk, fblk)
        gdown_o[fs, :] = t_mm(act[:, fs], gden[...]).astype(BF16)
    for k in range(4):
        ws = pl.ds(k * (width // 4), width // 4)
        gup_o[ws, :] = t_mm(n2[:, ws], gpre[...]).astype(BF16)
    lax.fori_loop(ends[3], ends[4], pass_block, 0)
    for i in range(4):
        gshare_o[chunk(i), :] = reduce.total(i)
    lax.fori_loop(0, n_ep, end_block, 0)
    own.wait()

    def sent(i, carry):
        a2a_copy(lax.rem(e + 1 + i, n_ep), e).wait_send()
        return carry

    lax.fori_loop(0, n_ep - 1, sent, 0)
    for i in range(4):
        reduce.sent(i)


def dense_block(n2, targets, cotangent, mix, up, down, wdiff, experts):
    n_tp, n_ep = lax.axis_size("tp"), lax.axis_size("ep")
    rows, width = n2.shape
    slots = 3 * rows // (2 * experts)
    units = up.shape[1]
    nx, share = n_tp // 2, width // n_tp
    dx = max(nx - 1, 1)
    vm = pl.BlockSpec(memory_space=pltpu.VMEM)
    dma = pltpu.SemaphoreType.DMA
    shape = jax.ShapeDtypeStruct
    return pl.pallas_call(
        functools.partial(dense_kernel, n_tp, n_ep),
        out_shape=(
            shape((n_tp, experts, slots, share), BF16),
            shape((width, units), BF16),
            shape((units, width), BF16),
            shape((2, nx, rows, share), BF16),
            shape((rows, share), F32),
            shape((8, width), F32),
        ),
        in_specs=[vm] * 7,
        out_specs=(pl.BlockSpec(memory_space=pl.ANY),) + (vm,) * 5,
        scratch_shapes=[
            pltpu.VMEM((experts, slots, share), BF16),
            pltpu.VMEM((rows, units), BF16),
            pltpu.VMEM((rows, units), BF16),
            pltpu.VMEM((rows, width), BF16),
            pltpu.VMEM((2, nx, rows, share), BF16),
            pltpu.VMEM((nx, rows, share), BF16),
            pltpu.VMEM((nx, rows, share), BF16),
            dma((experts,)), dma((experts,)), dma((experts, dx)), dma((experts, dx)),
            dma((nx, experts)), dma((nx, experts)), dma,
            dma((4,)), dma((4,)), dma((4, dx)), dma((4, dx)),
        ],
        compiler_params=pltpu.CompilerParams(
            collective_id=1, has_side_effects=True, vmem_limit_bytes=VMEM_LIMIT
        ),
        cost_estimate=pl.CostEstimate(flops=16 * 10**9, bytes_accessed=30 * 10**6, transcendentals=0),
        name="dense_and_dispatch",
    )(n2, targets, cotangent, mix, up, down, wdiff)


class EpBits:
    def __init__(self, first, rows, order, sems, base):
        self.first, self.rows, self.order, self.base = first, rows, order, base
        self.ss, self.rs = sems
        self.t, self.x, self.c, self.e = place()
        self.low = [0]
        for s, b in enumerate(order):
            self.low.append(self.low[-1] + self.bit(b) * (rows >> (s + 1)))

    def bit(self, b):
        return lax.rem(lax.div(self.e, 2**b), 2)

    def cut(self, low, size):
        return pl.ds(pl.multiple_of(self.first + low, 16), size)

    def size(self, s):
        return self.rows >> (s + 1)

    def landing(self, s):
        return self.first + self.rows - (self.rows >> s)

    def move(self, src, dst, s):
        b = self.order[s]
        partner = self.e + (1 - 2 * self.bit(b)) * 2**b
        return remote(src, dst, self.ss.at[self.base, s], self.rs.at[self.base, s], self.t, partner)


class EpSum(EpBits):
    def __init__(self, data, land, first, rows, order, sems, base):
        super().__init__(first, rows, order, sems, base)
        self.data, self.land = data, land

    def half(self, s, keep):
        size, bit = self.size(s), self.bit(self.order[s])
        which = bit if keep else 1 - bit
        if s == 0:
            return self.data.at[self.cut(which * size, size)]
        return self.land.at[pl.ds(pl.multiple_of(self.landing(s - 1) + which * size, 16), size)]

    def out(self, s):
        return self.move(self.half(s, False), self.land.at[pl.ds(self.landing(s), self.size(s))], s)

    def start(self, s):
        self.out(s).start()

    def add(self, s):
        self.out(s).wait_recv()
        spot = pl.ds(self.landing(s), self.size(s))
        self.land[spot, :] = (self.land[spot, :].astype(F32) + self.half(s, True)[...].astype(F32)).astype(BF16)

    def result(self):
        last = len(self.order) - 1
        return self.land[pl.ds(self.landing(last), self.size(last)), :]

    def sent(self):
        for s in range(len(self.order)):
            self.out(s).wait_send()


class EpGather(EpBits):
    def __init__(self, full, first, rows, order, sems, base):
        super().__init__(first, rows, order, sems, base)
        self.full = full

    def part(self, s, other):
        size, bit = self.size(s), self.bit(self.order[s])
        return self.full.at[self.cut(self.low[s] + ((1 - bit) if other else bit) * size, size)]

    def own(self):
        return self.part(len(self.order) - 1, False)

    def give(self, s, src=None):
        part = self.part(s, False)
        self.move(part if src is None else src, part, s).start()

    def take(self, s):
        part = self.part(s, True)
        self.move(part, part, s).wait_recv()

    def sent(self):
        for s in range(len(self.order)):
            part = self.part(s, False)
            self.move(part, part, s).wait_send()


def ep_cuts(rows, n_ep):
    return max(q for q in (4, 2, 1) if q == 1 or rows % (16 * q * n_ep) == 0)


class Slots:
    def __init__(self):
        self.lists, self.at = {}, 0

    def put(self, slot, action):
        self.lists.setdefault(slot, []).append(action)

    def run(self, slot):
        for action in self.lists.get(slot, []):
            action()

    def next(self, count=1):
        for _ in range(count):
            self.run(self.at)
            self.at += 1

    def rest(self):
        for slot in sorted(self.lists):
            if slot >= self.at:
                self.run(slot)
        self.at = 1 + max(self.lists, default=-1)


def plan_sum(slots, piece, first, bits, lag=2, stride=1):
    def step(s):
        piece.add(s)
        if s + 1 < bits:
            piece.start(s + 1)

    slots.put(first, lambda: piece.start(0))
    for s in range(bits):
        slots.put(first + lag + stride * s, lambda s=s: step(s))


def plan_gather(slots, piece, own, sem, first, bits):
    piece.give(bits - 1, own)
    pltpu.make_async_copy(own, piece.own(), sem).start()

    def step(s):
        if s == bits - 1:
            pltpu.make_async_copy(own, piece.own(), sem).wait()
        piece.take(s)
        if s > 0:
            piece.give(s - 1)

    for s in range(bits - 1, -1, -1):
        slots.put(first + 2 * (bits - 1 - s) if s else 99, lambda s=s: step(s))


def expert_kernel(
    n_tp, n_ep, rows, crow, eup, edown, mixw, wdiff, gshare, tgtc, gup,
    geup_o, gedown_o, gsec_o, gmix_o, oshare_o, sup_o,
    act, gpre, grow, part, cbuf, xrcv, rsnd, ret, ypart, ybuf, yxrcv, ysnd, yret, uland,
    rcs, rcr, rxs, rxr, as_, ar_, lsem,
    ycs, ycr, yxs, yxr, ys_, yr_, ylsem, uss, urs,
):
    t, x, c, e = place()
    nx = n_tp // 2
    experts, slots, share = rows.shape[1:]
    total_rows = experts * slots
    half = crow.shape[3]
    width = 2 * half
    units = eup.shape[1]
    nb = experts // 4
    size = nb * slots
    tok_rows = tgtc.shape[0]
    blk = tok_rows // 4
    mate = 2 * x + 1 - c
    x_peers = [2 * lax.rem(x + d, nx) + c for d in range(1, nx)]
    greet([(mate, e)] + [(p, e) for p in x_peers], lambda i: (t, lax.rem(e + 1 + i, n_ep)), n_ep - 1)

    def piece(i):
        return lax.rem(lax.div(e, nb) + 1 + i, 4)

    def span(i):
        return pl.ds(pl.multiple_of(piece(i) * size, size), size)

    def chunk(i):
        return pl.ds(i * blk, blk)

    reduce = TpReduce(nx, (part, cbuf, xrcv), (rcs, rcr, rxs, rxr), span)
    reduce_y = TpReduce(nx, (ypart, ybuf, yxrcv), (ycs, ycr, yxs, yxr), span)
    back = EpReturn(rsnd, ret, slots, (as_, ar_, lsem))
    back_y = EpReturn(ysnd, yret, slots, (ys_, yr_, ylsem))
    bits = n_ep.bit_length() - 1
    order = list(range(bits))
    up_cuts = sup_o.shape[0]
    up_rows = gup.shape[0] // up_cuts
    sums = [EpSum(gup, uland, k * up_rows, up_rows, order, (uss, urs), k) for k in range(up_cuts)]
    slots_ = Slots()
    for k, one_sum in enumerate(sums):
        plan_sum(slots_, one_sum, k if k > 1 else 0, bits)
    fblk = min(256, units)
    steps = units // fblk
    gmix_o[...] = jnp.zeros_like(gmix_o)
    slots_.next(2)

    def work(i):
        bs = pl.ds(piece(i) * nb, nb)
        rs = span(i)

        def share_rows(g):
            return rows[g, bs].reshape(size, share)

        logits = jnp.zeros((size, 128), F32)
        for g in range(n_tp):
            logits = logits + mm(share_rows(g), mixw[pl.ds(g * share, share), :])
        lane = lax.broadcasted_iota(jnp.int32, logits.shape, 1)
        logits = jnp.where(lane < 2, logits, masked_value)
        mix = jnp.exp(logits - jnp.max(logits, axis=1, keepdims=True))
        mix = mix / jnp.sum(mix, axis=1, keepdims=True)
        mix0, mix1 = mix[:, 0:1], mix[:, 1:2]
        for h in range(2):
            grow[rs, pl.ds(h * half, half)] = (mix1 * crow[h, bs].reshape(size, half).astype(F32)).astype(BF16)

        def one(f, carry):
            fs = pl.ds(pl.multiple_of(f * fblk, fblk), fblk)
            pre = mm(share_rows(0), eup[pl.ds(0, share), fs])
            for g in range(1, n_tp):
                pre = pre + mm(share_rows(g), eup[pl.ds(g * share, share), fs])
            value, slope = gelu_pair(pre)
            act[rs, fs] = value.astype(BF16)
            gpre[rs, fs] = (mm_t(grow[rs, :], edown[fs, :]) * slope).astype(BF16)
            return carry

        lax.fori_loop(0, steps, one, 0)
        col1 = jnp.zeros((size, 1), F32)
        per_half = n_tp // 2
        for g in range(n_tp):
            gs = pl.ds(g * share, share)
            eout = mm(act[rs, :], edown[:, gs])
            cots = crow[g // per_half, bs, :, pl.ds((g % per_half) * share, share)].reshape(size, share)
            col1 = col1 + jnp.sum(eout * cots.astype(F32), axis=1, keepdims=True)
            ypart[g % 2, g // 2, rs, :] = (mix1 * eout).astype(BF16)
        logit = -(mix0 * mix1 * col1)
        for g in range(n_tp):
            gs = pl.ds(g * share, share)
            grad_in = mm_t(gpre[rs, :], eup[gs, :]) + logit * wdiff[:, gs]
            part[g % 2, g // 2, rs, :] = grad_in.astype(BF16)
            tally = jnp.sum(logit * share_rows(g).astype(F32), axis=0, keepdims=True)
            gmix_o[:, gs] = gmix_o[:, gs] + jnp.broadcast_to(tally, (8, share))
        reduce.start(i)
        reduce_y.start(i)

    def send_back(i):
        rsnd[span(i), :] = reduce.total(i).astype(BF16)
        back.send(piece(i) * nb, nb)

    def send_back_y(i):
        ysnd[span(i), :] = reduce_y.total(i).astype(BF16)
        back_y.send(piece(i) * nb, nb)

    def step(i, carry):
        work(i)

        @pl.when(i >= 1)
        def _():
            reduce.sum_cores(i - 1)

        @pl.when(i >= 2)
        def _():
            reduce_y.sum_cores(i - 2)
            send_back(i - 2)

        for j in range(4):

            @pl.when(i == j)
            def _():
                slots_.run(2 + j)

        return carry

    lax.fori_loop(0, 4, step, 0)
    slots_.at = 6
    reduce.sum_cores(3)
    reduce_y.sum_cores(2)
    slots_.next()

    def down_grad(k):
        fs = pl.ds(k * fblk, fblk)
        gedown_o[fs, :] = t_mm(act[:, fs], grow[...])

    def up_grad(g):
        geup_o[pl.ds(g * share, share), :] = t_mm(rows[g].reshape(total_rows, share), gpre[...])

    send_back_y(0)
    for k in range(steps // 2):
        down_grad(k)
    send_back(2)
    slots_.next()
    for k in range(steps // 2, steps):
        down_grad(k)
    send_back(3)
    reduce_y.sum_cores(3)
    send_back_y(1)
    slots_.next()
    up_grad(0)
    send_back_y(2)
    for g in range(1, n_tp // 2):
        up_grad(g)
    slots_.next()

    def hot_rows(i):
        ids = lax.broadcasted_iota(jnp.int32, (blk, total_rows), 1)
        return (ids == tgtc[chunk(i), 0:1]).astype(F32).astype(BF16)

    back.arrived(n_ep)
    for i in range(4):
        gsec_o[chunk(i), :] = (gshare[chunk(i), :] + mm(hot_rows(i), ret[...])).astype(BF16)
    send_back_y(3)
    slots_.next()
    for g in range(n_tp // 2, n_tp):
        up_grad(g)
    slots_.rest()
    for k in range(up_cuts):
        sup_o[k] = sums[k].result()
    back_y.arrived(n_ep)
    for i in range(4):
        oshare_o[chunk(i), :] = mm(hot_rows(i), yret[...])
    back.sent(n_ep)
    back_y.sent(n_ep)
    for i in range(4):
        reduce.sent(i)
        reduce_y.sent(i)
    for one_sum in sums:
        one_sum.sent()


class EpReturn:
    def __init__(self, snd, ret, slots, sems):
        self.snd, self.ret, self.slots = snd, ret, slots
        self.ss, self.rs, self.local = sems
        self.t, self.x, self.c, self.e = place()

    def block(self, k):
        return pl.ds(pl.multiple_of(k * self.slots, self.slots), self.slots)

    def copy(self, dest, src):
        return remote(
            self.snd.at[self.block(dest)], self.ret.at[self.block(src)], self.ss.at[dest], self.rs.at[src], self.t, dest
        )

    def own(self):
        mine = self.block(self.e)
        return pltpu.make_async_copy(self.snd.at[mine], self.ret.at[mine], self.local)

    def send(self, first, count):
        def one(k, carry):
            dest = first + k

            @pl.when(dest != self.e)
            def _():
                self.copy(dest, self.e).start()

            @pl.when(dest == self.e)
            def _():
                self.own().start()

            return carry

        lax.fori_loop(0, count, one, 0)

    def arrived(self, n_ep):
        def one(k, carry):
            self.copy(self.e, lax.rem(self.e + n_ep - k, n_ep)).wait_recv()
            return carry

        lax.fori_loop(1, n_ep, one, 0)
        self.own().wait()

    def sent(self, n_ep):
        def one(k, carry):
            self.copy(lax.rem(self.e + k, n_ep), self.e).wait_send()
            return carry

        lax.fori_loop(1, n_ep, one, 0)


class TpGather:
    def __init__(self, nx, full, share, blk, sems):
        self.full, self.share, self.blk, self.nx = full, share, blk, nx
        self.xs, self.xr, self.ms, self.mr = sems
        self.t, self.x, self.c, self.e = place()
        self.mate = 2 * self.x + 1 - self.c

    def cut(self, i, g):
        return self.full.at[
            pl.ds(i * self.blk, self.blk), pl.ds(pl.multiple_of(g * self.share, self.share), self.share)
        ]

    def across(self, i, d):
        there = 2 * lax.rem(self.x + d, self.nx) + self.c
        mine = self.cut(i, self.t)
        return remote(mine, mine, self.xs.at[i, d - 1], self.xr.at[i, d - 1], there, self.e)

    def beside(self, i, xi, c):
        got = self.cut(i, 2 * xi + c)
        return remote(got, got, self.ms.at[i, xi], self.mr.at[i, xi], self.mate, self.e)

    def put(self, i, value):
        cols = pl.ds(pl.multiple_of(self.t * self.share, self.share), self.share)
        self.full[pl.ds(i * self.blk, self.blk), cols] = value
        for d in range(1, self.nx):
            self.across(i, d).start()
        self.beside(i, self.x, self.c).start()

    def pass_on(self, i):
        for d in range(1, self.nx):
            xi = lax.rem(self.x + self.nx - d, self.nx)
            got = self.cut(i, 2 * xi + self.c)
            remote(got, got, self.xs.at[i, d - 1], self.xr.at[i, d - 1], self.mate, self.e).wait_recv()
            self.beside(i, xi, self.c).start()

    def finish(self, i):
        for xi in range(self.nx):
            self.beside(i, xi, 1 - self.c).wait_recv()
            self.beside(i, xi, self.c).wait_send()
        for d in range(1, self.nx):
            self.across(i, d).wait_send()


def expert_block(rows, cot_rows, eup, edown, mix_weight, wdiff, gshare, targets_col, gup):
    n_tp, n_ep = lax.axis_size("tp"), lax.axis_size("ep")
    _, experts, slots, share = rows.shape
    tok_rows = targets_col.shape[0]
    width, units = eup.shape
    nx = n_tp // 2
    dx = max(nx - 1, 1)
    total = experts * slots
    bits = n_ep.bit_length() - 1
    up_cuts = ep_cuts(width, n_ep)
    vm = pl.BlockSpec(memory_space=pltpu.VMEM)
    dma = pltpu.SemaphoreType.DMA
    shape = jax.ShapeDtypeStruct
    mixw = jnp.pad(mix_weight, ((0, 0), (0, 126)))
    return pl.pallas_call(
        functools.partial(expert_kernel, n_tp, n_ep),
        out_shape=(
            shape((width, units), F32),
            shape((units, width), F32),
            shape((tok_rows, share), BF16),
            shape((8, width), F32),
            shape((tok_rows, share), F32),
            shape((up_cuts, width // up_cuts // n_ep, units), BF16),
        ),
        in_specs=[vm] * 9,
        out_specs=(vm,) * 6,
        scratch_shapes=[
            pltpu.VMEM((total, units), BF16),
            pltpu.VMEM((total, units), BF16),
            pltpu.VMEM((total, width), BF16),
            pltpu.VMEM((2, nx, total, share), BF16),
            pltpu.VMEM((nx, total, share), BF16),
            pltpu.VMEM((nx, total, share), BF16),
            pltpu.VMEM((total, share), BF16),
            pltpu.VMEM((total, share), BF16),
            pltpu.VMEM((2, nx, total, share), BF16),
            pltpu.VMEM((nx, total, share), BF16),
            pltpu.VMEM((nx, total, share), BF16),
            pltpu.VMEM((total, share), BF16),
            pltpu.VMEM((total, share), BF16),
            pltpu.VMEM((width, units), BF16),
            dma((4,)), dma((4,)), dma((4, dx)), dma((4, dx)),
            dma((experts,)), dma((experts,)), dma,
            dma((4,)), dma((4,)), dma((4, dx)), dma((4, dx)),
            dma((experts,)), dma((experts,)), dma,
            dma((up_cuts, bits)), dma((up_cuts, bits)),
        ],
        compiler_params=pltpu.CompilerParams(
            collective_id=2, has_side_effects=True, vmem_limit_bytes=VMEM_LIMIT + 3 * 2**20
        ),
        cost_estimate=pl.CostEstimate(flops=24 * 10**9, bytes_accessed=50 * 10**6, transcendentals=0),
        name="experts",
    )(rows, cot_rows, eup, edown, mixw, wdiff, gshare, targets_col, gup)


class TpSum:
    def __init__(self, nx, full, bufs, sems, blk):
        self.full, self.blk, self.nx = full, blk, nx
        self.part, self.cbuf, self.xbuf = bufs
        self.cs, self.cr, self.xs, self.xr, self.gs, self.gr = sems
        self.t, self.x, self.c, self.e = place()
        self.mate = 2 * self.x + 1 - self.c
        half = self.cbuf.shape[1]
        self.mine = pl.ds(pl.multiple_of(self.c * half, half), half)
        self.other = pl.ds(pl.multiple_of((1 - self.c) * half, half), half)

    def span(self, i):
        return pl.ds(i * self.blk, self.blk)

    def core(self, i):
        return remote(
            self.part.at[self.span(i), self.other], self.cbuf.at[self.span(i)], self.cs.at[i], self.cr.at[i],
            self.mate, self.e,
        )

    def chip(self, i, d):
        there = 2 * lax.rem(self.x + d, self.nx) + self.c
        mine = self.xbuf.at[self.x, self.span(i)]
        return remote(mine, mine, self.xs.at[i, d - 1], self.xr.at[i, d - 1], there, self.e)

    def start(self, i):
        self.core(i).start()

    def sum_cores(self, i):
        self.core(i).wait_recv()
        both = self.part[self.span(i), self.mine].astype(F32) + self.cbuf[self.span(i), :].astype(F32)
        self.xbuf[self.x, self.span(i), :] = both.astype(BF16)
        for d in range(1, self.nx):
            self.chip(i, d).start()

    def share(self, i, cols):
        got = self.full.at[self.span(i), cols]
        return remote(got, got, self.gs.at[i], self.gr.at[i], self.mate, self.e)

    def sum_chips(self, i):
        for d in range(1, self.nx):
            src = lax.rem(self.x + self.nx - d, self.nx)
            got = self.xbuf.at[src, self.span(i)]
            remote(got, got, self.xs.at[i, d - 1], self.xr.at[i, d - 1], self.mate, self.e).wait_recv()
        total = self.xbuf[0, self.span(i), :].astype(F32)
        for j in range(1, self.nx):
            total = total + self.xbuf[j, self.span(i), :].astype(F32)
        self.full[self.span(i), self.mine] = total.astype(BF16)
        self.share(i, self.mine).start()

    def wait(self, i):
        self.share(i, self.other).wait_recv()
        self.share(i, self.mine).wait_send()

    def sent(self, i):
        self.core(i).wait_send()
        for d in range(1, self.nx):
            self.chip(i, d).wait_send()


def backward_kernel(
    n_tp, n_ep, tok, cot, attn, gshare, qkv, ht, lse, wqkv, wout, g1, b1, g2, segr, segc, oshare, sup, y, gdown,
    out_o, gh, part, wdat, small, gup_o, sdown_o,
    ga, gheads, kt, dqt, pcat, dcat, gcat, qcat, dk, dv, gj, bias,
    gsec, dbuf, dxrcv, dland,
    oxs, oxr, oms, omr, hxs, hxr, hms, hmr, uss, urs, usem, dcs, dcr, dxs, dxr, dss, drs,
):
    t, x, c, e = place()
    nx = n_tp // 2
    rows_all, width = tok.shape
    wl = wout.shape[0]
    heads = wl // HD
    blk = rows_all // 4
    share = oshare.shape[1]
    bits = n_ep.bit_length() - 1
    greet(
        [(2 * x + 1 - c, e)] + [(2 * lax.rem(x + d, nx) + c, e) for d in range(1, nx)],
        lambda i: (t, lax.rem(e + 1 + i, n_ep)),
        n_ep - 1,
    )

    def chunk(i):
        return pl.ds(i * blk, blk)

    gather = TpGather(nx, out_o, share, blk, (oxs, oxr, oms, omr))
    gather_g = TpGather(nx, gsec, share, blk, (hxs, hxr, hms, hmr))
    for i in (3, 2, 1, 0):
        gather_g.put(i, gshare[chunk(i), :])
    group = pcat.shape[1] // blk
    gw = group * HD
    up_cuts = sup.shape[0]
    up_rows = gup_o.shape[0] // up_cuts
    order = list(range(bits))
    wide = [EpGather(gup_o, k * up_rows, up_rows, order, (uss, urs), k) for k in range(up_cuts)]
    slots_ = Slots()
    for k, one in enumerate(wide):
        plan_gather(slots_, one, sup.at[k], usem.at[k], k + 1, bits)
    reduce_d = TpReduce(nx, (y, dbuf, dxrcv), (dcs, dcr, dxs, dxr), chunk)
    for i in range(4):
        reduce_d.start(i)
    down_cuts = sdown_o.shape[0]
    down_rows = gdown.shape[0] // down_cuts
    downs = [EpSum(gdown, dland, k * down_rows, down_rows, order, (dss, drs), k) for k in range(down_cuts)]
    for k, one in enumerate(downs):
        plan_sum(slots_, one, 0, bits, 1 + 2 * k + k // 3, 2)
    slots_.next()
    my_cols = pl.ds(pl.multiple_of(t * share, share), share)

    def put_output(i):
        rs = chunk(i)
        hidden = tok[rs, my_cols].astype(F32) + attn[rs, my_cols].astype(F32)
        gather.put(i, (hidden + oshare[rs, :] + reduce_d.total(i)).astype(BF16))

    sum_gain = jnp.zeros((1, width), F32)
    sum_bias = jnp.zeros((1, width), F32)
    gather_g.pass_on(3)
    for i in (3, 2, 1, 0):
        rs = chunk(i)
        if i > 0:
            gather_g.pass_on(i - 1)
        gather_g.finish(i)
        unit, spread = norm_rows(tok[rs, :].astype(F32) + attn[rs, :].astype(F32))
        up = gsec[rs, :].astype(F32)
        sum_gain = sum_gain + jnp.sum(up * unit, axis=0, keepdims=True)
        sum_bias = sum_bias + jnp.sum(up, axis=0, keepdims=True)
        gv = up * g2[...]
        inner = gv - jnp.mean(gv, axis=-1, keepdims=True) - unit * jnp.mean(gv * unit, axis=-1, keepdims=True)
        grad = cot[rs, :].astype(F32) + spread * inner
        gh[rs, :] = grad
        ga[rs, :] = grad.astype(BF16)
        gheads[rs, :] = mm_t(ga[rs, :], wout[...]).astype(BF16)
        reduce_d.sum_cores(i)
        slots_.next()
    small[...] = jnp.zeros_like(small)
    small[2:3, :] = sum_gain
    small[3:4, :] = sum_bias
    wdat[pl.ds(0, wl), :] = mm(ht[...], ga[...]).astype(BF16)
    for i in range(4):
        rs = chunk(i)
        unit, _ = norm_rows(tok[rs, :].astype(F32))
        ga[rs, :] = (unit * g1[...] + b1[...]).astype(BF16)
        kt[:, rs] = qkv[1, rs, :].astype(F32).T.astype(BF16)

    head_of = lax.div(lax.broadcasted_iota(jnp.int32, (blk, gw), 1), HD)

    def attend(i, first, last):
        keys = (i + 1) * blk
        ks = pl.ds(0, keys)
        hc = pl.ds(first * HD, gw)
        allowed = (segc[ks, :] == segr[:, chunk(i)]) & (
            lax.broadcasted_iota(jnp.int32, (keys, blk), 0)
            <= lax.broadcasted_iota(jnp.int32, (keys, blk), 1) + i * blk
        )
        bias[ks, :] = jnp.where(allowed, 0.0, masked_value)

        def one_head(k, carry):
            h = first + k
            q_h = jnp.where(head_of == k, qkv[0, chunk(i), hc].astype(F32) * 0.125, 0.0).astype(BF16)
            g_h = jnp.where(head_of == k, gheads[chunk(i), hc].astype(F32), 0.0).astype(BF16)
            hb = pl.ds(pl.multiple_of(k * blk, blk), blk)
            gcat[hb, :] = g_h
            qcat[hb, :] = q_h
            probs = jnp.exp(mm_t(qkv[1, ks, hc], q_h) + bias[ks, :] - lse[pl.ds(h, 1), chunk(i)])
            pcat[ks, hb] = probs.astype(BF16)
            grad = mm_t(qkv[2, ks, hc], g_h)
            mean = jnp.sum(probs * grad, axis=0, keepdims=True)
            scores = (probs * (grad - mean)).astype(BF16)
            dcat[ks, hb] = scores
            dqt[pl.ds(pl.multiple_of(k * HD, HD), HD), :] = mm(
                kt[pl.ds(pl.multiple_of(h * HD, HD), HD), ks], scores
            )
            return carry

        lax.fori_loop(0, group, one_head, 0)
        dv_new, dk_new = mm(pcat[ks, :], gcat[...]), mm(dcat[ks, :], qcat[...])
        if i == 3:
            dv[ks, :] = dv_new
            dk[ks, :] = dk_new
        else:
            dv[ks, :] = dv[ks, :] + dv_new
            dk[ks, :] = dk[ks, :] + dk_new
        gj[0, chunk(i), hc] = (dqt[...].T * 0.125).astype(BF16)
        gj[1, chunk(i), hc] = dk[chunk(i), :].astype(BF16)
        gj[2, chunk(i), hc] = dv[chunk(i), :].astype(BF16)
        if last:
            grad_in = mm_t(gj[0, chunk(i), :], wqkv[0])
            for j in range(1, 3):
                grad_in = grad_in + mm_t(gj[j, chunk(i), :], wqkv[j])
            part[chunk(i), :] = grad_in.astype(BF16)

    def weight_grads(first):
        for j in range(3):
            row = wl + j * wl + first * HD
            wdat[pl.ds(row, gw), :] = t_mm(gj[j, :, pl.ds(first * HD, gw)], ga[...]).astype(BF16)

    groups = list(range(0, heads, group))
    for first in groups:
        last = first == groups[-1]
        for i in (3, 2, 1, 0):
            attend(i, first, last)
            slots_.next()
            if first == 0 and i == 3:
                for k in (3, 2, 1, 0):
                    put_output(k)
            if last and i == 1:
                for k in (3, 2, 1, 0):
                    gather.pass_on(k)
        weight_grads(first)
    slots_.rest()
    for i in range(4):
        gather.finish(i)
    for k in range(down_cuts):
        sdown_o[k] = downs[k].result()
    for one in wide + downs:
        one.sent()
    for i in range(4):
        reduce_d.sent(i)


def finish_kernel(
    n_tp, n_ep, tok, gh, part, g1, first_sums, gmix, wpart, sdown,
    gtok_o, small_o, wsum_o, gdown_o,
    cbuf, xbuf, small, sland, mland, wland,
    wss, wrs, wgs, wgr, dss, drs, dsem, tcs, tcr, txs, txr, tgs, tgr, ss_, sr_, mgs, mgr,
):
    t, x, c, e = place()
    nx = n_tp // 2
    rows_all, width = tok.shape
    blk = rows_all // 4
    greet(
        [(lax.rem(t + d, n_tp), e) for d in range(1, n_tp)], lambda i: (t, lax.rem(e + 1 + i, n_ep)), n_ep - 1
    )

    def chunk(i):
        return pl.ds(i * blk, blk)

    tp_sum = TpSum(nx, gtok_o, (part, cbuf, xbuf), (tcs, tcr, txs, txr, tgs, tgr), blk)
    for i in range(4):
        tp_sum.start(i)

    def mix_copy(d):
        return remote(gmix, mland.at[t], mgs.at[d - 1], mgr.at[d - 1], lax.rem(t + d, n_tp), e)

    mland[t] = gmix[...]
    for d in range(1, n_tp):
        mix_copy(d).start()
    small[...] = first_sums[...]
    bits = n_ep.bit_length() - 1
    cuts = wss.shape[0]
    cut_rows = wpart.shape[0] // cuts
    order = list(range(bits))
    sums = [EpSum(wpart, wland, k * cut_rows, cut_rows, order, (wss, wrs), k) for k in range(cuts)]
    gathers = [EpGather(wsum_o, k * cut_rows, cut_rows, order, (wgs, wgr), k) for k in range(cuts)]
    down_cuts = sdown.shape[0]
    down_rows = gdown_o.shape[0] // down_cuts
    wide = [EpGather(gdown_o, k * down_rows, down_rows, order, (dss, drs), k) for k in range(down_cuts)]
    slots_ = Slots()
    for one_sum in sums:
        one_sum.start(0)
    for k, one in enumerate(wide):
        plan_gather(slots_, one, sdown.at[k], dsem.at[k], k + 1, bits)
    for i in range(4):
        tp_sum.sum_cores(i)

    tally = [jnp.zeros((1, width), F32), jnp.zeros((1, width), F32)]

    def finish(i):
        rs = chunk(i)
        tp_sum.wait(i)
        unit, spread = norm_rows(tok[rs, :].astype(F32))
        up = gtok_o[rs, :].astype(F32)
        tally[0] = tally[0] + jnp.sum(up * unit, axis=0, keepdims=True)
        tally[1] = tally[1] + jnp.sum(up, axis=0, keepdims=True)
        gv = up * g1[...]
        inner = gv - jnp.mean(gv, axis=-1, keepdims=True) - unit * jnp.mean(gv * unit, axis=-1, keepdims=True)
        gtok_o[rs, :] = (gh[rs, :] + spread * inner).astype(BF16)

    def step(k, stage):
        if stage < bits:
            sums[k].add(stage)
            if stage + 1 < bits:
                sums[k].start(stage + 1)
            else:
                gathers[k].own()[...] = sums[k].result()
                gathers[k].give(stage)
        else:
            s = 2 * bits - 1 - stage
            gathers[k].take(s)
            if s > 0:
                gathers[k].give(s - 1)

    beats = [[] for _ in range(cuts + 4 * bits)]
    for k in range(cuts):
        for stage in range(2 * bits - 1):
            beats[k + 1 + 2 * stage].append((stage, k))
    beats = [sorted(b, reverse=True) for b in beats if b]
    apart = max(len(beats) // 8, 1)
    for n, beat in enumerate(beats):
        for stage, k in beat:
            step(k, stage)
        slots_.next()
        at = n // apart
        if n % apart == 0 and at < 4:
            tp_sum.sum_chips(at)
        if n % apart == 0 and 1 <= at < 5:
            finish(at - 1)
    for i in range(len(beats[::apart]), 5):
        if i < 4:
            tp_sum.sum_chips(i)
        finish(i - 1)
    small[0:1, :] = tally[0]
    small[1:2, :] = tally[1]
    mix_total = jnp.zeros((1, width), F32)
    for d in range(1, n_tp):
        got = mland.at[lax.rem(t + n_tp - d, n_tp)]
        remote(got, got, mgs.at[d - 1], mgr.at[d - 1], lax.rem(t + d, n_tp), e).wait_recv()
    for j in range(n_tp):
        mix_total = mix_total + mland[j, 0:1, :]
    small[4:5, :] = mix_total
    sland[e] = small[...]

    def small_copy(dest, src):
        return remote(small, sland.at[src], ss_.at[dest], sr_.at[src], t, dest)

    def send_small(k, carry):
        small_copy(lax.rem(e + k, n_ep), e).start()
        return carry

    lax.fori_loop(1, n_ep, send_small, 0)

    slots_.rest()
    for k in range(cuts):
        step(k, 2 * bits - 1)

    def small_arrived(k, carry):
        small_copy(e, lax.rem(e + n_ep - k, n_ep)).wait_recv()
        return carry

    lax.fori_loop(1, n_ep, small_arrived, 0)
    small_o[...] = lax.fori_loop(0, n_ep, lambda k, total: total + sland[k], jnp.zeros_like(small_o))

    def sent(k, carry):
        dest = lax.rem(e + k, n_ep)
        small_copy(dest, e).wait_send()
        return carry

    lax.fori_loop(1, n_ep, sent, 0)
    for d in range(1, n_tp):
        mix_copy(d).wait_send()
    for i in range(4):
        tp_sum.sent(i)
    for one in sums + gathers + wide:
        one.sent()


def backward(tokens, cotangent, attn, gshare, qkv, ht, lse, wqkv, wout, g1, b1, g2, segments, oshare, sup, y, gdown):
    n_tp, n_ep = lax.axis_size("tp"), lax.axis_size("ep")
    rows, width = tokens.shape
    wl = wout.shape[0]
    nx = n_tp // 2
    dx = max(nx - 1, 1)
    blk = rows // 4
    group = min(2, wl // HD)
    bits = n_ep.bit_length() - 1
    up_cuts, up_rows, units = sup.shape
    share = oshare.shape[1]
    down_cuts = ep_cuts(units, n_ep)
    vm = pl.BlockSpec(memory_space=pltpu.VMEM)
    dma = pltpu.SemaphoreType.DMA
    shape = jax.ShapeDtypeStruct
    return pl.pallas_call(
        functools.partial(backward_kernel, n_tp, n_ep),
        out_shape=(
            shape((rows, width), BF16),
            shape((rows, width), F32),
            shape((rows, width), BF16),
            shape((4 * wl, width), BF16),
            shape((8, width), F32),
            shape((up_cuts * up_rows * n_ep, units), BF16),
            shape((down_cuts, units // down_cuts // n_ep, width), BF16),
        ),
        in_specs=[vm] * 18,
        out_specs=(vm,) * 5 + (pl.BlockSpec(memory_space=pl.ANY), vm),
        scratch_shapes=[
            pltpu.VMEM((rows, width), BF16),
            pltpu.VMEM((rows, wl), BF16),
            pltpu.VMEM((wl, rows), BF16),
            pltpu.VMEM((group * HD, blk), F32),
            pltpu.VMEM((rows, group * blk), BF16),
            pltpu.VMEM((rows, group * blk), BF16),
            pltpu.VMEM((group * blk, group * HD), BF16),
            pltpu.VMEM((group * blk, group * HD), BF16),
            pltpu.VMEM((rows, group * HD), F32),
            pltpu.VMEM((rows, group * HD), F32),
            pltpu.VMEM((3, rows, wl), BF16),
            pltpu.VMEM((rows, blk), F32),
            pltpu.VMEM((rows, width), BF16),
            pltpu.VMEM((nx, rows, share), BF16),
            pltpu.VMEM((nx, rows, share), BF16),
            pltpu.VMEM((units, width), BF16),
            dma((4, dx)), dma((4, dx)), dma((4, nx)), dma((4, nx)),
            dma((4, dx)), dma((4, dx)), dma((4, nx)), dma((4, nx)),
            dma((up_cuts, bits)), dma((up_cuts, bits)), dma((up_cuts,)),
            dma((4,)), dma((4,)), dma((4, dx)), dma((4, dx)), dma((down_cuts, bits)), dma((down_cuts, bits)),
        ],
        compiler_params=pltpu.CompilerParams(
            collective_id=3, has_side_effects=True, vmem_limit_bytes=VMEM_LIMIT
        ),
        cost_estimate=pl.CostEstimate(flops=60 * 10**9, bytes_accessed=50 * 10**6, transcendentals=0),
        name="attention_backward",
    )(
        tokens, cotangent, attn, gshare, qkv, ht, lse, wqkv, wout, g1.reshape(1, width), b1.reshape(1, width),
        g2.reshape(1, width), segments, segments.reshape(rows, 1), oshare, sup, y, gdown,
    )


def finish_block(tokens, gh, part, g1, first_sums, gmix, wpart, sdown):
    n_tp, n_ep = lax.axis_size("tp"), lax.axis_size("ep")
    rows, width = tokens.shape
    nx = n_tp // 2
    dx = max(nx - 1, 1)
    half = width // 2
    bits = n_ep.bit_length() - 1
    down_cuts, down_rows, _ = sdown.shape
    cuts = max(q for q in (8, 4, 2, 1) if q == 1 or wpart.shape[0] % (16 * q * n_ep) == 0)
    vm = pl.BlockSpec(memory_space=pltpu.VMEM)
    dma = pltpu.SemaphoreType.DMA
    return pl.pallas_call(
        functools.partial(finish_kernel, n_tp, n_ep),
        out_shape=(
            jax.ShapeDtypeStruct((rows, width), BF16),
            jax.ShapeDtypeStruct((8, width), F32),
            jax.ShapeDtypeStruct(wpart.shape, BF16),
            jax.ShapeDtypeStruct((down_cuts * down_rows * n_ep, width), BF16),
        ),
        in_specs=[vm] * 8,
        out_specs=(vm,) * 3 + (pl.BlockSpec(memory_space=pl.ANY),),
        scratch_shapes=[
            pltpu.VMEM((rows, half), BF16),
            pltpu.VMEM((nx, rows, half), BF16),
            pltpu.VMEM((8, width), F32),
            pltpu.VMEM((n_ep, 8, width), F32),
            pltpu.VMEM((n_tp, 8, width), F32),
            pltpu.VMEM(wpart.shape, BF16),
            dma((cuts, bits)), dma((cuts, bits)), dma((cuts, bits)), dma((cuts, bits)),
            dma((down_cuts, bits)), dma((down_cuts, bits)), dma((down_cuts,)),
            dma((4,)), dma((4,)), dma((4, dx)), dma((4, dx)), dma((4,)), dma((4,)),
            dma((n_ep,)), dma((n_ep,)), dma((n_tp,)), dma((n_tp,)),
        ],
        compiler_params=pltpu.CompilerParams(
            collective_id=4, has_side_effects=True, vmem_limit_bytes=VMEM_LIMIT
        ),
        cost_estimate=pl.CostEstimate(flops=40 * 10**9, bytes_accessed=50 * 10**6, transcendentals=0),
        name="finish_norm",
    )(tokens, gh, part, g1.reshape(1, width), first_sums, gmix, wpart, sdown)


def local(
    tokens, segments, routes, capacity, ln1_gain, ln1_bias, qkv_weight, out_weight, ln2_gain, ln2_bias,
    mix_weight, up_weight, down_weight, expert_up, expert_down, cotangent,
):
    width = tokens.shape[1]
    wl = out_weight.shape[0]
    experts = capacity.shape[0]
    qkv, heads_t, lse, normed2, attn_sum, mix, cot_rows, targets, targets_col = forward(
        tokens, cotangent, segments, routes, capacity, ln1_gain, ln1_bias, ln2_gain, ln2_bias,
        qkv_weight, out_weight, mix_weight,
    )
    mix_float = mix_weight.astype(F32)
    wdiff = (mix_float[:, 0] - mix_float[:, 1]).reshape(1, width)
    rows_in, grad_up, grad_down, y_part, gshare, gmix_dense = dense_block(
        normed2, targets, cotangent, mix, up_weight, down_weight, wdiff, experts
    )
    grad_expert_up, grad_expert_down, gsec, gmix_rows, out_share, part_up = expert_block(
        rows_in, cot_rows, expert_up[0], expert_down[0], mix_weight, wdiff, gshare, targets_col, grad_up
    )
    output, grad_hidden, part, wpart, first_sums, grad_up, part_down = backward(
        tokens, cotangent, attn_sum, gsec, qkv, heads_t, lse, qkv_weight, out_weight, ln1_gain, ln1_bias,
        ln2_gain, segments, out_share, part_up, y_part, grad_down,
    )
    grad_tokens, small, wsum, grad_down = finish_block(
        tokens, grad_hidden, part, ln1_gain, first_sums, gmix_dense + gmix_rows, wpart, part_down
    )
    grad_qkv = wsum[wl:].reshape(3, wl, width).transpose(0, 2, 1).astype(F32)
    return (
        output,
        grad_tokens,
        small[0],
        small[1],
        grad_qkv,
        wsum[:wl].astype(F32),
        small[2],
        small[3],
        jnp.stack([small[4], -small[4]], axis=1),
        grad_up.astype(F32),
        grad_down.astype(F32),
        grad_expert_up[None],
        grad_expert_down[None],
    )


def solution(mesh):
    return jax.shard_map(
        local,
        mesh=mesh,
        in_specs=(
            P("ep", None),
            P("ep", None),
            P("ep"),
            P(),
            P(),
            P(),
            P(None, None, "tp"),
            P("tp", None),
            P(),
            P(),
            P(),
            P(None, "tp"),
            P("tp", None),
            P("ep", None, "tp"),
            P("ep", "tp", None),
            P("ep", None),
        ),
        out_specs=(
            P("ep", None),
            P("ep", None),
            P(),
            P(),
            P(None, None, "tp"),
            P("tp", None),
            P(),
            P(),
            P(),
            P(None, "tp"),
            P("tp", None),
            P("ep", None, "tp"),
            P("ep", "tp", None),
        ),
        check_vma=False,
    )
```

```python
import functools
import math

import jax
import jax.numpy as jnp
from jax import lax
from jax.experimental import pallas as pl
from jax.experimental.pallas import tpu as pltpu
from jax.sharding import PartitionSpec as P

HD = 64
epsilon = 1e-05
masked_value = -1e30
F32 = jnp.float32
BF16 = jnp.bfloat16
VMEM_LIMIT = 60 * 2**20
MESH = pl.DeviceIdType.MESH


def mm(a, b):
    return lax.dot_general(a, b, (((1,), (0,)), ((), ())), preferred_element_type=F32)


def mm_t(a, b):
    return lax.dot_general(a, b, (((1,), (1,)), ((), ())), preferred_element_type=F32)


def t_mm(a, b):
    return lax.dot_general(a, b, (((0,), (0,)), ((), ())), preferred_element_type=F32)


def norm_rows(x):
    centred = x - jnp.mean(x, axis=-1, keepdims=True)
    spread = lax.rsqrt(jnp.mean(centred * centred, axis=-1, keepdims=True) + epsilon)
    return centred * spread, spread


def place():
    t = lax.axis_index("tp")
    return t, lax.div(t, 2), lax.rem(t, 2), lax.axis_index("ep")


def remote(src, dst, send, recv, t, e):
    return pltpu.make_async_remote_copy(
        src_ref=src, dst_ref=dst, send_sem=send, recv_sem=recv, device_id=(t, e), device_id_type=MESH
    )


def greet(partners, loop_partner, loop_count):
    bar = pltpu.get_barrier_semaphore()
    for t, e in partners:
        pl.semaphore_signal(bar, inc=1, device_id=(t, e), device_id_type=MESH)

    def one(i, carry):
        t, e = loop_partner(i)
        pl.semaphore_signal(bar, inc=1, device_id=(t, e), device_id_type=MESH)
        return carry

    if loop_count:
        lax.fori_loop(0, loop_count, one, 0)
    pl.semaphore_wait(bar, len(partners) + loop_count)


def onehot_rows(tgt, first, count):
    rows = lax.broadcasted_iota(jnp.int32, (count, tgt.shape[1]), 0) + first
    return (rows == tgt).astype(F32).astype(BF16)


def forward_kernel(
    n_tp, n_ep, tok, cot, segr, segc, rts, cap, g1, b1, g2, b2, wqkv, wout, mixw,
    qkv_o, ht_o, lse_o, n2_o, attn_o, mix_o, crow_o, tgt_o, tgtc_o,
    vt, snd, part, cbuf, xbuf, bias,
    as_, ar_, fs_, fr_, cs_, cr_, xs_, xr_, gs_, gr_, lsem,
):
    t, x, c, e = place()
    nx = n_tp // 2
    rows_all, width = tok.shape
    half = width // 2
    experts, slots = snd.shape[0], snd.shape[1]
    wl = wout.shape[0]
    heads = wl // HD
    blk = rows_all // 4
    mate = 2 * x + 1 - c
    x_peers = [2 * lax.rem(x + d, nx) + c for d in range(1, nx)]
    greet([(mate, e)] + [(p, e) for p in x_peers], lambda i: (t, lax.rem(e + 1 + i, n_ep)), n_ep - 1)

    hot = lax.broadcasted_iota(jnp.int32, (experts, rows_all), 0) == rts[...]
    hot_f = hot.astype(F32)
    hot_b = hot_f.astype(BF16)
    counts = jnp.zeros((experts, rows_all), F32)
    for k in range(4):
        earlier = (
            lax.broadcasted_iota(jnp.int32, (blk, rows_all), 0) + k * blk
            < lax.broadcasted_iota(jnp.int32, (blk, rows_all), 1)
        )
        counts = counts + mm(hot_b[:, k * blk : (k + 1) * blk], earlier.astype(F32).astype(BF16))
    rank = jnp.sum(counts * hot_f, axis=0, keepdims=True).astype(jnp.int32)
    limit = jnp.sum(jnp.where(hot, cap[...], 0), axis=0, keepdims=True)
    tgt = jnp.where(rank < limit, rts[...] * slots + rank, -1)
    tgt_o[...] = tgt
    tgtc_o[...] = jnp.broadcast_to(tgt.astype(F32), (8, rows_all)).T.astype(jnp.int32)

    my_half = pl.ds(pl.multiple_of(c * half, half), half)

    def rows_for(dest):
        hot_rows = onehot_rows(tgt_o[...], dest * slots, slots)
        return mm(hot_rows, cot[:, my_half]).astype(BF16)

    def a2a_copy(dest, src):
        return remote(snd.at[dest], crow_o.at[c, src], as_.at[dest], ar_.at[src], t, dest)

    def send_rows(i, carry):
        dest = lax.rem(e + 1 + i, n_ep)
        snd[dest] = rows_for(dest)
        a2a_copy(dest, e).start()
        return carry

    lax.fori_loop(0, n_ep - 1, send_rows, 0)
    snd[e] = rows_for(e)
    own = pltpu.make_async_copy(snd.at[e], crow_o.at[c, e], lsem)
    own.start()
    remote(snd.at[e], crow_o.at[c, e], fs_.at[e], fr_.at[e], mate, e).start()

    def project(i):
        rs = pl.ds(i * blk, blk)
        unit, _ = norm_rows(tok[rs, :].astype(F32))
        normed = (unit * g1[...] + b1[...]).astype(BF16)
        for j in range(3):
            qkv_o[j, rs, :] = mm(normed, wqkv[j]).astype(BF16)
        vt[:, rs] = qkv_o[2, rs, :].astype(F32).T.astype(BF16)

    def chunk(i):
        return pl.ds(i * blk, blk)

    other_half = pl.ds(pl.multiple_of((1 - c) * half, half), half)

    def core_copy(i):
        return remote(part.at[chunk(i), other_half], cbuf.at[chunk(i)], cs_.at[i], cr_.at[i], mate, e)

    def x_copy(i, d):
        return remote(
            xbuf.at[x, chunk(i)], xbuf.at[x, chunk(i)], xs_.at[i, d - 1], xr_.at[i, d - 1], x_peers[d - 1], e
        )

    def x_arrival(i, d):
        src = lax.rem(x + nx - d, nx)
        return remote(
            xbuf.at[src, chunk(i)], xbuf.at[src, chunk(i)], xs_.at[i, d - 1], xr_.at[i, d - 1], x_peers[d - 1], e
        )

    def share_copy(i):
        return remote(
            attn_o.at[chunk(i), my_half], attn_o.at[chunk(i), my_half], gs_.at[i], gr_.at[i], mate, e
        )

    def share_arrival(i):
        return remote(
            attn_o.at[chunk(i), other_half], attn_o.at[chunk(i), other_half], gs_.at[i], gr_.at[i], mate, e
        )

    def attend(i):
        keys = (i + 1) * blk
        ks = pl.ds(0, keys)
        allowed = (segc[ks, :] == segr[:, chunk(i)]) & (
            lax.broadcasted_iota(jnp.int32, (keys, blk), 0)
            <= lax.broadcasted_iota(jnp.int32, (keys, blk), 1) + i * blk
        )
        bias[ks, :] = jnp.where(allowed, 0.0, masked_value)
        head_of = lax.div(lax.broadcasted_iota(jnp.int32, (blk, wl), 1), HD)

        def one_head(h, carry):
            q_h = jnp.where(head_of == h, qkv_o[0, chunk(i), :].astype(F32) * 0.125, 0.0).astype(BF16)
            scores = mm_t(qkv_o[1, ks, :], q_h) + bias[ks, :]
            top = jnp.max(scores, axis=0, keepdims=True)
            weights = jnp.exp(scores - top)
            mass = jnp.sum(weights, axis=0, keepdims=True)
            lse_o[pl.ds(h, 1), chunk(i)] = top + jnp.log(mass)
            probs = (weights * (1.0 / mass)).astype(BF16)
            hs = pl.ds(pl.multiple_of(h * HD, HD), HD)
            ht_o[hs, chunk(i)] = mm(vt[hs, ks], probs).astype(BF16)
            return carry

        lax.fori_loop(0, heads, one_head, 0)
        part[chunk(i), :] = t_mm(ht_o[:, chunk(i)], wout[...]).astype(BF16)
        core_copy(i).start()

    def sum_cores(i):
        core_copy(i).wait_recv()
        both = part[chunk(i), my_half].astype(F32) + cbuf[chunk(i), :].astype(F32)
        xbuf[x, chunk(i), :] = both.astype(BF16)
        for d in range(1, nx):
            x_copy(i, d).start()

    def sum_chips(i):
        for d in range(1, nx):
            x_arrival(i, d).wait_recv()
        total = xbuf[0, chunk(i), :].astype(F32)
        for j in range(1, nx):
            total = total + xbuf[j, chunk(i), :].astype(F32)
        attn_o[chunk(i), my_half] = total.astype(BF16)
        share_copy(i).start()

    def finish(i):
        share_arrival(i).wait_recv()
        hidden = tok[chunk(i), :].astype(F32) + attn_o[chunk(i), :].astype(F32)
        unit, _ = norm_rows(hidden)
        normed = (unit * g2[...] + b2[...]).astype(BF16)
        n2_o[chunk(i), :] = normed
        logits = mm(normed, mixw[...])
        lane = lax.broadcasted_iota(jnp.int32, logits.shape, 1)
        logits = jnp.where(lane < 2, logits, masked_value)
        mix = jnp.exp(logits - jnp.max(logits, axis=1, keepdims=True))
        mix_o[chunk(i), :] = mix / jnp.sum(mix, axis=1, keepdims=True)

    for i in range(4):
        project(i)
        if i >= 1:
            sum_cores(i - 1)
        attend(i)
        if i >= 2:
            sum_chips(i - 2)
    sum_cores(3)

    def forward_rows(i, carry):
        src = lax.rem(e + n_ep - 1 - i, n_ep)
        a2a_copy(e, src).wait_recv()
        remote(crow_o.at[c, src], crow_o.at[c, src], fs_.at[src], fr_.at[src], mate, e).start()
        return carry

    def forward_done(src, carry):
        remote(crow_o.at[1 - c, src], crow_o.at[1 - c, src], fs_.at[src], fr_.at[src], mate, e).wait()
        return carry

    finish(0)
    sum_chips(2)
    finish(1)
    sum_chips(3)
    finish(2)
    finish(3)
    lax.fori_loop(0, n_ep - 1, forward_rows, 0)
    lax.fori_loop(0, n_ep, forward_done, 0)
    own.wait()

    def sent(i, carry):
        a2a_copy(lax.rem(e + 1 + i, n_ep), e).wait_send()
        return carry

    lax.fori_loop(0, n_ep - 1, sent, 0)
    for i in range(4):
        core_copy(i).wait_send()
        for d in range(1, nx):
            x_copy(i, d).wait_send()
        share_copy(i).wait_send()


def forward(tokens, cotangent, segments, routes, capacity, g1, b1, g2, b2, wqkv, wout, mix_weight):
    n_tp, n_ep = lax.axis_size("tp"), lax.axis_size("ep")
    rows, width = tokens.shape
    wl = wout.shape[0]
    experts = capacity.shape[0]
    slots = 3 * rows // (2 * experts)
    nx = n_tp // 2
    half = width // 2
    vm = pl.BlockSpec(memory_space=pltpu.VMEM)
    dma = pltpu.SemaphoreType.DMA
    shape = jax.ShapeDtypeStruct
    mixw = jnp.pad(mix_weight, ((0, 0), (0, 126)))
    return pl.pallas_call(
        functools.partial(forward_kernel, n_tp, n_ep),
        out_shape=(
            shape((3, rows, wl), BF16),
            shape((wl, rows), BF16),
            shape((wl // HD, rows), F32),
            shape((rows, width), BF16),
            shape((rows, width), BF16),
            shape((rows, 128), F32),
            shape((2, experts, slots, half), BF16),
            shape((1, rows), jnp.int32),
            shape((rows, 8), jnp.int32),
        ),
        in_specs=[vm] * 13,
        out_specs=(vm,) * 6 + (pl.BlockSpec(memory_space=pl.ANY), vm, vm),
        scratch_shapes=[
            pltpu.VMEM((wl, rows), BF16),
            pltpu.VMEM((experts, slots, half), BF16),
            pltpu.VMEM((rows, width), BF16),
            pltpu.VMEM((rows, half), BF16),
            pltpu.VMEM((nx, rows, half), BF16),
            pltpu.VMEM((rows, rows // 4), F32),
            dma((experts,)), dma((experts,)), dma((experts,)), dma((experts,)),
            dma((4,)), dma((4,)), dma((4, max(nx - 1, 1))), dma((4, max(nx - 1, 1))), dma((4,)), dma((4,)),
            dma,
        ],
        compiler_params=pltpu.CompilerParams(
            collective_id=0, has_side_effects=True, vmem_limit_bytes=VMEM_LIMIT
        ),
        cost_estimate=pl.CostEstimate(flops=8 * 10**9, bytes_accessed=30 * 10**6, transcendentals=0),
        name="attention_forward",
    )(
        tokens, cotangent, segments, segments.reshape(rows, 1), routes.reshape(1, rows),
        capacity.reshape(experts, 1), g1.reshape(1, width), b1.reshape(1, width), g2.reshape(1, width),
        b2.reshape(1, width), wqkv, wout, mixw,
    )


def gelu_pair(v):
    c0 = math.sqrt(2.0 / math.pi)
    sq = v * v
    th = jnp.tanh(c0 * v * (1.0 + 0.044715 * sq))
    half_up = 0.5 + 0.5 * th
    slope = half_up + (0.5 * c0) * v * (1.0 - th * th) * (1.0 + (3.0 * 0.044715) * sq)
    return v * half_up, slope


class TpReduce:
    def __init__(self, nx, bufs, sems, span):
        self.part, self.cbuf, self.xrcv = bufs
        self.cs, self.cr, self.xs, self.xr = sems
        self.nx, self.span = nx, span
        self.t, self.x, self.c, self.e = place()
        self.mate = 2 * self.x + 1 - self.c

    def core(self, i):
        return remote(
            self.part.at[1 - self.c, :, self.span(i)], self.cbuf.at[:, self.span(i)],
            self.cs.at[i], self.cr.at[i], self.mate, self.e,
        )

    def chip(self, i, d):
        there = lax.rem(self.x + d, self.nx)
        return remote(
            self.cbuf.at[there, self.span(i)], self.xrcv.at[self.x, self.span(i)],
            self.xs.at[i, d - 1], self.xr.at[i, d - 1], 2 * there + self.c, self.e,
        )

    def arrival(self, i, d):
        src = lax.rem(self.x + self.nx - d, self.nx)
        return remote(
            self.cbuf.at[src, self.span(i)], self.xrcv.at[src, self.span(i)],
            self.xs.at[i, d - 1], self.xr.at[i, d - 1], 2 * src + self.c, self.e,
        ), src

    def start(self, i):
        self.core(i).start()

    def sum_cores(self, i):
        self.core(i).wait_recv()
        s = self.span(i)
        for j in range(self.nx):
            self.cbuf[j, s, :] = (
                self.part[self.c, j, s, :].astype(F32) + self.cbuf[j, s, :].astype(F32)
            ).astype(BF16)
        for d in range(1, self.nx):
            self.chip(i, d).start()

    def total(self, i):
        s = self.span(i)
        total = self.cbuf[self.x, s, :].astype(F32)
        for d in range(1, self.nx):
            copy, src = self.arrival(i, d)
            copy.wait_recv()
            total = total + self.xrcv[src, s, :].astype(F32)
        return total

    def sent(self, i):
        self.core(i).wait_send()
        for d in range(1, self.nx):
            self.chip(i, d).wait_send()


def dense_kernel(
    n_tp, n_ep, n2, tgt, cot, mix, up, down, wdiff,
    rows_o, gup_o, gdown_o, y_o, gshare_o, gmix_o,
    snd, act, gpre, gden, part, cbuf, xrcv,
    as_, ar_, xs_, xr_, ms_, mr_, lsem, rcs, rcr, rxs, rxr,
):
    t, x, c, e = place()
    nx = n_tp // 2
    rows_all, width = n2.shape
    slots, share = snd.shape[1], snd.shape[2]
    units = up.shape[1]
    blk = rows_all // 4
    mate = 2 * x + 1 - c
    x_peers = [2 * lax.rem(x + d, nx) + c for d in range(1, nx)]
    greet([(mate, e)] + [(p, e) for p in x_peers], lambda i: (t, lax.rem(e + 1 + i, n_ep)), n_ep - 1)
    my_cols = pl.ds(pl.multiple_of(t * share, share), share)

    def rows_for(dest):
        return mm(onehot_rows(tgt[...], dest * slots, slots), n2[:, my_cols]).astype(BF16)

    def a2a_copy(dest, src):
        return remote(snd.at[dest], rows_o.at[t, src], as_.at[dest], ar_.at[src], t, dest)

    def send_rows(i, carry):
        dest = lax.rem(e + 1 + i, n_ep)
        snd[dest] = rows_for(dest)
        a2a_copy(dest, e).start()
        return carry

    def x_copy(here, src, d):
        return remote(here, rows_o.at[t, src], xs_.at[src, d - 1], xr_.at[src, d - 1], x_peers[d - 1], e)

    def mate_copy(here, xi, src):
        return remote(here, rows_o.at[2 * xi + c, src], ms_.at[xi, src], mr_.at[xi, src], mate, e)

    def spread(here, src):
        for d in range(1, nx):
            x_copy(here, src, d).start()
        mate_copy(here, x, src).start()

    lax.fori_loop(0, n_ep - 1, send_rows, 0)
    snd[e] = rows_for(e)
    own = pltpu.make_async_copy(snd.at[e], rows_o.at[t, e], lsem)
    own.start()
    spread(snd.at[e], e)

    def source(k):
        return lax.rem(e + n_ep - k, n_ep)

    def spread_block(k, carry):
        src = source(k)
        a2a_copy(e, src).wait_recv()
        spread(rows_o.at[t, src], src)
        return carry

    def pass_block(k, carry):
        src = source(k)
        for d in range(1, nx):
            xi = lax.rem(x + nx - d, nx)
            got = rows_o.at[2 * xi + c, src]
            remote(got, got, xs_.at[src, d - 1], xr_.at[src, d - 1], mate, e).wait_recv()
            mate_copy(got, xi, src).start()
        return carry

    def end_block(src, carry):
        for xi in range(nx):
            got = rows_o.at[2 * xi + 1 - c, src]
            remote(got, got, ms_.at[xi, src], mr_.at[xi, src], mate, e).wait()
        for d in range(1, nx):
            x_copy(rows_o.at[t, src], src, d).wait_send()
        return carry

    def chunk(i):
        return pl.ds(i * blk, blk)

    reduce = TpReduce(nx, (part, cbuf, xrcv), (rcs, rcr, rxs, rxr), chunk)
    fblk = min(256, units)
    steps = units // fblk

    def dense(i, tally):
        rs = chunk(i)
        mix0, mix1 = mix[rs, 0:1], mix[rs, 1:2]
        gden[rs, :] = (mix0 * cot[rs, :].astype(F32)).astype(BF16)

        def one(f, carry):
            fs = pl.ds(pl.multiple_of(f * fblk, fblk), fblk)
            value, slope = gelu_pair(mm(n2[rs, :], up[:, fs]))
            act[rs, fs] = value.astype(BF16)
            gpre[rs, fs] = (mm_t(gden[rs, :], down[fs, :]) * slope).astype(BF16)
            return carry

        lax.fori_loop(0, steps, one, 0)
        col0 = jnp.zeros((blk, 1), F32)
        for g in range(n_tp):
            gs = pl.ds(g * share, share)
            dense_part = mm(act[rs, :], down[:, gs])
            col0 = col0 + jnp.sum(dense_part * cot[rs, gs].astype(F32), axis=1, keepdims=True)
            y_o[g % 2, g // 2, rs, :] = (mix0 * dense_part).astype(BF16)
        logit = mix0 * mix1 * col0
        for g in range(n_tp):
            gs = pl.ds(g * share, share)
            back = mm_t(gpre[rs, :], up[gs, :]) + logit * wdiff[:, gs]
            part[g % 2, g // 2, rs, :] = back.astype(BF16)
        reduce.start(i)
        return tally + jnp.sum(logit * n2[rs, :].astype(F32), axis=0, keepdims=True)

    ends = [1 + (n_ep - 1) * k // 4 for k in range(5)]
    tally = dense(0, jnp.zeros((1, width), F32))
    lax.fori_loop(ends[0], ends[1], spread_block, 0)
    tally = dense(1, tally)
    reduce.sum_cores(0)
    pass_block(0, 0)
    lax.fori_loop(ends[1], ends[2], spread_block, 0)
    lax.fori_loop(ends[0], ends[1], pass_block, 0)
    tally = dense(2, tally)
    reduce.sum_cores(1)
    lax.fori_loop(ends[2], ends[3], spread_block, 0)
    lax.fori_loop(ends[1], ends[2], pass_block, 0)
    tally = dense(3, tally)
    reduce.sum_cores(2)
    lax.fori_loop(ends[3], ends[4], spread_block, 0)
    lax.fori_loop(ends[2], ends[3], pass_block, 0)
    reduce.sum_cores(3)
    gmix_o[...] = jnp.broadcast_to(tally, gmix_o.shape)
    for k in range(steps):
        fs = pl.ds(k * fblk, fblk)
        gdown_o[fs, :] = t_mm(act[:, fs], gden[...]).astype(BF16)
    for k in range(4):
        ws = pl.ds(k * (width // 4), width // 4)
        gup_o[ws, :] = t_mm(n2[:, ws], gpre[...]).astype(BF16)
    lax.fori_loop(ends[3], ends[4], pass_block, 0)
    for i in range(4):
        gshare_o[chunk(i), :] = reduce.total(i)
    lax.fori_loop(0, n_ep, end_block, 0)
    own.wait()

    def sent(i, carry):
        a2a_copy(lax.rem(e + 1 + i, n_ep), e).wait_send()
        return carry

    lax.fori_loop(0, n_ep - 1, sent, 0)
    for i in range(4):
        reduce.sent(i)


def dense_block(n2, targets, cotangent, mix, up, down, wdiff, experts):
    n_tp, n_ep = lax.axis_size("tp"), lax.axis_size("ep")
    rows, width = n2.shape
    slots = 3 * rows // (2 * experts)
    units = up.shape[1]
    nx, share = n_tp // 2, width // n_tp
    dx = max(nx - 1, 1)
    vm = pl.BlockSpec(memory_space=pltpu.VMEM)
    dma = pltpu.SemaphoreType.DMA
    shape = jax.ShapeDtypeStruct
    return pl.pallas_call(
        functools.partial(dense_kernel, n_tp, n_ep),
        out_shape=(
            shape((n_tp, experts, slots, share), BF16),
            shape((width, units), BF16),
            shape((units, width), BF16),
            shape((2, nx, rows, share), BF16),
            shape((rows, share), F32),
            shape((8, width), F32),
        ),
        in_specs=[vm] * 7,
        out_specs=(pl.BlockSpec(memory_space=pl.ANY),) + (vm,) * 5,
        scratch_shapes=[
            pltpu.VMEM((experts, slots, share), BF16),
            pltpu.VMEM((rows, units), BF16),
            pltpu.VMEM((rows, units), BF16),
            pltpu.VMEM((rows, width), BF16),
            pltpu.VMEM((2, nx, rows, share), BF16),
            pltpu.VMEM((nx, rows, share), BF16),
            pltpu.VMEM((nx, rows, share), BF16),
            dma((experts,)), dma((experts,)), dma((experts, dx)), dma((experts, dx)),
            dma((nx, experts)), dma((nx, experts)), dma,
            dma((4,)), dma((4,)), dma((4, dx)), dma((4, dx)),
        ],
        compiler_params=pltpu.CompilerParams(
            collective_id=1, has_side_effects=True, vmem_limit_bytes=VMEM_LIMIT
        ),
        cost_estimate=pl.CostEstimate(flops=16 * 10**9, bytes_accessed=30 * 10**6, transcendentals=0),
        name="dense_and_dispatch",
    )(n2, targets, cotangent, mix, up, down, wdiff)


class EpBits:
    def __init__(self, first, rows, order, sems, base):
        self.first, self.rows, self.order, self.base = first, rows, order, base
        self.ss, self.rs = sems
        self.t, self.x, self.c, self.e = place()
        self.low = [0]
        for s, b in enumerate(order):
            self.low.append(self.low[-1] + self.bit(b) * (rows >> (s + 1)))

    def bit(self, b):
        return lax.rem(lax.div(self.e, 2**b), 2)

    def cut(self, low, size):
        return pl.ds(pl.multiple_of(self.first + low, 16), size)

    def size(self, s):
        return self.rows >> (s + 1)

    def landing(self, s):
        return self.first + self.rows - (self.rows >> s)

    def move(self, src, dst, s):
        b = self.order[s]
        partner = self.e + (1 - 2 * self.bit(b)) * 2**b
        return remote(src, dst, self.ss.at[self.base, s], self.rs.at[self.base, s], self.t, partner)


class EpSum(EpBits):
    def __init__(self, data, land, first, rows, order, sems, base):
        super().__init__(first, rows, order, sems, base)
        self.data, self.land = data, land

    def half(self, s, keep):
        size, bit = self.size(s), self.bit(self.order[s])
        which = bit if keep else 1 - bit
        if s == 0:
            return self.data.at[self.cut(which * size, size)]
        return self.land.at[pl.ds(pl.multiple_of(self.landing(s - 1) + which * size, 16), size)]

    def out(self, s):
        return self.move(self.half(s, False), self.land.at[pl.ds(self.landing(s), self.size(s))], s)

    def start(self, s):
        self.out(s).start()

    def add(self, s):
        self.out(s).wait_recv()
        spot = pl.ds(self.landing(s), self.size(s))
        self.land[spot, :] = (self.land[spot, :].astype(F32) + self.half(s, True)[...].astype(F32)).astype(BF16)

    def result(self):
        last = len(self.order) - 1
        return self.land[pl.ds(self.landing(last), self.size(last)), :]

    def sent(self):
        for s in range(len(self.order)):
            self.out(s).wait_send()


class EpGather(EpBits):
    def __init__(self, full, first, rows, order, sems, base):
        super().__init__(first, rows, order, sems, base)
        self.full = full

    def part(self, s, other):
        size, bit = self.size(s), self.bit(self.order[s])
        return self.full.at[self.cut(self.low[s] + ((1 - bit) if other else bit) * size, size)]

    def own(self):
        return self.part(len(self.order) - 1, False)

    def give(self, s, src=None):
        part = self.part(s, False)
        self.move(part if src is None else src, part, s).start()

    def take(self, s):
        part = self.part(s, True)
        self.move(part, part, s).wait_recv()

    def sent(self):
        for s in range(len(self.order)):
            part = self.part(s, False)
            self.move(part, part, s).wait_send()


def ep_cuts(rows, n_ep):
    return max(q for q in (4, 2, 1) if q == 1 or rows % (16 * q * n_ep) == 0)


def piece_orders(cuts, n_ep):
    natural = list(range(n_ep.bit_length() - 1))
    turned = [natural[1], natural[0]] + natural[2:]
    return [turned if 4 * k >= 3 * cuts and cuts > 1 else natural for k in range(cuts)]


class Slots:
    def __init__(self):
        self.lists, self.at = {}, 0

    def put(self, slot, action):
        self.lists.setdefault(slot, []).append(action)

    def run(self, slot):
        for action in self.lists.get(slot, []):
            action()

    def next(self, count=1):
        for _ in range(count):
            self.run(self.at)
            self.at += 1

    def rest(self):
        for slot in sorted(self.lists):
            if slot >= self.at:
                self.run(slot)
        self.at = 1 + max(self.lists, default=-1)


def plan_sum(slots, piece, first, bits, lag=2, stride=1):
    def step(s):
        piece.add(s)
        if s + 1 < bits:
            piece.start(s + 1)

    slots.put(first, lambda: piece.start(0))
    for s in range(bits):
        slots.put(first + lag + stride * s, lambda s=s: step(s))


def plan_gather(slots, piece, own, sem, first, bits):
    piece.give(bits - 1, own)
    pltpu.make_async_copy(own, piece.own(), sem).start()

    def step(s):
        if s == bits - 1:
            pltpu.make_async_copy(own, piece.own(), sem).wait()
        piece.take(s)
        if s > 0:
            piece.give(s - 1)

    for s in range(bits - 1, -1, -1):
        slots.put(first + 2 * (bits - 1 - s) if s else 99, lambda s=s: step(s))


def expert_kernel(
    n_tp, n_ep, rows, crow, eup, edown, mixw, wdiff, gshare, tgtc, gup,
    geup_o, gedown_o, gsec_o, gmix_o, oshare_o, sup_o,
    act, gpre, grow, part, cbuf, xrcv, rsnd, ret, ypart, ybuf, yxrcv, ysnd, yret, uland,
    rcs, rcr, rxs, rxr, as_, ar_, lsem,
    ycs, ycr, yxs, yxr, ys_, yr_, ylsem, uss, urs,
):
    t, x, c, e = place()
    nx = n_tp // 2
    experts, slots, share = rows.shape[1:]
    total_rows = experts * slots
    half = crow.shape[3]
    width = 2 * half
    units = eup.shape[1]
    nb = experts // 4
    size = nb * slots
    tok_rows = tgtc.shape[0]
    blk = tok_rows // 4
    mate = 2 * x + 1 - c
    x_peers = [2 * lax.rem(x + d, nx) + c for d in range(1, nx)]
    greet([(mate, e)] + [(p, e) for p in x_peers], lambda i: (t, lax.rem(e + 1 + i, n_ep)), n_ep - 1)

    def piece(i):
        return lax.rem(lax.div(e, nb) + 1 + i, 4)

    def span(i):
        return pl.ds(pl.multiple_of(piece(i) * size, size), size)

    def chunk(i):
        return pl.ds(i * blk, blk)

    reduce = TpReduce(nx, (part, cbuf, xrcv), (rcs, rcr, rxs, rxr), span)
    reduce_y = TpReduce(nx, (ypart, ybuf, yxrcv), (ycs, ycr, yxs, yxr), span)
    back = EpReturn(rsnd, ret, slots, (as_, ar_, lsem))
    back_y = EpReturn(ysnd, yret, slots, (ys_, yr_, ylsem))
    bits = n_ep.bit_length() - 1
    up_cuts = sup_o.shape[0]
    up_rows = gup.shape[0] // up_cuts
    orders = piece_orders(up_cuts, n_ep)
    sums = [EpSum(gup, uland, k * up_rows, up_rows, orders[k], (uss, urs), k) for k in range(up_cuts)]
    slots_ = Slots()
    for k, one_sum in enumerate(sums):
        plan_sum(slots_, one_sum, k if k > 1 else 0, bits)
    fblk = min(256, units)
    steps = units // fblk
    gmix_o[...] = jnp.zeros_like(gmix_o)
    slots_.next(2)

    def work(i):
        bs = pl.ds(piece(i) * nb, nb)
        rs = span(i)

        def share_rows(g):
            return rows[g, bs].reshape(size, share)

        logits = jnp.zeros((size, 128), F32)
        for g in range(n_tp):
            logits = logits + mm(share_rows(g), mixw[pl.ds(g * share, share), :])
        lane = lax.broadcasted_iota(jnp.int32, logits.shape, 1)
        logits = jnp.where(lane < 2, logits, masked_value)
        mix = jnp.exp(logits - jnp.max(logits, axis=1, keepdims=True))
        mix = mix / jnp.sum(mix, axis=1, keepdims=True)
        mix0, mix1 = mix[:, 0:1], mix[:, 1:2]
        for h in range(2):
            grow[rs, pl.ds(h * half, half)] = (mix1 * crow[h, bs].reshape(size, half).astype(F32)).astype(BF16)

        def one(f, carry):
            fs = pl.ds(pl.multiple_of(f * fblk, fblk), fblk)
            pre = mm(share_rows(0), eup[pl.ds(0, share), fs])
            for g in range(1, n_tp):
                pre = pre + mm(share_rows(g), eup[pl.ds(g * share, share), fs])
            value, slope = gelu_pair(pre)
            act[rs, fs] = value.astype(BF16)
            gpre[rs, fs] = (mm_t(grow[rs, :], edown[fs, :]) * slope).astype(BF16)
            return carry

        lax.fori_loop(0, steps, one, 0)
        col1 = jnp.zeros((size, 1), F32)
        per_half = n_tp // 2
        for g in range(n_tp):
            gs = pl.ds(g * share, share)
            eout = mm(act[rs, :], edown[:, gs])
            cots = crow[g // per_half, bs, :, pl.ds((g % per_half) * share, share)].reshape(size, share)
            col1 = col1 + jnp.sum(eout * cots.astype(F32), axis=1, keepdims=True)
            ypart[g % 2, g // 2, rs, :] = (mix1 * eout).astype(BF16)
        logit = -(mix0 * mix1 * col1)
        for g in range(n_tp):
            gs = pl.ds(g * share, share)
            grad_in = mm_t(gpre[rs, :], eup[gs, :]) + logit * wdiff[:, gs]
            part[g % 2, g // 2, rs, :] = grad_in.astype(BF16)
            tally = jnp.sum(logit * share_rows(g).astype(F32), axis=0, keepdims=True)
            gmix_o[:, gs] = gmix_o[:, gs] + jnp.broadcast_to(tally, (8, share))
        reduce.start(i)
        reduce_y.start(i)

    def send_back(i):
        rsnd[span(i), :] = reduce.total(i).astype(BF16)
        back.send(piece(i) * nb, nb)

    def send_back_y(i):
        ysnd[span(i), :] = reduce_y.total(i).astype(BF16)
        back_y.send(piece(i) * nb, nb)

    def step(i, carry):
        work(i)

        @pl.when(i >= 1)
        def _():
            reduce.sum_cores(i - 1)

        @pl.when(i >= 2)
        def _():
            reduce_y.sum_cores(i - 2)
            send_back(i - 2)

        for j in range(4):

            @pl.when(i == j)
            def _():
                slots_.run(2 + j)

        return carry

    lax.fori_loop(0, 4, step, 0)
    slots_.at = 6
    reduce.sum_cores(3)
    reduce_y.sum_cores(2)
    slots_.next()

    def down_grad(k):
        fs = pl.ds(k * fblk, fblk)
        gedown_o[fs, :] = t_mm(act[:, fs], grow[...])

    def up_grad(g):
        geup_o[pl.ds(g * share, share), :] = t_mm(rows[g].reshape(total_rows, share), gpre[...])

    send_back_y(0)
    for k in range(steps // 2):
        down_grad(k)
    send_back(2)
    slots_.next()
    for k in range(steps // 2, steps):
        down_grad(k)
    send_back(3)
    reduce_y.sum_cores(3)
    send_back_y(1)
    slots_.next()
    up_grad(0)
    send_back_y(2)
    for g in range(1, n_tp // 2):
        up_grad(g)
    slots_.next()

    def hot_rows(i):
        ids = lax.broadcasted_iota(jnp.int32, (blk, total_rows), 1)
        return (ids == tgtc[chunk(i), 0:1]).astype(F32).astype(BF16)

    back.arrived(n_ep)
    for i in range(4):
        gsec_o[chunk(i), :] = (gshare[chunk(i), :] + mm(hot_rows(i), ret[...])).astype(BF16)
    send_back_y(3)
    slots_.next()
    for g in range(n_tp // 2, n_tp):
        up_grad(g)
    slots_.rest()
    for k in range(up_cuts):
        sup_o[k] = sums[k].result()
    back_y.arrived(n_ep)
    for i in range(4):
        oshare_o[chunk(i), :] = mm(hot_rows(i), yret[...])
    back.sent(n_ep)
    back_y.sent(n_ep)
    for i in range(4):
        reduce.sent(i)
        reduce_y.sent(i)
    for one_sum in sums:
        one_sum.sent()


class EpReturn:
    def __init__(self, snd, ret, slots, sems):
        self.snd, self.ret, self.slots = snd, ret, slots
        self.ss, self.rs, self.local = sems
        self.t, self.x, self.c, self.e = place()

    def block(self, k):
        return pl.ds(pl.multiple_of(k * self.slots, self.slots), self.slots)

    def copy(self, dest, src):
        return remote(
            self.snd.at[self.block(dest)], self.ret.at[self.block(src)], self.ss.at[dest], self.rs.at[src], self.t, dest
        )

    def own(self):
        mine = self.block(self.e)
        return pltpu.make_async_copy(self.snd.at[mine], self.ret.at[mine], self.local)

    def send(self, first, count):
        def one(k, carry):
            dest = first + k

            @pl.when(dest != self.e)
            def _():
                self.copy(dest, self.e).start()

            @pl.when(dest == self.e)
            def _():
                self.own().start()

            return carry

        lax.fori_loop(0, count, one, 0)

    def arrived(self, n_ep):
        def one(k, carry):
            self.copy(self.e, lax.rem(self.e + n_ep - k, n_ep)).wait_recv()
            return carry

        lax.fori_loop(1, n_ep, one, 0)
        self.own().wait()

    def sent(self, n_ep):
        def one(k, carry):
            self.copy(lax.rem(self.e + k, n_ep), self.e).wait_send()
            return carry

        lax.fori_loop(1, n_ep, one, 0)


class TpGather:
    def __init__(self, nx, full, share, blk, sems):
        self.full, self.share, self.blk, self.nx = full, share, blk, nx
        self.xs, self.xr, self.ms, self.mr = sems
        self.t, self.x, self.c, self.e = place()
        self.mate = 2 * self.x + 1 - self.c

    def cut(self, i, g):
        return self.full.at[
            pl.ds(i * self.blk, self.blk), pl.ds(pl.multiple_of(g * self.share, self.share), self.share)
        ]

    def across(self, i, d):
        there = 2 * lax.rem(self.x + d, self.nx) + self.c
        mine = self.cut(i, self.t)
        return remote(mine, mine, self.xs.at[i, d - 1], self.xr.at[i, d - 1], there, self.e)

    def beside(self, i, xi, c):
        got = self.cut(i, 2 * xi + c)
        return remote(got, got, self.ms.at[i, xi], self.mr.at[i, xi], self.mate, self.e)

    def put(self, i, value):
        cols = pl.ds(pl.multiple_of(self.t * self.share, self.share), self.share)
        self.full[pl.ds(i * self.blk, self.blk), cols] = value
        for d in range(1, self.nx):
            self.across(i, d).start()
        self.beside(i, self.x, self.c).start()

    def pass_on(self, i):
        for d in range(1, self.nx):
            xi = lax.rem(self.x + self.nx - d, self.nx)
            got = self.cut(i, 2 * xi + self.c)
            remote(got, got, self.xs.at[i, d - 1], self.xr.at[i, d - 1], self.mate, self.e).wait_recv()
            self.beside(i, xi, self.c).start()

    def finish(self, i):
        for xi in range(self.nx):
            self.beside(i, xi, 1 - self.c).wait_recv()
            self.beside(i, xi, self.c).wait_send()
        for d in range(1, self.nx):
            self.across(i, d).wait_send()


def expert_block(rows, cot_rows, eup, edown, mix_weight, wdiff, gshare, targets_col, gup):
    n_tp, n_ep = lax.axis_size("tp"), lax.axis_size("ep")
    _, experts, slots, share = rows.shape
    tok_rows = targets_col.shape[0]
    width, units = eup.shape
    nx = n_tp // 2
    dx = max(nx - 1, 1)
    total = experts * slots
    bits = n_ep.bit_length() - 1
    up_cuts = ep_cuts(width, n_ep)
    vm = pl.BlockSpec(memory_space=pltpu.VMEM)
    dma = pltpu.SemaphoreType.DMA
    shape = jax.ShapeDtypeStruct
    mixw = jnp.pad(mix_weight, ((0, 0), (0, 126)))
    return pl.pallas_call(
        functools.partial(expert_kernel, n_tp, n_ep),
        out_shape=(
            shape((width, units), F32),
            shape((units, width), F32),
            shape((tok_rows, share), BF16),
            shape((8, width), F32),
            shape((tok_rows, share), F32),
            shape((up_cuts, width // up_cuts // n_ep, units), BF16),
        ),
        in_specs=[vm] * 9,
        out_specs=(vm,) * 6,
        scratch_shapes=[
            pltpu.VMEM((total, units), BF16),
            pltpu.VMEM((total, units), BF16),
            pltpu.VMEM((total, width), BF16),
            pltpu.VMEM((2, nx, total, share), BF16),
            pltpu.VMEM((nx, total, share), BF16),
            pltpu.VMEM((nx, total, share), BF16),
            pltpu.VMEM((total, share), BF16),
            pltpu.VMEM((total, share), BF16),
            pltpu.VMEM((2, nx, total, share), BF16),
            pltpu.VMEM((nx, total, share), BF16),
            pltpu.VMEM((nx, total, share), BF16),
            pltpu.VMEM((total, share), BF16),
            pltpu.VMEM((total, share), BF16),
            pltpu.VMEM((width, units), BF16),
            dma((4,)), dma((4,)), dma((4, dx)), dma((4, dx)),
            dma((experts,)), dma((experts,)), dma,
            dma((4,)), dma((4,)), dma((4, dx)), dma((4, dx)),
            dma((experts,)), dma((experts,)), dma,
            dma((up_cuts, bits)), dma((up_cuts, bits)),
        ],
        compiler_params=pltpu.CompilerParams(
            collective_id=2, has_side_effects=True, vmem_limit_bytes=VMEM_LIMIT + 3 * 2**20
        ),
        cost_estimate=pl.CostEstimate(flops=24 * 10**9, bytes_accessed=50 * 10**6, transcendentals=0),
        name="experts",
    )(rows, cot_rows, eup, edown, mixw, wdiff, gshare, targets_col, gup)


class TpSum:
    def __init__(self, nx, full, bufs, sems, blk):
        self.full, self.blk, self.nx = full, blk, nx
        self.part, self.cbuf, self.xbuf = bufs
        self.cs, self.cr, self.xs, self.xr, self.gs, self.gr = sems
        self.t, self.x, self.c, self.e = place()
        self.mate = 2 * self.x + 1 - self.c
        half = self.cbuf.shape[1]
        self.mine = pl.ds(pl.multiple_of(self.c * half, half), half)
        self.other = pl.ds(pl.multiple_of((1 - self.c) * half, half), half)

    def span(self, i):
        return pl.ds(i * self.blk, self.blk)

    def core(self, i):
        return remote(
            self.part.at[self.span(i), self.other], self.cbuf.at[self.span(i)], self.cs.at[i], self.cr.at[i],
            self.mate, self.e,
        )

    def chip(self, i, d):
        there = 2 * lax.rem(self.x + d, self.nx) + self.c
        mine = self.xbuf.at[self.x, self.span(i)]
        return remote(mine, mine, self.xs.at[i, d - 1], self.xr.at[i, d - 1], there, self.e)

    def start(self, i):
        self.core(i).start()

    def sum_cores(self, i):
        self.core(i).wait_recv()
        both = self.part[self.span(i), self.mine].astype(F32) + self.cbuf[self.span(i), :].astype(F32)
        self.xbuf[self.x, self.span(i), :] = both.astype(BF16)
        for d in range(1, self.nx):
            self.chip(i, d).start()

    def share(self, i, cols):
        got = self.full.at[self.span(i), cols]
        return remote(got, got, self.gs.at[i], self.gr.at[i], self.mate, self.e)

    def sum_chips(self, i):
        for d in range(1, self.nx):
            src = lax.rem(self.x + self.nx - d, self.nx)
            got = self.xbuf.at[src, self.span(i)]
            remote(got, got, self.xs.at[i, d - 1], self.xr.at[i, d - 1], self.mate, self.e).wait_recv()
        total = self.xbuf[0, self.span(i), :].astype(F32)
        for j in range(1, self.nx):
            total = total + self.xbuf[j, self.span(i), :].astype(F32)
        self.full[self.span(i), self.mine] = total.astype(BF16)
        self.share(i, self.mine).start()

    def wait(self, i):
        self.share(i, self.other).wait_recv()
        self.share(i, self.mine).wait_send()

    def sent(self, i):
        self.core(i).wait_send()
        for d in range(1, self.nx):
            self.chip(i, d).wait_send()


def backward_kernel(
    n_tp, n_ep, tok, cot, attn, gshare, qkv, ht, lse, wqkv, wout, g1, b1, g2, segr, segc, oshare, sup, y, gdown,
    out_o, gh, part, wdat, small, gup_o, sdown_o,
    ga, gheads, kt, dqt, pcat, dcat, gcat, qcat, dk, dv, gj, bias,
    gsec, dbuf, dxrcv, dland,
    oxs, oxr, oms, omr, hxs, hxr, hms, hmr, uss, urs, usem, dcs, dcr, dxs, dxr, dss, drs,
):
    t, x, c, e = place()
    nx = n_tp // 2
    rows_all, width = tok.shape
    wl = wout.shape[0]
    heads = wl // HD
    blk = rows_all // 4
    share = oshare.shape[1]
    bits = n_ep.bit_length() - 1
    greet(
        [(2 * x + 1 - c, e)] + [(2 * lax.rem(x + d, nx) + c, e) for d in range(1, nx)],
        lambda i: (t, lax.rem(e + 1 + i, n_ep)),
        n_ep - 1,
    )

    def chunk(i):
        return pl.ds(i * blk, blk)

    gather = TpGather(nx, out_o, share, blk, (oxs, oxr, oms, omr))
    gather_g = TpGather(nx, gsec, share, blk, (hxs, hxr, hms, hmr))
    for i in (3, 2, 1, 0):
        gather_g.put(i, gshare[chunk(i), :])
    group = pcat.shape[1] // blk
    gw = group * HD
    up_cuts = sup.shape[0]
    up_rows = gup_o.shape[0] // up_cuts
    orders = piece_orders(up_cuts, n_ep)
    wide = [EpGather(gup_o, k * up_rows, up_rows, orders[k], (uss, urs), k) for k in range(up_cuts)]
    slots_ = Slots()
    for k, one in enumerate(wide):
        plan_gather(slots_, one, sup.at[k], usem.at[k], k + 1, bits)
    reduce_d = TpReduce(nx, (y, dbuf, dxrcv), (dcs, dcr, dxs, dxr), chunk)
    for i in range(4):
        reduce_d.start(i)
    down_cuts = sdown_o.shape[0]
    down_rows = gdown.shape[0] // down_cuts
    down_orders = piece_orders(down_cuts, n_ep)
    downs = [EpSum(gdown, dland, k * down_rows, down_rows, down_orders[k], (dss, drs), k) for k in range(down_cuts)]
    for k, one in enumerate(downs):
        plan_sum(slots_, one, 0, bits, 1 + 2 * k + k // 3, 2)
    slots_.next()
    my_cols = pl.ds(pl.multiple_of(t * share, share), share)

    def put_output(i):
        rs = chunk(i)
        hidden = tok[rs, my_cols].astype(F32) + attn[rs, my_cols].astype(F32)
        gather.put(i, (hidden + oshare[rs, :] + reduce_d.total(i)).astype(BF16))

    sum_gain = jnp.zeros((1, width), F32)
    sum_bias = jnp.zeros((1, width), F32)
    gather_g.pass_on(3)
    for i in (3, 2, 1, 0):
        rs = chunk(i)
        if i > 0:
            gather_g.pass_on(i - 1)
        gather_g.finish(i)
        unit, spread = norm_rows(tok[rs, :].astype(F32) + attn[rs, :].astype(F32))
        up = gsec[rs, :].astype(F32)
        sum_gain = sum_gain + jnp.sum(up * unit, axis=0, keepdims=True)
        sum_bias = sum_bias + jnp.sum(up, axis=0, keepdims=True)
        gv = up * g2[...]
        inner = gv - jnp.mean(gv, axis=-1, keepdims=True) - unit * jnp.mean(gv * unit, axis=-1, keepdims=True)
        grad = cot[rs, :].astype(F32) + spread * inner
        gh[rs, :] = grad
        ga[rs, :] = grad.astype(BF16)
        gheads[rs, :] = mm_t(ga[rs, :], wout[...]).astype(BF16)
        reduce_d.sum_cores(i)
        slots_.next()
    small[...] = jnp.zeros_like(small)
    small[2:3, :] = sum_gain
    small[3:4, :] = sum_bias
    wdat[pl.ds(0, wl), :] = mm(ht[...], ga[...]).astype(BF16)
    for i in range(4):
        rs = chunk(i)
        unit, _ = norm_rows(tok[rs, :].astype(F32))
        ga[rs, :] = (unit * g1[...] + b1[...]).astype(BF16)
        kt[:, rs] = qkv[1, rs, :].astype(F32).T.astype(BF16)

    head_of = lax.div(lax.broadcasted_iota(jnp.int32, (blk, gw), 1), HD)

    def attend(i, first, last):
        keys = (i + 1) * blk
        ks = pl.ds(0, keys)
        hc = pl.ds(first * HD, gw)
        allowed = (segc[ks, :] == segr[:, chunk(i)]) & (
            lax.broadcasted_iota(jnp.int32, (keys, blk), 0)
            <= lax.broadcasted_iota(jnp.int32, (keys, blk), 1) + i * blk
        )
        bias[ks, :] = jnp.where(allowed, 0.0, masked_value)

        def one_head(k, carry):
            h = first + k
            q_h = jnp.where(head_of == k, qkv[0, chunk(i), hc].astype(F32) * 0.125, 0.0).astype(BF16)
            g_h = jnp.where(head_of == k, gheads[chunk(i), hc].astype(F32), 0.0).astype(BF16)
            hb = pl.ds(pl.multiple_of(k * blk, blk), blk)
            gcat[hb, :] = g_h
            qcat[hb, :] = q_h
            probs = jnp.exp(mm_t(qkv[1, ks, hc], q_h) + bias[ks, :] - lse[pl.ds(h, 1), chunk(i)])
            pcat[ks, hb] = probs.astype(BF16)
            grad = mm_t(qkv[2, ks, hc], g_h)
            mean = jnp.sum(probs * grad, axis=0, keepdims=True)
            scores = (probs * (grad - mean)).astype(BF16)
            dcat[ks, hb] = scores
            dqt[pl.ds(pl.multiple_of(k * HD, HD), HD), :] = mm(
                kt[pl.ds(pl.multiple_of(h * HD, HD), HD), ks], scores
            )
            return carry

        lax.fori_loop(0, group, one_head, 0)
        dv_new, dk_new = mm(pcat[ks, :], gcat[...]), mm(dcat[ks, :], qcat[...])
        if i == 3:
            dv[ks, :] = dv_new
            dk[ks, :] = dk_new
        else:
            dv[ks, :] = dv[ks, :] + dv_new
            dk[ks, :] = dk[ks, :] + dk_new
        gj[0, chunk(i), hc] = (dqt[...].T * 0.125).astype(BF16)
        gj[1, chunk(i), hc] = dk[chunk(i), :].astype(BF16)
        gj[2, chunk(i), hc] = dv[chunk(i), :].astype(BF16)
        if last:
            grad_in = mm_t(gj[0, chunk(i), :], wqkv[0])
            for j in range(1, 3):
                grad_in = grad_in + mm_t(gj[j, chunk(i), :], wqkv[j])
            part[chunk(i), :] = grad_in.astype(BF16)

    def weight_grads(first):
        for j in range(3):
            row = wl + j * wl + first * HD
            wdat[pl.ds(row, gw), :] = t_mm(gj[j, :, pl.ds(first * HD, gw)], ga[...]).astype(BF16)

    groups = list(range(0, heads, group))
    for first in groups:
        last = first == groups[-1]
        for i in (3, 2, 1, 0):
            attend(i, first, last)
            slots_.next()
            if first == 0 and i == 3:
                for k in (3, 2, 1, 0):
                    put_output(k)
            if last and i == 1:
                for k in (3, 2, 1, 0):
                    gather.pass_on(k)
        weight_grads(first)
    slots_.rest()
    for i in range(4):
        gather.finish(i)
    for k in range(down_cuts):
        sdown_o[k] = downs[k].result()
    for one in wide + downs:
        one.sent()
    for i in range(4):
        reduce_d.sent(i)


def finish_kernel(
    n_tp, n_ep, tok, gh, part, g1, first_sums, gmix, wpart, sdown,
    gtok_o, small_o, wsum_o, gdown_o,
    cbuf, xbuf, small, sland, mland, wland,
    wss, wrs, wgs, wgr, dss, drs, dsem, tcs, tcr, txs, txr, tgs, tgr, ss_, sr_, mgs, mgr,
):
    t, x, c, e = place()
    nx = n_tp // 2
    rows_all, width = tok.shape
    blk = rows_all // 4
    greet(
        [(lax.rem(t + d, n_tp), e) for d in range(1, n_tp)], lambda i: (t, lax.rem(e + 1 + i, n_ep)), n_ep - 1
    )

    def chunk(i):
        return pl.ds(i * blk, blk)

    tp_sum = TpSum(nx, gtok_o, (part, cbuf, xbuf), (tcs, tcr, txs, txr, tgs, tgr), blk)
    for i in range(4):
        tp_sum.start(i)

    def mix_copy(d):
        return remote(gmix, mland.at[t], mgs.at[d - 1], mgr.at[d - 1], lax.rem(t + d, n_tp), e)

    mland[t] = gmix[...]
    for d in range(1, n_tp):
        mix_copy(d).start()
    small[...] = first_sums[...]
    bits = n_ep.bit_length() - 1
    cuts = wss.shape[0]
    cut_rows = wpart.shape[0] // cuts
    orders = piece_orders(cuts, n_ep)
    sums = [EpSum(wpart, wland, k * cut_rows, cut_rows, orders[k], (wss, wrs), k) for k in range(cuts)]
    gathers = [EpGather(wsum_o, k * cut_rows, cut_rows, orders[k], (wgs, wgr), k) for k in range(cuts)]
    down_cuts = sdown.shape[0]
    down_rows = gdown_o.shape[0] // down_cuts
    down_orders = piece_orders(down_cuts, n_ep)
    wide = [EpGather(gdown_o, k * down_rows, down_rows, down_orders[k], (dss, drs), k) for k in range(down_cuts)]
    slots_ = Slots()
    for one_sum in sums:
        one_sum.start(0)
    for k, one in enumerate(wide):
        plan_gather(slots_, one, sdown.at[k], dsem.at[k], k + 1, bits)
    for i in range(4):
        tp_sum.sum_cores(i)

    tally = [jnp.zeros((1, width), F32), jnp.zeros((1, width), F32)]

    def finish(i):
        rs = chunk(i)
        tp_sum.wait(i)
        unit, spread = norm_rows(tok[rs, :].astype(F32))
        up = gtok_o[rs, :].astype(F32)
        tally[0] = tally[0] + jnp.sum(up * unit, axis=0, keepdims=True)
        tally[1] = tally[1] + jnp.sum(up, axis=0, keepdims=True)
        gv = up * g1[...]
        inner = gv - jnp.mean(gv, axis=-1, keepdims=True) - unit * jnp.mean(gv * unit, axis=-1, keepdims=True)
        gtok_o[rs, :] = (gh[rs, :] + spread * inner).astype(BF16)

    def step(k, stage):
        if stage < bits:
            sums[k].add(stage)
            if stage + 1 < bits:
                sums[k].start(stage + 1)
            else:
                gathers[k].own()[...] = sums[k].result()
                gathers[k].give(stage)
        else:
            s = 2 * bits - 1 - stage
            gathers[k].take(s)
            if s > 0:
                gathers[k].give(s - 1)

    beats = [[] for _ in range(cuts + 4 * bits)]
    for k in range(cuts):
        for stage in range(2 * bits - 1):
            beats[k + 1 + 2 * stage].append((stage, k))
    beats = [sorted(b, reverse=True) for b in beats if b]
    apart = max(len(beats) // 8, 1)
    for n, beat in enumerate(beats):
        for stage, k in beat:
            step(k, stage)
        slots_.next()
        at = n // apart
        if n % apart == 0 and at < 4:
            tp_sum.sum_chips(at)
        if n % apart == 0 and 1 <= at < 5:
            finish(at - 1)
    for i in range(len(beats[::apart]), 5):
        if i < 4:
            tp_sum.sum_chips(i)
        finish(i - 1)
    small[0:1, :] = tally[0]
    small[1:2, :] = tally[1]
    mix_total = jnp.zeros((1, width), F32)
    for d in range(1, n_tp):
        got = mland.at[lax.rem(t + n_tp - d, n_tp)]
        remote(got, got, mgs.at[d - 1], mgr.at[d - 1], lax.rem(t + d, n_tp), e).wait_recv()
    for j in range(n_tp):
        mix_total = mix_total + mland[j, 0:1, :]
    small[4:5, :] = mix_total
    sland[e] = small[...]

    def small_copy(dest, src):
        return remote(small, sland.at[src], ss_.at[dest], sr_.at[src], t, dest)

    def send_small(k, carry):
        small_copy(lax.rem(e + k, n_ep), e).start()
        return carry

    lax.fori_loop(1, n_ep, send_small, 0)

    slots_.rest()
    for k in range(cuts):
        step(k, 2 * bits - 1)

    def small_arrived(k, carry):
        small_copy(e, lax.rem(e + n_ep - k, n_ep)).wait_recv()
        return carry

    lax.fori_loop(1, n_ep, small_arrived, 0)
    small_o[...] = lax.fori_loop(0, n_ep, lambda k, total: total + sland[k], jnp.zeros_like(small_o))

    def sent(k, carry):
        dest = lax.rem(e + k, n_ep)
        small_copy(dest, e).wait_send()
        return carry

    lax.fori_loop(1, n_ep, sent, 0)
    for d in range(1, n_tp):
        mix_copy(d).wait_send()
    for i in range(4):
        tp_sum.sent(i)
    for one in sums + gathers + wide:
        one.sent()


def backward(tokens, cotangent, attn, gshare, qkv, ht, lse, wqkv, wout, g1, b1, g2, segments, oshare, sup, y, gdown):
    n_tp, n_ep = lax.axis_size("tp"), lax.axis_size("ep")
    rows, width = tokens.shape
    wl = wout.shape[0]
    nx = n_tp // 2
    dx = max(nx - 1, 1)
    blk = rows // 4
    group = min(2, wl // HD)
    bits = n_ep.bit_length() - 1
    up_cuts, up_rows, units = sup.shape
    share = oshare.shape[1]
    down_cuts = ep_cuts(units, n_ep)
    vm = pl.BlockSpec(memory_space=pltpu.VMEM)
    dma = pltpu.SemaphoreType.DMA
    shape = jax.ShapeDtypeStruct
    return pl.pallas_call(
        functools.partial(backward_kernel, n_tp, n_ep),
        out_shape=(
            shape((rows, width), BF16),
            shape((rows, width), F32),
            shape((rows, width), BF16),
            shape((4 * wl, width), BF16),
            shape((8, width), F32),
            shape((up_cuts * up_rows * n_ep, units), BF16),
            shape((down_cuts, units // down_cuts // n_ep, width), BF16),
        ),
        in_specs=[vm] * 18,
        out_specs=(vm,) * 5 + (pl.BlockSpec(memory_space=pl.ANY), vm),
        scratch_shapes=[
            pltpu.VMEM((rows, width), BF16),
            pltpu.VMEM((rows, wl), BF16),
            pltpu.VMEM((wl, rows), BF16),
            pltpu.VMEM((group * HD, blk), F32),
            pltpu.VMEM((rows, group * blk), BF16),
            pltpu.VMEM((rows, group * blk), BF16),
            pltpu.VMEM((group * blk, group * HD), BF16),
            pltpu.VMEM((group * blk, group * HD), BF16),
            pltpu.VMEM((rows, group * HD), F32),
            pltpu.VMEM((rows, group * HD), F32),
            pltpu.VMEM((3, rows, wl), BF16),
            pltpu.VMEM((rows, blk), F32),
            pltpu.VMEM((rows, width), BF16),
            pltpu.VMEM((nx, rows, share), BF16),
            pltpu.VMEM((nx, rows, share), BF16),
            pltpu.VMEM((units, width), BF16),
            dma((4, dx)), dma((4, dx)), dma((4, nx)), dma((4, nx)),
            dma((4, dx)), dma((4, dx)), dma((4, nx)), dma((4, nx)),
            dma((up_cuts, bits)), dma((up_cuts, bits)), dma((up_cuts,)),
            dma((4,)), dma((4,)), dma((4, dx)), dma((4, dx)), dma((down_cuts, bits)), dma((down_cuts, bits)),
        ],
        compiler_params=pltpu.CompilerParams(
            collective_id=3, has_side_effects=True, vmem_limit_bytes=VMEM_LIMIT
        ),
        cost_estimate=pl.CostEstimate(flops=60 * 10**9, bytes_accessed=50 * 10**6, transcendentals=0),
        name="attention_backward",
    )(
        tokens, cotangent, attn, gshare, qkv, ht, lse, wqkv, wout, g1.reshape(1, width), b1.reshape(1, width),
        g2.reshape(1, width), segments, segments.reshape(rows, 1), oshare, sup, y, gdown,
    )


def finish_block(tokens, gh, part, g1, first_sums, gmix, wpart, sdown):
    n_tp, n_ep = lax.axis_size("tp"), lax.axis_size("ep")
    rows, width = tokens.shape
    nx = n_tp // 2
    dx = max(nx - 1, 1)
    half = width // 2
    bits = n_ep.bit_length() - 1
    down_cuts, down_rows, _ = sdown.shape
    cuts = max(q for q in (8, 4, 2, 1) if q == 1 or wpart.shape[0] % (16 * q * n_ep) == 0)
    vm = pl.BlockSpec(memory_space=pltpu.VMEM)
    dma = pltpu.SemaphoreType.DMA
    return pl.pallas_call(
        functools.partial(finish_kernel, n_tp, n_ep),
        out_shape=(
            jax.ShapeDtypeStruct((rows, width), BF16),
            jax.ShapeDtypeStruct((8, width), F32),
            jax.ShapeDtypeStruct(wpart.shape, BF16),
            jax.ShapeDtypeStruct((down_cuts * down_rows * n_ep, width), BF16),
        ),
        in_specs=[vm] * 8,
        out_specs=(vm,) * 3 + (pl.BlockSpec(memory_space=pl.ANY),),
        scratch_shapes=[
            pltpu.VMEM((rows, half), BF16),
            pltpu.VMEM((nx, rows, half), BF16),
            pltpu.VMEM((8, width), F32),
            pltpu.VMEM((n_ep, 8, width), F32),
            pltpu.VMEM((n_tp, 8, width), F32),
            pltpu.VMEM(wpart.shape, BF16),
            dma((cuts, bits)), dma((cuts, bits)), dma((cuts, bits)), dma((cuts, bits)),
            dma((down_cuts, bits)), dma((down_cuts, bits)), dma((down_cuts,)),
            dma((4,)), dma((4,)), dma((4, dx)), dma((4, dx)), dma((4,)), dma((4,)),
            dma((n_ep,)), dma((n_ep,)), dma((n_tp,)), dma((n_tp,)),
        ],
        compiler_params=pltpu.CompilerParams(
            collective_id=4, has_side_effects=True, vmem_limit_bytes=VMEM_LIMIT
        ),
        cost_estimate=pl.CostEstimate(flops=40 * 10**9, bytes_accessed=50 * 10**6, transcendentals=0),
        name="finish_norm",
    )(tokens, gh, part, g1.reshape(1, width), first_sums, gmix, wpart, sdown)


def outputs_kernel(out, gtok, geup, gedown, gup, gdown, gout, gqkv, out_o, gtok_o, geup_o, gedown_o, gup_o, gdown_o, gout_o, gqkv_o):
    out_o[...] = out[...]
    gtok_o[...] = gtok[...]
    geup_o[0] = geup[...]
    gedown_o[0] = gedown[...]
    gup_o[...] = gup[...].astype(F32)
    gdown_o[...] = gdown[...].astype(F32)
    gout_o[...] = gout[...].astype(F32)
    wl = gqkv_o.shape[2]
    for j in range(3):
        gqkv_o[j] = gqkv[pl.ds((1 + j) * wl, wl), :].astype(F32).T


def write_outputs(out, gtok, geup, gedown, gup, gdown, wsum):
    rows, width = out.shape
    units = gup.shape[1]
    wl = wsum.shape[0] // 4
    steps = 8

    def by_rows(count, columns):
        return pl.BlockSpec((count // steps, columns), lambda i: (i, 0))

    lead_up = pl.BlockSpec((1, width // steps, units), lambda i: (0, i, 0))
    lead_down = pl.BlockSpec((1, units // steps, width), lambda i: (0, i, 0))
    shape = jax.ShapeDtypeStruct
    moved = 2 * (2 * rows * width) * 2 + 4 * width * units * 7 + 6 * 4 * wl * width
    return pl.pallas_call(
        outputs_kernel,
        grid=(steps,),
        out_shape=(
            shape((rows, width), BF16),
            shape((rows, width), BF16),
            shape((1, width, units), F32),
            shape((1, units, width), F32),
            shape((width, units), F32),
            shape((units, width), F32),
            shape((wl, width), F32),
            shape((3, width, wl), F32),
        ),
        in_specs=[
            by_rows(rows, width), by_rows(rows, width), by_rows(width, units), by_rows(units, width),
            by_rows(width, units), by_rows(units, width), by_rows(wl, width),
            pl.BlockSpec((4 * wl, width // steps), lambda i: (0, i)),
        ],
        out_specs=(
            by_rows(rows, width), by_rows(rows, width), lead_up, lead_down,
            by_rows(width, units), by_rows(units, width), by_rows(wl, width),
            pl.BlockSpec((3, width // steps, wl), lambda i: (0, i, 0)),
        ),
        cost_estimate=pl.CostEstimate(flops=10**6, bytes_accessed=moved, transcendentals=0),
        compiler_params=pltpu.CompilerParams(vmem_limit_bytes=VMEM_LIMIT + 3 * 2**20),
        name="final_outputs",
    )(out, gtok, geup, gedown, gup, gdown, wsum, wsum)


def local(
    tokens, segments, routes, capacity, ln1_gain, ln1_bias, qkv_weight, out_weight, ln2_gain, ln2_bias,
    mix_weight, up_weight, down_weight, expert_up, expert_down, cotangent,
):
    width = tokens.shape[1]
    experts = capacity.shape[0]
    qkv, heads_t, lse, normed2, attn_sum, mix, cot_rows, targets, targets_col = forward(
        tokens, cotangent, segments, routes, capacity, ln1_gain, ln1_bias, ln2_gain, ln2_bias,
        qkv_weight, out_weight, mix_weight,
    )
    mix_float = mix_weight.astype(F32)
    wdiff = (mix_float[:, 0] - mix_float[:, 1]).reshape(1, width)
    rows_in, grad_up, grad_down, y_part, gshare, gmix_dense = dense_block(
        normed2, targets, cotangent, mix, up_weight, down_weight, wdiff, experts
    )
    grad_expert_up, grad_expert_down, gsec, gmix_rows, out_share, part_up = expert_block(
        rows_in, cot_rows, expert_up[0], expert_down[0], mix_weight, wdiff, gshare, targets_col, grad_up
    )
    output, grad_hidden, part, wpart, first_sums, grad_up, part_down = backward(
        tokens, cotangent, attn_sum, gsec, qkv, heads_t, lse, qkv_weight, out_weight, ln1_gain, ln1_bias,
        ln2_gain, segments, out_share, part_up, y_part, grad_down,
    )
    grad_tokens, small, wsum, grad_down = finish_block(
        tokens, grad_hidden, part, ln1_gain, first_sums, gmix_dense + gmix_rows, wpart, part_down
    )
    output, grad_tokens, grad_expert_up, grad_expert_down, grad_up, grad_down, grad_out, grad_qkv = write_outputs(
        output, grad_tokens, grad_expert_up, grad_expert_down, grad_up, grad_down, wsum
    )
    return (
        output,
        grad_tokens,
        small[0],
        small[1],
        grad_qkv,
        grad_out,
        small[2],
        small[3],
        jnp.stack([small[4], -small[4]], axis=1),
        grad_up,
        grad_down,
        grad_expert_up,
        grad_expert_down,
    )


def solution(mesh):
    return jax.shard_map(
        local,
        mesh=mesh,
        in_specs=(
            P("ep", None),
            P("ep", None),
            P("ep"),
            P(),
            P(),
            P(),
            P(None, None, "tp"),
            P("tp", None),
            P(),
            P(),
            P(),
            P(None, "tp"),
            P("tp", None),
            P("ep", None, "tp"),
            P("ep", "tp", None),
            P("ep", None),
        ),
        out_specs=(
            P("ep", None),
            P("ep", None),
            P(),
            P(),
            P(None, None, "tp"),
            P("tp", None),
            P(),
            P(),
            P(),
            P(None, "tp"),
            P("tp", None),
            P("ep", None, "tp"),
            P("ep", "tp", None),
        ),
        check_vma=False,
    )
```

```python
import functools
import math

import jax
import jax.numpy as jnp
from jax import lax
from jax.experimental import pallas as pl
from jax.experimental.pallas import tpu as pltpu
from jax.sharding import PartitionSpec as P

HD = 64
epsilon = 1e-05
masked_value = -1e30
F32 = jnp.float32
BF16 = jnp.bfloat16
VMEM_LIMIT = 60 * 2**20
MESH = pl.DeviceIdType.MESH


def mm(a, b):
    return lax.dot_general(a, b, (((1,), (0,)), ((), ())), preferred_element_type=F32)


def mm_t(a, b):
    return lax.dot_general(a, b, (((1,), (1,)), ((), ())), preferred_element_type=F32)


def t_mm(a, b):
    return lax.dot_general(a, b, (((0,), (0,)), ((), ())), preferred_element_type=F32)


def norm_rows(x):
    centred = x - jnp.mean(x, axis=-1, keepdims=True)
    spread = lax.rsqrt(jnp.mean(centred * centred, axis=-1, keepdims=True) + epsilon)
    return centred * spread, spread


def place():
    t = lax.axis_index("tp")
    return t, lax.div(t, 2), lax.rem(t, 2), lax.axis_index("ep")


def remote(src, dst, send, recv, t, e):
    return pltpu.make_async_remote_copy(
        src_ref=src, dst_ref=dst, send_sem=send, recv_sem=recv, device_id=(t, e), device_id_type=MESH
    )


def greet(partners, loop_partner, loop_count):
    bar = pltpu.get_barrier_semaphore()
    for t, e in partners:
        pl.semaphore_signal(bar, inc=1, device_id=(t, e), device_id_type=MESH)

    def one(i, carry):
        t, e = loop_partner(i)
        pl.semaphore_signal(bar, inc=1, device_id=(t, e), device_id_type=MESH)
        return carry

    if loop_count:
        lax.fori_loop(0, loop_count, one, 0)
    pl.semaphore_wait(bar, len(partners) + loop_count)


def onehot_rows(tgt, first, count):
    rows = lax.broadcasted_iota(jnp.int32, (count, tgt.shape[1]), 0) + first
    return (rows == tgt).astype(F32).astype(BF16)


def forward_kernel(
    n_tp, n_ep, tok, cot, segr, segc, rts, cap, g1, b1, g2, b2, wqkv, wout, mixw,
    qkv_o, ht_o, lse_o, n2_o, attn_o, mix_o, crow_o, tgt_o, tgtc_o,
    vt, snd, part, cbuf, xbuf, bias,
    as_, ar_, fs_, fr_, cs_, cr_, xs_, xr_, gs_, gr_, lsem,
):
    t, x, c, e = place()
    nx = n_tp // 2
    rows_all, width = tok.shape
    half = width // 2
    experts, slots = snd.shape[0], snd.shape[1]
    wl = wout.shape[0]
    heads = wl // HD
    blk = rows_all // 4
    mate = 2 * x + 1 - c
    x_peers = [2 * lax.rem(x + d, nx) + c for d in range(1, nx)]
    greet([(mate, e)] + [(p, e) for p in x_peers], lambda i: (t, lax.rem(e + 1 + i, n_ep)), n_ep - 1)

    hot = lax.broadcasted_iota(jnp.int32, (experts, rows_all), 0) == rts[...]
    hot_f = hot.astype(F32)
    hot_b = hot_f.astype(BF16)
    counts = jnp.zeros((experts, rows_all), F32)
    for k in range(4):
        earlier = (
            lax.broadcasted_iota(jnp.int32, (blk, rows_all), 0) + k * blk
            < lax.broadcasted_iota(jnp.int32, (blk, rows_all), 1)
        )
        counts = counts + mm(hot_b[:, k * blk : (k + 1) * blk], earlier.astype(F32).astype(BF16))
    rank = jnp.sum(counts * hot_f, axis=0, keepdims=True).astype(jnp.int32)
    limit = jnp.sum(jnp.where(hot, cap[...], 0), axis=0, keepdims=True)
    tgt = jnp.where(rank < limit, rts[...] * slots + rank, -1)
    tgt_o[...] = tgt
    tgtc_o[...] = jnp.broadcast_to(tgt.astype(F32), (8, rows_all)).T.astype(jnp.int32)

    my_half = pl.ds(pl.multiple_of(c * half, half), half)

    def rows_for(dest):
        hot_rows = onehot_rows(tgt_o[...], dest * slots, slots)
        return mm(hot_rows, cot[:, my_half]).astype(BF16)

    def a2a_copy(dest, src):
        return remote(snd.at[dest], crow_o.at[c, src], as_.at[dest], ar_.at[src], t, dest)

    def send_rows(i, carry):
        dest = lax.rem(e + 1 + i, n_ep)
        snd[dest] = rows_for(dest)
        a2a_copy(dest, e).start()
        return carry

    lax.fori_loop(0, n_ep - 1, send_rows, 0)
    snd[e] = rows_for(e)
    own = pltpu.make_async_copy(snd.at[e], crow_o.at[c, e], lsem)
    own.start()
    remote(snd.at[e], crow_o.at[c, e], fs_.at[e], fr_.at[e], mate, e).start()

    def project(i):
        rs = pl.ds(i * blk, blk)
        unit, _ = norm_rows(tok[rs, :].astype(F32))
        normed = (unit * g1[...] + b1[...]).astype(BF16)
        for j in range(3):
            qkv_o[j, rs, :] = mm(normed, wqkv[j]).astype(BF16)
        vt[:, rs] = qkv_o[2, rs, :].astype(F32).T.astype(BF16)

    def chunk(i):
        return pl.ds(i * blk, blk)

    other_half = pl.ds(pl.multiple_of((1 - c) * half, half), half)

    def core_copy(i):
        return remote(part.at[chunk(i), other_half], cbuf.at[chunk(i)], cs_.at[i], cr_.at[i], mate, e)

    def x_copy(i, d):
        return remote(
            xbuf.at[x, chunk(i)], xbuf.at[x, chunk(i)], xs_.at[i, d - 1], xr_.at[i, d - 1], x_peers[d - 1], e
        )

    def x_arrival(i, d):
        src = lax.rem(x + nx - d, nx)
        return remote(
            xbuf.at[src, chunk(i)], xbuf.at[src, chunk(i)], xs_.at[i, d - 1], xr_.at[i, d - 1], x_peers[d - 1], e
        )

    def share_copy(i):
        return remote(
            attn_o.at[chunk(i), my_half], attn_o.at[chunk(i), my_half], gs_.at[i], gr_.at[i], mate, e
        )

    def share_arrival(i):
        return remote(
            attn_o.at[chunk(i), other_half], attn_o.at[chunk(i), other_half], gs_.at[i], gr_.at[i], mate, e
        )

    def attend(i):
        keys = (i + 1) * blk
        ks = pl.ds(0, keys)
        allowed = (segc[ks, :] == segr[:, chunk(i)]) & (
            lax.broadcasted_iota(jnp.int32, (keys, blk), 0)
            <= lax.broadcasted_iota(jnp.int32, (keys, blk), 1) + i * blk
        )
        bias[ks, :] = jnp.where(allowed, 0.0, masked_value)
        head_of = lax.div(lax.broadcasted_iota(jnp.int32, (blk, wl), 1), HD)

        def one_head(h, carry):
            q_h = jnp.where(head_of == h, qkv_o[0, chunk(i), :].astype(F32) * 0.125, 0.0).astype(BF16)
            scores = mm_t(qkv_o[1, ks, :], q_h) + bias[ks, :]
            top = jnp.max(scores, axis=0, keepdims=True)
            weights = jnp.exp(scores - top)
            mass = jnp.sum(weights, axis=0, keepdims=True)
            lse_o[pl.ds(h, 1), chunk(i)] = top + jnp.log(mass)
            probs = (weights * (1.0 / mass)).astype(BF16)
            hs = pl.ds(pl.multiple_of(h * HD, HD), HD)
            ht_o[hs, chunk(i)] = mm(vt[hs, ks], probs).astype(BF16)
            return carry

        lax.fori_loop(0, heads, one_head, 0)
        part[chunk(i), :] = t_mm(ht_o[:, chunk(i)], wout[...]).astype(BF16)
        core_copy(i).start()

    def sum_cores(i):
        core_copy(i).wait_recv()
        both = part[chunk(i), my_half].astype(F32) + cbuf[chunk(i), :].astype(F32)
        xbuf[x, chunk(i), :] = both.astype(BF16)
        for d in range(1, nx):
            x_copy(i, d).start()

    def sum_chips(i):
        for d in range(1, nx):
            x_arrival(i, d).wait_recv()
        total = xbuf[0, chunk(i), :].astype(F32)
        for j in range(1, nx):
            total = total + xbuf[j, chunk(i), :].astype(F32)
        attn_o[chunk(i), my_half] = total.astype(BF16)
        share_copy(i).start()

    def finish(i):
        share_arrival(i).wait_recv()
        hidden = tok[chunk(i), :].astype(F32) + attn_o[chunk(i), :].astype(F32)
        unit, _ = norm_rows(hidden)
        normed = (unit * g2[...] + b2[...]).astype(BF16)
        n2_o[chunk(i), :] = normed
        logits = mm(normed, mixw[...])
        lane = lax.broadcasted_iota(jnp.int32, logits.shape, 1)
        logits = jnp.where(lane < 2, logits, masked_value)
        mix = jnp.exp(logits - jnp.max(logits, axis=1, keepdims=True))
        mix_o[chunk(i), :] = mix / jnp.sum(mix, axis=1, keepdims=True)

    for i in range(4):
        project(i)
        if i >= 1:
            sum_cores(i - 1)
        attend(i)
        if i >= 2:
            sum_chips(i - 2)
    sum_cores(3)

    def forward_rows(i, carry):
        src = lax.rem(e + n_ep - 1 - i, n_ep)
        a2a_copy(e, src).wait_recv()
        remote(crow_o.at[c, src], crow_o.at[c, src], fs_.at[src], fr_.at[src], mate, e).start()
        return carry

    def forward_done(src, carry):
        remote(crow_o.at[1 - c, src], crow_o.at[1 - c, src], fs_.at[src], fr_.at[src], mate, e).wait()
        return carry

    finish(0)
    sum_chips(2)
    finish(1)
    sum_chips(3)
    finish(2)
    finish(3)
    lax.fori_loop(0, n_ep - 1, forward_rows, 0)
    lax.fori_loop(0, n_ep, forward_done, 0)
    own.wait()

    def sent(i, carry):
        a2a_copy(lax.rem(e + 1 + i, n_ep), e).wait_send()
        return carry

    lax.fori_loop(0, n_ep - 1, sent, 0)
    for i in range(4):
        core_copy(i).wait_send()
        for d in range(1, nx):
            x_copy(i, d).wait_send()
        share_copy(i).wait_send()


def forward(tokens, cotangent, segments, routes, capacity, g1, b1, g2, b2, wqkv, wout, mix_weight):
    n_tp, n_ep = lax.axis_size("tp"), lax.axis_size("ep")
    rows, width = tokens.shape
    wl = wout.shape[0]
    experts = capacity.shape[0]
    slots = 3 * rows // (2 * experts)
    nx = n_tp // 2
    half = width // 2
    vm = pl.BlockSpec(memory_space=pltpu.VMEM)
    dma = pltpu.SemaphoreType.DMA
    shape = jax.ShapeDtypeStruct
    mixw = jnp.pad(mix_weight, ((0, 0), (0, 126)))
    return pl.pallas_call(
        functools.partial(forward_kernel, n_tp, n_ep),
        out_shape=(
            shape((3, rows, wl), BF16),
            shape((wl, rows), BF16),
            shape((wl // HD, rows), F32),
            shape((rows, width), BF16),
            shape((rows, width), BF16),
            shape((rows, 128), F32),
            shape((2, experts, slots, half), BF16),
            shape((1, rows), jnp.int32),
            shape((rows, 8), jnp.int32),
        ),
        in_specs=[vm] * 13,
        out_specs=(vm,) * 6 + (pl.BlockSpec(memory_space=pl.ANY), vm, vm),
        scratch_shapes=[
            pltpu.VMEM((wl, rows), BF16),
            pltpu.VMEM((experts, slots, half), BF16),
            pltpu.VMEM((rows, width), BF16),
            pltpu.VMEM((rows, half), BF16),
            pltpu.VMEM((nx, rows, half), BF16),
            pltpu.VMEM((rows, rows // 4), F32),
            dma((experts,)), dma((experts,)), dma((experts,)), dma((experts,)),
            dma((4,)), dma((4,)), dma((4, max(nx - 1, 1))), dma((4, max(nx - 1, 1))), dma((4,)), dma((4,)),
            dma,
        ],
        compiler_params=pltpu.CompilerParams(
            collective_id=0, has_side_effects=True, vmem_limit_bytes=VMEM_LIMIT
        ),
        cost_estimate=pl.CostEstimate(flops=8 * 10**9, bytes_accessed=30 * 10**6, transcendentals=0),
        name="attention_forward",
    )(
        tokens, cotangent, segments, segments.reshape(rows, 1), routes.reshape(1, rows),
        capacity.reshape(experts, 1), g1.reshape(1, width), b1.reshape(1, width), g2.reshape(1, width),
        b2.reshape(1, width), wqkv, wout, mixw,
    )


def gelu_pair(v):
    c0 = math.sqrt(2.0 / math.pi)
    sq = v * v
    th = jnp.tanh(c0 * v * (1.0 + 0.044715 * sq))
    half_up = 0.5 + 0.5 * th
    slope = half_up + (0.5 * c0) * v * (1.0 - th * th) * (1.0 + (3.0 * 0.044715) * sq)
    return v * half_up, slope


class TpReduce:
    def __init__(self, nx, bufs, sems, span):
        self.part, self.cbuf, self.xrcv = bufs
        self.cs, self.cr, self.xs, self.xr = sems
        self.nx, self.span = nx, span
        self.t, self.x, self.c, self.e = place()
        self.mate = 2 * self.x + 1 - self.c

    def core(self, i):
        return remote(
            self.part.at[1 - self.c, :, self.span(i)], self.cbuf.at[:, self.span(i)],
            self.cs.at[i], self.cr.at[i], self.mate, self.e,
        )

    def chip(self, i, d):
        there = lax.rem(self.x + d, self.nx)
        return remote(
            self.cbuf.at[there, self.span(i)], self.xrcv.at[self.x, self.span(i)],
            self.xs.at[i, d - 1], self.xr.at[i, d - 1], 2 * there + self.c, self.e,
        )

    def arrival(self, i, d):
        src = lax.rem(self.x + self.nx - d, self.nx)
        return remote(
            self.cbuf.at[src, self.span(i)], self.xrcv.at[src, self.span(i)],
            self.xs.at[i, d - 1], self.xr.at[i, d - 1], 2 * src + self.c, self.e,
        ), src

    def start(self, i):
        self.core(i).start()

    def sum_cores(self, i):
        self.core(i).wait_recv()
        s = self.span(i)
        for j in range(self.nx):
            self.cbuf[j, s, :] = (
                self.part[self.c, j, s, :].astype(F32) + self.cbuf[j, s, :].astype(F32)
            ).astype(BF16)
        for d in range(1, self.nx):
            self.chip(i, d).start()

    def total(self, i):
        s = self.span(i)
        total = self.cbuf[self.x, s, :].astype(F32)
        for d in range(1, self.nx):
            copy, src = self.arrival(i, d)
            copy.wait_recv()
            total = total + self.xrcv[src, s, :].astype(F32)
        return total

    def sent(self, i):
        self.core(i).wait_send()
        for d in range(1, self.nx):
            self.chip(i, d).wait_send()


def dense_kernel(
    n_tp, n_ep, n2, tgt, cot, mix, up, down, wdiff,
    rows_o, gup_o, gdown_o, y_o, gshare_o, gmix_o,
    snd, act, gpre, gden, part, cbuf, xrcv,
    as_, ar_, xs_, xr_, ms_, mr_, lsem, rcs, rcr, rxs, rxr,
):
    t, x, c, e = place()
    nx = n_tp // 2
    rows_all, width = n2.shape
    slots, share = snd.shape[1], snd.shape[2]
    units = up.shape[1]
    blk = rows_all // 4
    mate = 2 * x + 1 - c
    x_peers = [2 * lax.rem(x + d, nx) + c for d in range(1, nx)]
    greet([(mate, e)] + [(p, e) for p in x_peers], lambda i: (t, lax.rem(e + 1 + i, n_ep)), n_ep - 1)
    my_cols = pl.ds(pl.multiple_of(t * share, share), share)

    def rows_for(dest):
        return mm(onehot_rows(tgt[...], dest * slots, slots), n2[:, my_cols]).astype(BF16)

    def a2a_copy(dest, src):
        return remote(snd.at[dest], rows_o.at[t, src], as_.at[dest], ar_.at[src], t, dest)

    def send_rows(i, carry):
        dest = lax.rem(e + 1 + i, n_ep)
        snd[dest] = rows_for(dest)
        a2a_copy(dest, e).start()
        return carry

    def x_copy(here, src, d):
        return remote(here, rows_o.at[t, src], xs_.at[src, d - 1], xr_.at[src, d - 1], x_peers[d - 1], e)

    def mate_copy(here, xi, src):
        return remote(here, rows_o.at[2 * xi + c, src], ms_.at[xi, src], mr_.at[xi, src], mate, e)

    def spread(here, src):
        for d in range(1, nx):
            x_copy(here, src, d).start()
        mate_copy(here, x, src).start()

    lax.fori_loop(0, n_ep - 1, send_rows, 0)
    snd[e] = rows_for(e)
    own = pltpu.make_async_copy(snd.at[e], rows_o.at[t, e], lsem)
    own.start()
    spread(snd.at[e], e)

    def source(k):
        return lax.rem(e + n_ep - k, n_ep)

    def spread_block(k, carry):
        src = source(k)
        a2a_copy(e, src).wait_recv()
        spread(rows_o.at[t, src], src)
        return carry

    def pass_block(k, carry):
        src = source(k)
        for d in range(1, nx):
            xi = lax.rem(x + nx - d, nx)
            got = rows_o.at[2 * xi + c, src]
            remote(got, got, xs_.at[src, d - 1], xr_.at[src, d - 1], mate, e).wait_recv()
            mate_copy(got, xi, src).start()
        return carry

    def end_block(src, carry):
        for xi in range(nx):
            got = rows_o.at[2 * xi + 1 - c, src]
            remote(got, got, ms_.at[xi, src], mr_.at[xi, src], mate, e).wait()
        for d in range(1, nx):
            x_copy(rows_o.at[t, src], src, d).wait_send()
        return carry

    def chunk(i):
        return pl.ds(i * blk, blk)

    reduce = TpReduce(nx, (part, cbuf, xrcv), (rcs, rcr, rxs, rxr), chunk)
    fblk = min(256, units)
    steps = units // fblk

    def dense(i, tally):
        rs = chunk(i)
        mix0, mix1 = mix[rs, 0:1], mix[rs, 1:2]
        gden[rs, :] = (mix0 * cot[rs, :].astype(F32)).astype(BF16)

        def one(f, carry):
            fs = pl.ds(pl.multiple_of(f * fblk, fblk), fblk)
            value, slope = gelu_pair(mm(n2[rs, :], up[:, fs]))
            act[rs, fs] = value.astype(BF16)
            gpre[rs, fs] = (mm_t(gden[rs, :], down[fs, :]) * slope).astype(BF16)
            return carry

        lax.fori_loop(0, steps, one, 0)
        col0 = jnp.zeros((blk, 1), F32)
        for g in range(n_tp):
            gs = pl.ds(g * share, share)
            dense_part = mm(act[rs, :], down[:, gs])
            col0 = col0 + jnp.sum(dense_part * cot[rs, gs].astype(F32), axis=1, keepdims=True)
            y_o[g % 2, g // 2, rs, :] = (mix0 * dense_part).astype(BF16)
        logit = mix0 * mix1 * col0
        for g in range(n_tp):
            gs = pl.ds(g * share, share)
            back = mm_t(gpre[rs, :], up[gs, :]) + logit * wdiff[:, gs]
            part[g % 2, g // 2, rs, :] = back.astype(BF16)
        reduce.start(i)
        return tally + jnp.sum(logit * n2[rs, :].astype(F32), axis=0, keepdims=True)

    ends = [1 + (n_ep - 1) * k // 4 for k in range(5)]
    tally = dense(0, jnp.zeros((1, width), F32))
    lax.fori_loop(ends[0], ends[1], spread_block, 0)
    tally = dense(1, tally)
    reduce.sum_cores(0)
    pass_block(0, 0)
    lax.fori_loop(ends[1], ends[2], spread_block, 0)
    lax.fori_loop(ends[0], ends[1], pass_block, 0)
    tally = dense(2, tally)
    reduce.sum_cores(1)
    lax.fori_loop(ends[2], ends[3], spread_block, 0)
    lax.fori_loop(ends[1], ends[2], pass_block, 0)
    tally = dense(3, tally)
    reduce.sum_cores(2)
    lax.fori_loop(ends[3], ends[4], spread_block, 0)
    lax.fori_loop(ends[2], ends[3], pass_block, 0)
    reduce.sum_cores(3)
    gmix_o[...] = jnp.broadcast_to(tally, gmix_o.shape)
    for k in range(steps):
        fs = pl.ds(k * fblk, fblk)
        gdown_o[fs, :] = t_mm(act[:, fs], gden[...]).astype(BF16)
    for k in range(4):
        ws = pl.ds(k * (width // 4), width // 4)
        gup_o[ws, :] = t_mm(n2[:, ws], gpre[...]).astype(BF16)
    lax.fori_loop(ends[3], ends[4], pass_block, 0)
    for i in range(4):
        gshare_o[chunk(i), :] = reduce.total(i)
    lax.fori_loop(0, n_ep, end_block, 0)
    own.wait()

    def sent(i, carry):
        a2a_copy(lax.rem(e + 1 + i, n_ep), e).wait_send()
        return carry

    lax.fori_loop(0, n_ep - 1, sent, 0)
    for i in range(4):
        reduce.sent(i)


def dense_block(n2, targets, cotangent, mix, up, down, wdiff, experts):
    n_tp, n_ep = lax.axis_size("tp"), lax.axis_size("ep")
    rows, width = n2.shape
    slots = 3 * rows // (2 * experts)
    units = up.shape[1]
    nx, share = n_tp // 2, width // n_tp
    dx = max(nx - 1, 1)
    vm = pl.BlockSpec(memory_space=pltpu.VMEM)
    dma = pltpu.SemaphoreType.DMA
    shape = jax.ShapeDtypeStruct
    return pl.pallas_call(
        functools.partial(dense_kernel, n_tp, n_ep),
        out_shape=(
            shape((n_tp, experts, slots, share), BF16),
            shape((width, units), BF16),
            shape((units, width), BF16),
            shape((2, nx, rows, share), BF16),
            shape((rows, share), F32),
            shape((8, width), F32),
        ),
        in_specs=[vm] * 7,
        out_specs=(pl.BlockSpec(memory_space=pl.ANY),) + (vm,) * 5,
        scratch_shapes=[
            pltpu.VMEM((experts, slots, share), BF16),
            pltpu.VMEM((rows, units), BF16),
            pltpu.VMEM((rows, units), BF16),
            pltpu.VMEM((rows, width), BF16),
            pltpu.VMEM((2, nx, rows, share), BF16),
            pltpu.VMEM((nx, rows, share), BF16),
            pltpu.VMEM((nx, rows, share), BF16),
            dma((experts,)), dma((experts,)), dma((experts, dx)), dma((experts, dx)),
            dma((nx, experts)), dma((nx, experts)), dma,
            dma((4,)), dma((4,)), dma((4, dx)), dma((4, dx)),
        ],
        compiler_params=pltpu.CompilerParams(
            collective_id=1, has_side_effects=True, vmem_limit_bytes=VMEM_LIMIT
        ),
        cost_estimate=pl.CostEstimate(flops=16 * 10**9, bytes_accessed=30 * 10**6, transcendentals=0),
        name="dense_and_dispatch",
    )(n2, targets, cotangent, mix, up, down, wdiff)


class EpBits:
    def __init__(self, first, rows, order, sems, base):
        self.first, self.rows, self.order, self.base = first, rows, order, base
        self.ss, self.rs = sems
        self.t, self.x, self.c, self.e = place()
        self.low = [0]
        for s, b in enumerate(order):
            self.low.append(self.low[-1] + self.bit(b) * (rows >> (s + 1)))

    def bit(self, b):
        return lax.rem(lax.div(self.e, 2**b), 2)

    def cut(self, low, size):
        return pl.ds(pl.multiple_of(self.first + low, 16), size)

    def size(self, s):
        return self.rows >> (s + 1)

    def landing(self, s):
        return self.first + self.rows - (self.rows >> s)

    def move(self, src, dst, s):
        b = self.order[s]
        partner = self.e + (1 - 2 * self.bit(b)) * 2**b
        return remote(src, dst, self.ss.at[self.base, s], self.rs.at[self.base, s], self.t, partner)


class EpSum(EpBits):
    def __init__(self, data, land, first, rows, order, sems, base):
        super().__init__(first, rows, order, sems, base)
        self.data, self.land = data, land

    def half(self, s, keep):
        size, bit = self.size(s), self.bit(self.order[s])
        which = bit if keep else 1 - bit
        if s == 0:
            return self.data.at[self.cut(which * size, size)]
        return self.land.at[pl.ds(pl.multiple_of(self.landing(s - 1) + which * size, 16), size)]

    def out(self, s):
        return self.move(self.half(s, False), self.land.at[pl.ds(self.landing(s), self.size(s))], s)

    def start(self, s):
        self.out(s).start()

    def add(self, s):
        self.out(s).wait_recv()
        spot = pl.ds(self.landing(s), self.size(s))
        self.land[spot, :] = (self.land[spot, :].astype(F32) + self.half(s, True)[...].astype(F32)).astype(BF16)

    def result(self):
        last = len(self.order) - 1
        return self.land[pl.ds(self.landing(last), self.size(last)), :]

    def sent(self):
        for s in range(len(self.order)):
            self.out(s).wait_send()


class EpGather(EpBits):
    def __init__(self, full, first, rows, order, sems, base):
        super().__init__(first, rows, order, sems, base)
        self.full = full

    def part(self, s, other):
        size, bit = self.size(s), self.bit(self.order[s])
        return self.full.at[self.cut(self.low[s] + ((1 - bit) if other else bit) * size, size)]

    def own(self):
        return self.part(len(self.order) - 1, False)

    def give(self, s, src=None):
        part = self.part(s, False)
        self.move(part if src is None else src, part, s).start()

    def take(self, s):
        part = self.part(s, True)
        self.move(part, part, s).wait_recv()

    def sent(self):
        for s in range(len(self.order)):
            part = self.part(s, False)
            self.move(part, part, s).wait_send()


def ep_cuts(rows, n_ep):
    return max(q for q in (4, 2, 1) if q == 1 or rows % (16 * q * n_ep) == 0)


def piece_orders(cuts, n_ep):
    natural = list(range(n_ep.bit_length() - 1))
    turned = [natural[1], natural[0]] + natural[2:]
    return [turned if 4 * k >= 3 * cuts and cuts > 1 else natural for k in range(cuts)]


class Slots:
    def __init__(self):
        self.lists, self.at = {}, 0

    def put(self, slot, action):
        self.lists.setdefault(slot, []).append(action)

    def run(self, slot):
        for action in self.lists.get(slot, []):
            action()

    def next(self, count=1):
        for _ in range(count):
            self.run(self.at)
            self.at += 1

    def rest(self):
        for slot in sorted(self.lists):
            if slot >= self.at:
                self.run(slot)
        self.at = 1 + max(self.lists, default=-1)


def plan_sum(slots, piece, first, bits, lag=2, stride=1):
    def step(s):
        piece.add(s)
        if s + 1 < bits:
            piece.start(s + 1)

    slots.put(first, lambda: piece.start(0))
    for s in range(bits):
        slots.put(first + lag + stride * s, lambda s=s: step(s))


def plan_gather(slots, piece, own, sem, first, bits):
    piece.give(bits - 1, own)
    pltpu.make_async_copy(own, piece.own(), sem).start()

    def step(s):
        if s == bits - 1:
            pltpu.make_async_copy(own, piece.own(), sem).wait()
        piece.take(s)
        if s > 0:
            piece.give(s - 1)

    for s in range(bits - 1, -1, -1):
        slots.put(first + 2 * (bits - 1 - s) if s else 99, lambda s=s: step(s))


def expert_kernel(
    n_tp, n_ep, rows, crow, eup, edown, mixw, wdiff, gshare, tgtc, gup,
    geup_o, gedown_o, gsec_o, gmix_o, oshare_o, sup_o,
    act, gpre, grow, part, cbuf, xrcv, rsnd, ret, ypart, ybuf, yxrcv, ysnd, yret, uland,
    rcs, rcr, rxs, rxr, as_, ar_, lsem,
    ycs, ycr, yxs, yxr, ys_, yr_, ylsem, uss, urs,
):
    t, x, c, e = place()
    nx = n_tp // 2
    experts, slots, share = rows.shape[1:]
    total_rows = experts * slots
    half = crow.shape[3]
    width = 2 * half
    units = eup.shape[1]
    nb = experts // 4
    size = nb * slots
    tok_rows = tgtc.shape[0]
    blk = tok_rows // 4
    mate = 2 * x + 1 - c
    x_peers = [2 * lax.rem(x + d, nx) + c for d in range(1, nx)]
    greet([(mate, e)] + [(p, e) for p in x_peers], lambda i: (t, lax.rem(e + 1 + i, n_ep)), n_ep - 1)

    def piece(i):
        return lax.rem(lax.div(e, nb) + 1 + i, 4)

    def span(i):
        return pl.ds(pl.multiple_of(piece(i) * size, size), size)

    def chunk(i):
        return pl.ds(i * blk, blk)

    reduce = TpReduce(nx, (part, cbuf, xrcv), (rcs, rcr, rxs, rxr), span)
    reduce_y = TpReduce(nx, (ypart, ybuf, yxrcv), (ycs, ycr, yxs, yxr), span)
    back = EpReturn(rsnd, ret, slots, (as_, ar_, lsem))
    back_y = EpReturn(ysnd, yret, slots, (ys_, yr_, ylsem))
    bits = n_ep.bit_length() - 1
    up_cuts = sup_o.shape[0]
    up_rows = gup.shape[0] // up_cuts
    orders = piece_orders(up_cuts, n_ep)
    sums = [EpSum(gup, uland, k * up_rows, up_rows, orders[k], (uss, urs), k) for k in range(up_cuts)]
    slots_ = Slots()
    for k, one_sum in enumerate(sums):
        first, lag, stride = ((0, 3, 1), (0, 4, 1), (1, 4, 1), (1, 3, 2))[k]
        plan_sum(slots_, one_sum, first, bits, lag, stride)
    fblk = min(256, units)
    steps = units // fblk
    gmix_o[...] = jnp.zeros_like(gmix_o)
    slots_.next(2)

    def work(i):
        bs = pl.ds(piece(i) * nb, nb)
        rs = span(i)

        def share_rows(g):
            return rows[g, bs].reshape(size, share)

        logits = jnp.zeros((size, 128), F32)
        for g in range(n_tp):
            logits = logits + mm(share_rows(g), mixw[pl.ds(g * share, share), :])
        lane = lax.broadcasted_iota(jnp.int32, logits.shape, 1)
        logits = jnp.where(lane < 2, logits, masked_value)
        mix = jnp.exp(logits - jnp.max(logits, axis=1, keepdims=True))
        mix = mix / jnp.sum(mix, axis=1, keepdims=True)
        mix0, mix1 = mix[:, 0:1], mix[:, 1:2]
        for h in range(2):
            grow[rs, pl.ds(h * half, half)] = (mix1 * crow[h, bs].reshape(size, half).astype(F32)).astype(BF16)

        def one(f, carry):
            fs = pl.ds(pl.multiple_of(f * fblk, fblk), fblk)
            pre = mm(share_rows(0), eup[pl.ds(0, share), fs])
            for g in range(1, n_tp):
                pre = pre + mm(share_rows(g), eup[pl.ds(g * share, share), fs])
            value, slope = gelu_pair(pre)
            act[rs, fs] = value.astype(BF16)
            gpre[rs, fs] = (mm_t(grow[rs, :], edown[fs, :]) * slope).astype(BF16)
            return carry

        lax.fori_loop(0, steps, one, 0)
        col1 = jnp.zeros((size, 1), F32)
        per_half = n_tp // 2
        for g in range(n_tp):
            gs = pl.ds(g * share, share)
            eout = mm(act[rs, :], edown[:, gs])
            cots = crow[g // per_half, bs, :, pl.ds((g % per_half) * share, share)].reshape(size, share)
            col1 = col1 + jnp.sum(eout * cots.astype(F32), axis=1, keepdims=True)
            ypart[g % 2, g // 2, rs, :] = (mix1 * eout).astype(BF16)
        logit = -(mix0 * mix1 * col1)
        for g in range(n_tp):
            gs = pl.ds(g * share, share)
            grad_in = mm_t(gpre[rs, :], eup[gs, :]) + logit * wdiff[:, gs]
            part[g % 2, g // 2, rs, :] = grad_in.astype(BF16)
            tally = jnp.sum(logit * share_rows(g).astype(F32), axis=0, keepdims=True)
            gmix_o[:, gs] = gmix_o[:, gs] + jnp.broadcast_to(tally, (8, share))
        reduce.start(i)
        reduce_y.start(i)

    def send_back(i):
        rsnd[span(i), :] = reduce.total(i).astype(BF16)
        back.send(piece(i) * nb, nb)

    def send_back_y(i):
        ysnd[span(i), :] = reduce_y.total(i).astype(BF16)
        back_y.send(piece(i) * nb, nb)

    def step(i, carry):
        work(i)

        @pl.when(i >= 1)
        def _():
            reduce.sum_cores(i - 1)

        @pl.when(i >= 2)
        def _():
            reduce_y.sum_cores(i - 2)
            send_back(i - 2)

        for j in range(4):

            @pl.when(i == j)
            def _():
                slots_.run(2 + j)

        return carry

    lax.fori_loop(0, 4, step, 0)
    slots_.at = 6
    reduce.sum_cores(3)
    reduce_y.sum_cores(2)
    slots_.next()

    def down_grad(k):
        fs = pl.ds(k * fblk, fblk)
        gedown_o[fs, :] = t_mm(act[:, fs], grow[...])

    def up_grad(g):
        geup_o[pl.ds(g * share, share), :] = t_mm(rows[g].reshape(total_rows, share), gpre[...])

    send_back_y(0)
    for k in range(steps // 2):
        down_grad(k)
    send_back(2)
    slots_.next()
    for k in range(steps // 2, steps):
        down_grad(k)
    send_back(3)
    reduce_y.sum_cores(3)
    send_back_y(1)
    slots_.next()
    up_grad(0)
    send_back_y(2)
    for g in range(1, n_tp // 2):
        up_grad(g)
    slots_.next()

    def hot_rows(i):
        ids = lax.broadcasted_iota(jnp.int32, (blk, total_rows), 1)
        return (ids == tgtc[chunk(i), 0:1]).astype(F32).astype(BF16)

    back.arrived(n_ep)
    for i in range(4):
        gsec_o[chunk(i), :] = (gshare[chunk(i), :] + mm(hot_rows(i), ret[...])).astype(BF16)
    send_back_y(3)
    slots_.next()
    for g in range(n_tp // 2, n_tp):
        up_grad(g)
    slots_.rest()
    for k in range(up_cuts):
        sup_o[k] = sums[k].result()
    back_y.arrived(n_ep)
    for i in range(4):
        oshare_o[chunk(i), :] = mm(hot_rows(i), yret[...])
    back.sent(n_ep)
    back_y.sent(n_ep)
    for i in range(4):
        reduce.sent(i)
        reduce_y.sent(i)
    for one_sum in sums:
        one_sum.sent()


class EpReturn:
    def __init__(self, snd, ret, slots, sems):
        self.snd, self.ret, self.slots = snd, ret, slots
        self.ss, self.rs, self.local = sems
        self.t, self.x, self.c, self.e = place()

    def block(self, k):
        return pl.ds(pl.multiple_of(k * self.slots, self.slots), self.slots)

    def copy(self, dest, src):
        return remote(
            self.snd.at[self.block(dest)], self.ret.at[self.block(src)], self.ss.at[dest], self.rs.at[src], self.t, dest
        )

    def own(self):
        mine = self.block(self.e)
        return pltpu.make_async_copy(self.snd.at[mine], self.ret.at[mine], self.local)

    def send(self, first, count):
        def one(k, carry):
            dest = first + k

            @pl.when(dest != self.e)
            def _():
                self.copy(dest, self.e).start()

            @pl.when(dest == self.e)
            def _():
                self.own().start()

            return carry

        lax.fori_loop(0, count, one, 0)

    def arrived(self, n_ep):
        def one(k, carry):
            self.copy(self.e, lax.rem(self.e + n_ep - k, n_ep)).wait_recv()
            return carry

        lax.fori_loop(1, n_ep, one, 0)
        self.own().wait()

    def sent(self, n_ep):
        def one(k, carry):
            self.copy(lax.rem(self.e + k, n_ep), self.e).wait_send()
            return carry

        lax.fori_loop(1, n_ep, one, 0)


class TpGather:
    def __init__(self, nx, full, share, blk, sems):
        self.full, self.share, self.blk, self.nx = full, share, blk, nx
        self.xs, self.xr, self.ms, self.mr = sems
        self.t, self.x, self.c, self.e = place()
        self.mate = 2 * self.x + 1 - self.c

    def cut(self, i, g):
        return self.full.at[
            pl.ds(i * self.blk, self.blk), pl.ds(pl.multiple_of(g * self.share, self.share), self.share)
        ]

    def across(self, i, d):
        there = 2 * lax.rem(self.x + d, self.nx) + self.c
        mine = self.cut(i, self.t)
        return remote(mine, mine, self.xs.at[i, d - 1], self.xr.at[i, d - 1], there, self.e)

    def beside(self, i, xi, c):
        got = self.cut(i, 2 * xi + c)
        return remote(got, got, self.ms.at[i, xi], self.mr.at[i, xi], self.mate, self.e)

    def put(self, i, value):
        cols = pl.ds(pl.multiple_of(self.t * self.share, self.share), self.share)
        self.full[pl.ds(i * self.blk, self.blk), cols] = value
        for d in range(1, self.nx):
            self.across(i, d).start()
        self.beside(i, self.x, self.c).start()

    def pass_on(self, i):
        for d in range(1, self.nx):
            xi = lax.rem(self.x + self.nx - d, self.nx)
            got = self.cut(i, 2 * xi + self.c)
            remote(got, got, self.xs.at[i, d - 1], self.xr.at[i, d - 1], self.mate, self.e).wait_recv()
            self.beside(i, xi, self.c).start()

    def finish(self, i):
        for xi in range(self.nx):
            self.beside(i, xi, 1 - self.c).wait_recv()
            self.beside(i, xi, self.c).wait_send()
        for d in range(1, self.nx):
            self.across(i, d).wait_send()


def expert_block(rows, cot_rows, eup, edown, mix_weight, wdiff, gshare, targets_col, gup):
    n_tp, n_ep = lax.axis_size("tp"), lax.axis_size("ep")
    _, experts, slots, share = rows.shape
    tok_rows = targets_col.shape[0]
    width, units = eup.shape
    nx = n_tp // 2
    dx = max(nx - 1, 1)
    total = experts * slots
    bits = n_ep.bit_length() - 1
    up_cuts = ep_cuts(width, n_ep)
    vm = pl.BlockSpec(memory_space=pltpu.VMEM)
    dma = pltpu.SemaphoreType.DMA
    shape = jax.ShapeDtypeStruct
    mixw = jnp.pad(mix_weight, ((0, 0), (0, 126)))
    return pl.pallas_call(
        functools.partial(expert_kernel, n_tp, n_ep),
        out_shape=(
            shape((width, units), F32),
            shape((units, width), F32),
            shape((tok_rows, share), BF16),
            shape((8, width), F32),
            shape((tok_rows, share), F32),
            shape((up_cuts, width // up_cuts // n_ep, units), BF16),
        ),
        in_specs=[vm] * 9,
        out_specs=(vm,) * 6,
        scratch_shapes=[
            pltpu.VMEM((total, units), BF16),
            pltpu.VMEM((total, units), BF16),
            pltpu.VMEM((total, width), BF16),
            pltpu.VMEM((2, nx, total, share), BF16),
            pltpu.VMEM((nx, total, share), BF16),
            pltpu.VMEM((nx, total, share), BF16),
            pltpu.VMEM((total, share), BF16),
            pltpu.VMEM((total, share), BF16),
            pltpu.VMEM((2, nx, total, share), BF16),
            pltpu.VMEM((nx, total, share), BF16),
            pltpu.VMEM((nx, total, share), BF16),
            pltpu.VMEM((total, share), BF16),
            pltpu.VMEM((total, share), BF16),
            pltpu.VMEM((width, units), BF16),
            dma((4,)), dma((4,)), dma((4, dx)), dma((4, dx)),
            dma((experts,)), dma((experts,)), dma,
            dma((4,)), dma((4,)), dma((4, dx)), dma((4, dx)),
            dma((experts,)), dma((experts,)), dma,
            dma((up_cuts, bits)), dma((up_cuts, bits)),
        ],
        compiler_params=pltpu.CompilerParams(
            collective_id=2, has_side_effects=True, vmem_limit_bytes=VMEM_LIMIT + 3 * 2**20
        ),
        cost_estimate=pl.CostEstimate(flops=24 * 10**9, bytes_accessed=50 * 10**6, transcendentals=0),
        name="experts",
    )(rows, cot_rows, eup, edown, mixw, wdiff, gshare, targets_col, gup)


class TpSum:
    def __init__(self, nx, full, bufs, sems, blk):
        self.full, self.blk, self.nx = full, blk, nx
        self.part, self.cbuf, self.xbuf = bufs
        self.cs, self.cr, self.xs, self.xr, self.gs, self.gr = sems
        self.t, self.x, self.c, self.e = place()
        self.mate = 2 * self.x + 1 - self.c
        half = self.cbuf.shape[1]
        self.mine = pl.ds(pl.multiple_of(self.c * half, half), half)
        self.other = pl.ds(pl.multiple_of((1 - self.c) * half, half), half)

    def span(self, i):
        return pl.ds(i * self.blk, self.blk)

    def core(self, i):
        return remote(
            self.part.at[self.span(i), self.other], self.cbuf.at[self.span(i)], self.cs.at[i], self.cr.at[i],
            self.mate, self.e,
        )

    def chip(self, i, d):
        there = 2 * lax.rem(self.x + d, self.nx) + self.c
        mine = self.xbuf.at[self.x, self.span(i)]
        return remote(mine, mine, self.xs.at[i, d - 1], self.xr.at[i, d - 1], there, self.e)

    def start(self, i):
        self.core(i).start()

    def sum_cores(self, i):
        self.core(i).wait_recv()
        both = self.part[self.span(i), self.mine].astype(F32) + self.cbuf[self.span(i), :].astype(F32)
        self.xbuf[self.x, self.span(i), :] = both.astype(BF16)
        for d in range(1, self.nx):
            self.chip(i, d).start()

    def share(self, i, cols):
        got = self.full.at[self.span(i), cols]
        return remote(got, got, self.gs.at[i], self.gr.at[i], self.mate, self.e)

    def sum_chips(self, i):
        for d in range(1, self.nx):
            src = lax.rem(self.x + self.nx - d, self.nx)
            got = self.xbuf.at[src, self.span(i)]
            remote(got, got, self.xs.at[i, d - 1], self.xr.at[i, d - 1], self.mate, self.e).wait_recv()
        total = self.xbuf[0, self.span(i), :].astype(F32)
        for j in range(1, self.nx):
            total = total + self.xbuf[j, self.span(i), :].astype(F32)
        self.full[self.span(i), self.mine] = total.astype(BF16)
        self.share(i, self.mine).start()

    def wait(self, i):
        self.share(i, self.other).wait_recv()
        self.share(i, self.mine).wait_send()

    def sent(self, i):
        self.core(i).wait_send()
        for d in range(1, self.nx):
            self.chip(i, d).wait_send()


def backward_kernel(
    n_tp, n_ep, tok, cot, attn, gshare, qkv, ht, lse, wqkv, wout, g1, b1, g2, segr, segc, oshare, sup, y, gdown,
    out_o, gh, part, wdat, small, gup_o, sdown_o,
    ga, gheads, kt, dqt, pcat, dcat, gcat, qcat, dk, dv, gj, bias,
    gsec, dbuf, dxrcv, dland,
    oxs, oxr, oms, omr, hxs, hxr, hms, hmr, uss, urs, usem, dcs, dcr, dxs, dxr, dss, drs,
):
    t, x, c, e = place()
    nx = n_tp // 2
    rows_all, width = tok.shape
    wl = wout.shape[0]
    heads = wl // HD
    blk = rows_all // 4
    share = oshare.shape[1]
    bits = n_ep.bit_length() - 1
    greet(
        [(2 * x + 1 - c, e)] + [(2 * lax.rem(x + d, nx) + c, e) for d in range(1, nx)],
        lambda i: (t, lax.rem(e + 1 + i, n_ep)),
        n_ep - 1,
    )

    def chunk(i):
        return pl.ds(i * blk, blk)

    gather = TpGather(nx, out_o, share, blk, (oxs, oxr, oms, omr))
    gather_g = TpGather(nx, gsec, share, blk, (hxs, hxr, hms, hmr))
    for i in (3, 2, 1, 0):
        gather_g.put(i, gshare[chunk(i), :])
    group = pcat.shape[1] // blk
    gw = group * HD
    up_cuts = sup.shape[0]
    up_rows = gup_o.shape[0] // up_cuts
    orders = piece_orders(up_cuts, n_ep)
    wide = [EpGather(gup_o, k * up_rows, up_rows, orders[k], (uss, urs), k) for k in range(up_cuts)]
    slots_ = Slots()
    for k, one in enumerate(wide):
        plan_gather(slots_, one, sup.at[k], usem.at[k], k + 1, bits)
    reduce_d = TpReduce(nx, (y, dbuf, dxrcv), (dcs, dcr, dxs, dxr), chunk)
    for i in range(4):
        reduce_d.start(i)
    down_cuts = sdown_o.shape[0]
    down_rows = gdown.shape[0] // down_cuts
    down_orders = piece_orders(down_cuts, n_ep)
    downs = [EpSum(gdown, dland, k * down_rows, down_rows, down_orders[k], (dss, drs), k) for k in range(down_cuts)]
    for k, one in enumerate(downs):
        plan_sum(slots_, one, 0, bits, 1 + 2 * k + k // 3, 2)
    slots_.next()
    my_cols = pl.ds(pl.multiple_of(t * share, share), share)

    def put_output(i):
        rs = chunk(i)
        hidden = tok[rs, my_cols].astype(F32) + attn[rs, my_cols].astype(F32)
        gather.put(i, (hidden + oshare[rs, :] + reduce_d.total(i)).astype(BF16))

    sum_gain = jnp.zeros((1, width), F32)
    sum_bias = jnp.zeros((1, width), F32)
    gather_g.pass_on(3)
    for i in (3, 2, 1, 0):
        rs = chunk(i)
        if i > 0:
            gather_g.pass_on(i - 1)
        gather_g.finish(i)
        unit, spread = norm_rows(tok[rs, :].astype(F32) + attn[rs, :].astype(F32))
        up = gsec[rs, :].astype(F32)
        sum_gain = sum_gain + jnp.sum(up * unit, axis=0, keepdims=True)
        sum_bias = sum_bias + jnp.sum(up, axis=0, keepdims=True)
        gv = up * g2[...]
        inner = gv - jnp.mean(gv, axis=-1, keepdims=True) - unit * jnp.mean(gv * unit, axis=-1, keepdims=True)
        grad = cot[rs, :].astype(F32) + spread * inner
        gh[rs, :] = grad
        ga[rs, :] = grad.astype(BF16)
        gheads[rs, :] = mm_t(ga[rs, :], wout[...]).astype(BF16)
        reduce_d.sum_cores(i)
        slots_.next()
    small[...] = jnp.zeros_like(small)
    small[2:3, :] = sum_gain
    small[3:4, :] = sum_bias
    wdat[pl.ds(0, wl), :] = mm(ht[...], ga[...]).astype(BF16)
    for i in range(4):
        rs = chunk(i)
        unit, _ = norm_rows(tok[rs, :].astype(F32))
        ga[rs, :] = (unit * g1[...] + b1[...]).astype(BF16)
        kt[:, rs] = qkv[1, rs, :].astype(F32).T.astype(BF16)

    head_of = lax.div(lax.broadcasted_iota(jnp.int32, (blk, gw), 1), HD)

    def attend(i, first, last):
        keys = (i + 1) * blk
        ks = pl.ds(0, keys)
        hc = pl.ds(first * HD, gw)
        allowed = (segc[ks, :] == segr[:, chunk(i)]) & (
            lax.broadcasted_iota(jnp.int32, (keys, blk), 0)
            <= lax.broadcasted_iota(jnp.int32, (keys, blk), 1) + i * blk
        )
        bias[ks, :] = jnp.where(allowed, 0.0, masked_value)

        def one_head(k, carry):
            h = first + k
            q_h = jnp.where(head_of == k, qkv[0, chunk(i), hc].astype(F32) * 0.125, 0.0).astype(BF16)
            g_h = jnp.where(head_of == k, gheads[chunk(i), hc].astype(F32), 0.0).astype(BF16)
            hb = pl.ds(pl.multiple_of(k * blk, blk), blk)
            gcat[hb, :] = g_h
            qcat[hb, :] = q_h
            probs = jnp.exp(mm_t(qkv[1, ks, hc], q_h) + bias[ks, :] - lse[pl.ds(h, 1), chunk(i)])
            pcat[ks, hb] = probs.astype(BF16)
            grad = mm_t(qkv[2, ks, hc], g_h)
            mean = jnp.sum(probs * grad, axis=0, keepdims=True)
            scores = (probs * (grad - mean)).astype(BF16)
            dcat[ks, hb] = scores
            dqt[pl.ds(pl.multiple_of(k * HD, HD), HD), :] = mm(
                kt[pl.ds(pl.multiple_of(h * HD, HD), HD), ks], scores
            )
            return carry

        lax.fori_loop(0, group, one_head, 0)
        dv_new, dk_new = mm(pcat[ks, :], gcat[...]), mm(dcat[ks, :], qcat[...])
        if i == 3:
            dv[ks, :] = dv_new
            dk[ks, :] = dk_new
        else:
            dv[ks, :] = dv[ks, :] + dv_new
            dk[ks, :] = dk[ks, :] + dk_new
        gj[0, chunk(i), hc] = (dqt[...].T * 0.125).astype(BF16)
        gj[1, chunk(i), hc] = dk[chunk(i), :].astype(BF16)
        gj[2, chunk(i), hc] = dv[chunk(i), :].astype(BF16)
        if last:
            grad_in = mm_t(gj[0, chunk(i), :], wqkv[0])
            for j in range(1, 3):
                grad_in = grad_in + mm_t(gj[j, chunk(i), :], wqkv[j])
            part[chunk(i), :] = grad_in.astype(BF16)

    def weight_grads(first):
        for j in range(3):
            row = wl + j * wl + first * HD
            wdat[pl.ds(row, gw), :] = t_mm(gj[j, :, pl.ds(first * HD, gw)], ga[...]).astype(BF16)

    groups = list(range(0, heads, group))
    for first in groups:
        last = first == groups[-1]
        for i in (3, 2, 1, 0):
            attend(i, first, last)
            slots_.next()
            if first == 0 and i == 3:
                for k in (3, 2, 1, 0):
                    put_output(k)
            if last and i == 1:
                for k in (3, 2, 1, 0):
                    gather.pass_on(k)
        weight_grads(first)
    slots_.rest()
    for i in range(4):
        gather.finish(i)
    for k in range(down_cuts):
        sdown_o[k] = downs[k].result()
    for one in wide + downs:
        one.sent()
    for i in range(4):
        reduce_d.sent(i)


def finish_kernel(
    n_tp, n_ep, tok, gh, part, g1, first_sums, gmix, wpart, sdown,
    gtok_o, small_o, wsum_o, gdown_o,
    cbuf, xbuf, small, sland, mland, wland,
    wss, wrs, wgs, wgr, dss, drs, dsem, tcs, tcr, txs, txr, tgs, tgr, ss_, sr_, mgs, mgr,
):
    t, x, c, e = place()
    nx = n_tp // 2
    rows_all, width = tok.shape
    blk = rows_all // 4
    greet(
        [(lax.rem(t + d, n_tp), e) for d in range(1, n_tp)], lambda i: (t, lax.rem(e + 1 + i, n_ep)), n_ep - 1
    )

    def chunk(i):
        return pl.ds(i * blk, blk)

    tp_sum = TpSum(nx, gtok_o, (part, cbuf, xbuf), (tcs, tcr, txs, txr, tgs, tgr), blk)
    for i in range(4):
        tp_sum.start(i)

    def mix_copy(d):
        return remote(gmix, mland.at[t], mgs.at[d - 1], mgr.at[d - 1], lax.rem(t + d, n_tp), e)

    mland[t] = gmix[...]
    for d in range(1, n_tp):
        mix_copy(d).start()
    small[...] = first_sums[...]
    bits = n_ep.bit_length() - 1
    cuts = wss.shape[0]
    cut_rows = wpart.shape[0] // cuts
    orders = piece_orders(cuts, n_ep)
    sums = [EpSum(wpart, wland, k * cut_rows, cut_rows, orders[k], (wss, wrs), k) for k in range(cuts)]
    gathers = [EpGather(wsum_o, k * cut_rows, cut_rows, orders[k], (wgs, wgr), k) for k in range(cuts)]
    down_cuts = sdown.shape[0]
    down_rows = gdown_o.shape[0] // down_cuts
    down_orders = piece_orders(down_cuts, n_ep)
    wide = [EpGather(gdown_o, k * down_rows, down_rows, down_orders[k], (dss, drs), k) for k in range(down_cuts)]
    slots_ = Slots()
    for one_sum in sums:
        one_sum.start(0)
    for k, one in enumerate(wide):
        plan_gather(slots_, one, sdown.at[k], dsem.at[k], k + 1, bits)
    for i in range(4):
        tp_sum.sum_cores(i)

    tally = [jnp.zeros((1, width), F32), jnp.zeros((1, width), F32)]

    def finish(i):
        rs = chunk(i)
        tp_sum.wait(i)
        unit, spread = norm_rows(tok[rs, :].astype(F32))
        up = gtok_o[rs, :].astype(F32)
        tally[0] = tally[0] + jnp.sum(up * unit, axis=0, keepdims=True)
        tally[1] = tally[1] + jnp.sum(up, axis=0, keepdims=True)
        gv = up * g1[...]
        inner = gv - jnp.mean(gv, axis=-1, keepdims=True) - unit * jnp.mean(gv * unit, axis=-1, keepdims=True)
        gtok_o[rs, :] = (gh[rs, :] + spread * inner).astype(BF16)

    def step(k, stage):
        if stage < bits:
            sums[k].add(stage)
            if stage + 1 < bits:
                sums[k].start(stage + 1)
            else:
                gathers[k].own()[...] = sums[k].result()
                gathers[k].give(stage)
        else:
            s = 2 * bits - 1 - stage
            gathers[k].take(s)
            if s > 0:
                gathers[k].give(s - 1)

    beats = [[] for _ in range(cuts + 4 * bits)]
    for k in range(cuts):
        for stage in range(2 * bits - 1):
            beats[k + 1 + 2 * stage].append((stage, k))
    beats = [sorted(b, reverse=True) for b in beats if b]
    apart = max(len(beats) // 8, 1)
    for n, beat in enumerate(beats):
        for stage, k in beat:
            step(k, stage)
        slots_.next()
        at = n // apart
        if n % apart == 0 and at < 4:
            tp_sum.sum_chips(at)
        if n % apart == 0 and 1 <= at < 5:
            finish(at - 1)
    for i in range(len(beats[::apart]), 5):
        if i < 4:
            tp_sum.sum_chips(i)
        finish(i - 1)
    small[0:1, :] = tally[0]
    small[1:2, :] = tally[1]
    mix_total = jnp.zeros((1, width), F32)
    for d in range(1, n_tp):
        got = mland.at[lax.rem(t + n_tp - d, n_tp)]
        remote(got, got, mgs.at[d - 1], mgr.at[d - 1], lax.rem(t + d, n_tp), e).wait_recv()
    for j in range(n_tp):
        mix_total = mix_total + mland[j, 0:1, :]
    small[4:5, :] = mix_total
    sland[e] = small[...]

    def small_copy(dest, src):
        return remote(small, sland.at[src], ss_.at[dest], sr_.at[src], t, dest)

    def send_small(k, carry):
        small_copy(lax.rem(e + k, n_ep), e).start()
        return carry

    lax.fori_loop(1, n_ep, send_small, 0)

    slots_.rest()
    for k in range(cuts):
        step(k, 2 * bits - 1)

    def small_arrived(k, carry):
        small_copy(e, lax.rem(e + n_ep - k, n_ep)).wait_recv()
        return carry

    lax.fori_loop(1, n_ep, small_arrived, 0)
    small_o[...] = lax.fori_loop(0, n_ep, lambda k, total: total + sland[k], jnp.zeros_like(small_o))

    def sent(k, carry):
        dest = lax.rem(e + k, n_ep)
        small_copy(dest, e).wait_send()
        return carry

    lax.fori_loop(1, n_ep, sent, 0)
    for d in range(1, n_tp):
        mix_copy(d).wait_send()
    for i in range(4):
        tp_sum.sent(i)
    for one in sums + gathers + wide:
        one.sent()


def backward(tokens, cotangent, attn, gshare, qkv, ht, lse, wqkv, wout, g1, b1, g2, segments, oshare, sup, y, gdown):
    n_tp, n_ep = lax.axis_size("tp"), lax.axis_size("ep")
    rows, width = tokens.shape
    wl = wout.shape[0]
    nx = n_tp // 2
    dx = max(nx - 1, 1)
    blk = rows // 4
    group = min(2, wl // HD)
    bits = n_ep.bit_length() - 1
    up_cuts, up_rows, units = sup.shape
    share = oshare.shape[1]
    down_cuts = ep_cuts(units, n_ep)
    vm = pl.BlockSpec(memory_space=pltpu.VMEM)
    dma = pltpu.SemaphoreType.DMA
    shape = jax.ShapeDtypeStruct
    return pl.pallas_call(
        functools.partial(backward_kernel, n_tp, n_ep),
        out_shape=(
            shape((rows, width), BF16),
            shape((rows, width), F32),
            shape((rows, width), BF16),
            shape((4 * wl, width), BF16),
            shape((8, width), F32),
            shape((up_cuts * up_rows * n_ep, units), BF16),
            shape((down_cuts, units // down_cuts // n_ep, width), BF16),
        ),
        in_specs=[vm] * 18,
        out_specs=(vm,) * 5 + (pl.BlockSpec(memory_space=pl.ANY), vm),
        scratch_shapes=[
            pltpu.VMEM((rows, width), BF16),
            pltpu.VMEM((rows, wl), BF16),
            pltpu.VMEM((wl, rows), BF16),
            pltpu.VMEM((group * HD, blk), F32),
            pltpu.VMEM((rows, group * blk), BF16),
            pltpu.VMEM((rows, group * blk), BF16),
            pltpu.VMEM((group * blk, group * HD), BF16),
            pltpu.VMEM((group * blk, group * HD), BF16),
            pltpu.VMEM((rows, group * HD), F32),
            pltpu.VMEM((rows, group * HD), F32),
            pltpu.VMEM((3, rows, wl), BF16),
            pltpu.VMEM((rows, blk), F32),
            pltpu.VMEM((rows, width), BF16),
            pltpu.VMEM((nx, rows, share), BF16),
            pltpu.VMEM((nx, rows, share), BF16),
            pltpu.VMEM((units, width), BF16),
            dma((4, dx)), dma((4, dx)), dma((4, nx)), dma((4, nx)),
            dma((4, dx)), dma((4, dx)), dma((4, nx)), dma((4, nx)),
            dma((up_cuts, bits)), dma((up_cuts, bits)), dma((up_cuts,)),
            dma((4,)), dma((4,)), dma((4, dx)), dma((4, dx)), dma((down_cuts, bits)), dma((down_cuts, bits)),
        ],
        compiler_params=pltpu.CompilerParams(
            collective_id=3, has_side_effects=True, vmem_limit_bytes=VMEM_LIMIT
        ),
        cost_estimate=pl.CostEstimate(flops=60 * 10**9, bytes_accessed=50 * 10**6, transcendentals=0),
        name="attention_backward",
    )(
        tokens, cotangent, attn, gshare, qkv, ht, lse, wqkv, wout, g1.reshape(1, width), b1.reshape(1, width),
        g2.reshape(1, width), segments, segments.reshape(rows, 1), oshare, sup, y, gdown,
    )


def finish_block(tokens, gh, part, g1, first_sums, gmix, wpart, sdown):
    n_tp, n_ep = lax.axis_size("tp"), lax.axis_size("ep")
    rows, width = tokens.shape
    nx = n_tp // 2
    dx = max(nx - 1, 1)
    half = width // 2
    bits = n_ep.bit_length() - 1
    down_cuts, down_rows, _ = sdown.shape
    cuts = max(q for q in (8, 4, 2, 1) if q == 1 or wpart.shape[0] % (16 * q * n_ep) == 0)
    vm = pl.BlockSpec(memory_space=pltpu.VMEM)
    dma = pltpu.SemaphoreType.DMA
    return pl.pallas_call(
        functools.partial(finish_kernel, n_tp, n_ep),
        out_shape=(
            jax.ShapeDtypeStruct((rows, width), BF16),
            jax.ShapeDtypeStruct((8, width), F32),
            jax.ShapeDtypeStruct(wpart.shape, BF16),
            jax.ShapeDtypeStruct((down_cuts * down_rows * n_ep, width), BF16),
        ),
        in_specs=[vm] * 8,
        out_specs=(vm,) * 3 + (pl.BlockSpec(memory_space=pl.ANY),),
        scratch_shapes=[
            pltpu.VMEM((rows, half), BF16),
            pltpu.VMEM((nx, rows, half), BF16),
            pltpu.VMEM((8, width), F32),
            pltpu.VMEM((n_ep, 8, width), F32),
            pltpu.VMEM((n_tp, 8, width), F32),
            pltpu.VMEM(wpart.shape, BF16),
            dma((cuts, bits)), dma((cuts, bits)), dma((cuts, bits)), dma((cuts, bits)),
            dma((down_cuts, bits)), dma((down_cuts, bits)), dma((down_cuts,)),
            dma((4,)), dma((4,)), dma((4, dx)), dma((4, dx)), dma((4,)), dma((4,)),
            dma((n_ep,)), dma((n_ep,)), dma((n_tp,)), dma((n_tp,)),
        ],
        compiler_params=pltpu.CompilerParams(
            collective_id=4, has_side_effects=True, vmem_limit_bytes=VMEM_LIMIT
        ),
        cost_estimate=pl.CostEstimate(flops=40 * 10**9, bytes_accessed=50 * 10**6, transcendentals=0),
        name="finish_norm",
    )(tokens, gh, part, g1.reshape(1, width), first_sums, gmix, wpart, sdown)


def outputs_kernel(out, gtok, geup, gedown, gup, gdown, gout, gqkv, out_o, gtok_o, geup_o, gedown_o, gup_o, gdown_o, gout_o, gqkv_o):
    out_o[...] = out[...]
    gtok_o[...] = gtok[...]
    geup_o[0] = geup[...]
    gedown_o[0] = gedown[...]
    gup_o[...] = gup[...].astype(F32)
    gdown_o[...] = gdown[...].astype(F32)
    gout_o[...] = gout[...].astype(F32)
    wl = gqkv_o.shape[2]
    for j in range(3):
        gqkv_o[j] = gqkv[pl.ds((1 + j) * wl, wl), :].astype(F32).T


def write_outputs(out, gtok, geup, gedown, gup, gdown, wsum):
    rows, width = out.shape
    units = gup.shape[1]
    wl = wsum.shape[0] // 4
    steps = 8

    def by_rows(count, columns):
        return pl.BlockSpec((count // steps, columns), lambda i: (i, 0))

    lead_up = pl.BlockSpec((1, width // steps, units), lambda i: (0, i, 0))
    lead_down = pl.BlockSpec((1, units // steps, width), lambda i: (0, i, 0))
    shape = jax.ShapeDtypeStruct
    moved = 2 * (2 * rows * width) * 2 + 4 * width * units * 7 + 6 * 4 * wl * width
    return pl.pallas_call(
        outputs_kernel,
        grid=(steps,),
        out_shape=(
            shape((rows, width), BF16),
            shape((rows, width), BF16),
            shape((1, width, units), F32),
            shape((1, units, width), F32),
            shape((width, units), F32),
            shape((units, width), F32),
            shape((wl, width), F32),
            shape((3, width, wl), F32),
        ),
        in_specs=[
            by_rows(rows, width), by_rows(rows, width), by_rows(width, units), by_rows(units, width),
            by_rows(width, units), by_rows(units, width), by_rows(wl, width),
            pl.BlockSpec((4 * wl, width // steps), lambda i: (0, i)),
        ],
        out_specs=(
            by_rows(rows, width), by_rows(rows, width), lead_up, lead_down,
            by_rows(width, units), by_rows(units, width), by_rows(wl, width),
            pl.BlockSpec((3, width // steps, wl), lambda i: (0, i, 0)),
        ),
        cost_estimate=pl.CostEstimate(flops=10**6, bytes_accessed=moved, transcendentals=0),
        compiler_params=pltpu.CompilerParams(vmem_limit_bytes=VMEM_LIMIT + 3 * 2**20),
        name="final_outputs",
    )(out, gtok, geup, gedown, gup, gdown, wsum, wsum)


def local(
    tokens, segments, routes, capacity, ln1_gain, ln1_bias, qkv_weight, out_weight, ln2_gain, ln2_bias,
    mix_weight, up_weight, down_weight, expert_up, expert_down, cotangent,
):
    width = tokens.shape[1]
    experts = capacity.shape[0]
    qkv, heads_t, lse, normed2, attn_sum, mix, cot_rows, targets, targets_col = forward(
        tokens, cotangent, segments, routes, capacity, ln1_gain, ln1_bias, ln2_gain, ln2_bias,
        qkv_weight, out_weight, mix_weight,
    )
    mix_float = mix_weight.astype(F32)
    wdiff = (mix_float[:, 0] - mix_float[:, 1]).reshape(1, width)
    rows_in, grad_up, grad_down, y_part, gshare, gmix_dense = dense_block(
        normed2, targets, cotangent, mix, up_weight, down_weight, wdiff, experts
    )
    grad_expert_up, grad_expert_down, gsec, gmix_rows, out_share, part_up = expert_block(
        rows_in, cot_rows, expert_up[0], expert_down[0], mix_weight, wdiff, gshare, targets_col, grad_up
    )
    output, grad_hidden, part, wpart, first_sums, grad_up, part_down = backward(
        tokens, cotangent, attn_sum, gsec, qkv, heads_t, lse, qkv_weight, out_weight, ln1_gain, ln1_bias,
        ln2_gain, segments, out_share, part_up, y_part, grad_down,
    )
    grad_tokens, small, wsum, grad_down = finish_block(
        tokens, grad_hidden, part, ln1_gain, first_sums, gmix_dense + gmix_rows, wpart, part_down
    )
    output, grad_tokens, grad_expert_up, grad_expert_down, grad_up, grad_down, grad_out, grad_qkv = write_outputs(
        output, grad_tokens, grad_expert_up, grad_expert_down, grad_up, grad_down, wsum
    )
    return (
        output,
        grad_tokens,
        small[0],
        small[1],
        grad_qkv,
        grad_out,
        small[2],
        small[3],
        jnp.stack([small[4], -small[4]], axis=1),
        grad_up,
        grad_down,
        grad_expert_up,
        grad_expert_down,
    )


def solution(mesh):
    return jax.shard_map(
        local,
        mesh=mesh,
        in_specs=(
            P("ep", None),
            P("ep", None),
            P("ep"),
            P(),
            P(),
            P(),
            P(None, None, "tp"),
            P("tp", None),
            P(),
            P(),
            P(),
            P(None, "tp"),
            P("tp", None),
            P("ep", None, "tp"),
            P("ep", "tp", None),
            P("ep", None),
        ),
        out_specs=(
            P("ep", None),
            P("ep", None),
            P(),
            P(),
            P(None, None, "tp"),
            P("tp", None),
            P(),
            P(),
            P(),
            P(None, "tp"),
            P("tp", None),
            P("ep", None, "tp"),
            P("ep", "tp", None),
        ),
        check_vma=False,
    )
```
